256 devices in a mesh: tm: 8 (over z), space: 32 (over x, y, core).
Axes of the slice: x: 4, y: 4, z: 8, core: 2. Of those that a mesh axis runs over, the one named last changes fastest.
Arguments:
- increment: float32 [8, 1024, 12, 1024], P('tm', 'space'), may hold values from -6 to 6
- multiplier: float32 [8, 1024, 12, 1024], P('tm', 'space'), may hold values from -6 to 6
- obs_dual: float32 [8, 16384], P('tm', 'space'), may hold values from -6 to 6
- obs_index: int32 [8, 16384], P('tm', 'space'), may hold values from 0 to 6143
- obs_variance: float32 [8, 16384], P('tm', 'space'), may hold values from 0.25 to 4
- winds: float32 [8, 1024, 12, 1024], P('tm', 'space'), may hold values from -1 to 1
- spectral_var: float32 [1024, 12, 1024], P(None, None, 'space'), may hold values from 0.1 to 2
Outputs:
- model_rows: float32 [8, 1024, 12, 1024], P('tm', 'space')
- obs_rows: float32 [8, 16384], P('tm', 'space')
- state_rows: float32 [8, 1024, 12, 1024], P('tm', 'space')
The draws below stay inside these ranges and needn't reach their ends.
Inputs may be any that keep to these rules, and one draw needn't show every extreme that they name: `obs_index`: index of a block within the band of the observation's column, as in the reference program.
All inputs are finite; a program needn't handle non-finite values.
Results may differ from the reference program's by a relative error of at most 0.0061.
Values may be sent and summed in bfloat16 or wider, within the bound.
No kernel may reach another device: no remote copies, remote signals or barrier semaphores. Data moves between devices by JAX's collectives and lax.ppermute only.
A program may use at most 128 MiB of HBM per device.

```python
import math
import jax
import jax.numpy as jnp
from jax import lax

NX = 1024
LEV = 6
STEPS = 4
OBS_DEV = 512
FL = 12
NY = 1024
NSUB = 8
NOBS = 16384
NBLK = 6144


def place_ends(entries, rng, smallest, high):
    longest = entries.shape.index(max(entries.shape))
    spots = []
    for shift in (0, 1):
        where = [jax.random.randint(jax.random.fold_in(rng, axis), (), 0, length) for axis, length in enumerate(entries.shape)]
        where[longest] = (where[longest] + shift) % entries.shape[longest]
        spots.append(tuple(where))
    return entries.at[spots[0]].set(smallest).at[spots[1]].set(high)


def steps_of(own_key, shape, split, low, top_value):
    factor_of, own = 1.0, jax.random.fold_in(own_key, 6)
    for axis_at, shards_of in split:
        draws = jnp.exp(jax.random.uniform(jax.random.fold_in(own, axis_at), (shards_of,), jnp.float32, low / len(split), top_value / len(split)))
        factor_of = factor_of * jnp.repeat(draws, shape[axis_at] // shards_of).reshape([-1 if axis == axis_at else 1 for axis in range(len(shape))])
    return factor_of


def gaussian(own_key, dims, scale, most, cuts=(), kind=jnp.bfloat16):
    drawn = scale * jax.random.normal(own_key, dims, jnp.float32)
    if cuts:
        drawn = drawn * steps_of(own_key, dims, cuts, -0.22, 0.18)
    return jnp.clip(drawn, -most, most).astype(kind)


def setup_inputs(seed: int = 0) -> dict:
    splits = jax.random.split(jax.random.key(seed), 8)
    increment = gaussian(splits[0], (NSUB, NY, FL, NX), 1.0, 6.0, ((0, 8), (1, 32)), jnp.float32)
    multiplier = gaussian(splits[1], (NSUB, NY, FL, NX), 1.0, 6.0, ((0, 8), (1, 32)), jnp.float32)
    obs_dual = gaussian(splits[2], (NSUB, NOBS), 1.0, 6.0, ((0, 8), (1, 32)), jnp.float32)
    obs_index = place_ends(jax.random.randint(splits[3], (NSUB, NOBS), 0, NBLK), jax.random.fold_in(splits[3], 1), 0, NBLK - 1).astype(jnp.int32)
    obs_variance = jnp.clip(jnp.exp(math.log(4.0) - 2.7725887 * jax.random.uniform(splits[4], (NSUB, NOBS), jnp.float32) ** steps_of(splits[4], (NSUB, NOBS), ((0, 8), (1, 32)), -0.2, 0.2)), 0.25, 4.0)
    winds = jnp.clip(jax.random.uniform(splits[5], (NSUB, NY, 2 * LEV, NX), jnp.float32, -1.0, 1.0) * steps_of(splits[5], (NSUB, NY, 2 * LEV, NX), ((0, 8), (1, 32)), -0.4, 0.0), -1.0, 1.0)
    spectral_var = jnp.clip(jnp.exp(math.log(2.0) - 2.9957323 * jax.random.uniform(splits[6], (NY, FL, NX), jnp.float32) ** steps_of(splits[6], (NY, FL, NX), ((2, 32),), -0.2, 0.2)), 0.1, 2.0)
    return dict(increment=increment, multiplier=multiplier, obs_dual=obs_dual, obs_index=obs_index, obs_variance=obs_variance, winds=winds, spectral_var=spectral_var)


COURANT = 0.4
DIFFUSE = 0.2

def cosine_table(count):
    wave = jnp.arange(count, dtype=jnp.int32)[:, None]
    point = jnp.arange(count, dtype=jnp.int32)[None, :]
    phase = (2 * point + 1) * wave % (4 * count)
    table = jnp.cos(phase.astype(jnp.float32) * (math.pi / (2.0 * count))) * math.sqrt(2.0 / count)
    table = jnp.where(wave == 0, table * math.sqrt(0.5), table)
    return table.astype(jnp.bfloat16)

def advance(extended, wind_part, backward):
    levels = wind_part.shape[1] // 2
    east = jnp.tile(wind_part[:, :levels], (1, 2, 1))
    north = jnp.tile(wind_part[:, levels:], (1, 2, 1))
    centre = extended[1:-1]
    if backward:
        along = east[1:-1] * centre
        across = north * extended
    else:
        along = centre
        across = extended
    padded = jnp.pad(along, ((0, 0), (0, 0), (1, 1)))
    grad_east = (padded[:, :, 2:] - padded[:, :, :-2]) * 0.5
    grad_north = (across[2:] - across[:-2]) * 0.5
    side = jnp.pad(centre, ((0, 0), (0, 0), (1, 1)))
    laplace = extended[2:] + extended[:-2] + side[:, :, 2:] + side[:, :, :-2] - 4.0 * centre
    if backward:
        return centre + COURANT * (grad_east + grad_north) + DIFFUSE * laplace
    return centre - COURANT * (east[1:-1] * grad_east + north[1:-1] * grad_north) + DIFFUSE * laplace

def run_window(field, wind, backward):
    wind_pad = jnp.pad(wind, ((1, 1), (0, 0), (0, 0)))
    for position in range(STEPS):
        field = advance(jnp.pad(field, ((1, 1), (0, 0), (0, 0))), wind_pad, backward)
    return field

def covariance(field, spectral_var, cos_x, cos_y):
    rows, levels, width = field.shape
    flat = field.astype(jnp.bfloat16).reshape(rows * levels, width)
    spec = jnp.dot(flat, cos_x.T, preferred_element_type=jnp.float32).astype(jnp.bfloat16)
    lat = jnp.dot(cos_y, spec.reshape(rows, levels * width), preferred_element_type=jnp.float32)
    scaled = (lat * spectral_var.reshape(rows, levels * width)).astype(jnp.bfloat16)
    grid = jnp.dot(cos_y.T, scaled, preferred_element_type=jnp.float32).astype(jnp.bfloat16)
    result = jnp.dot(grid.reshape(rows * levels, width), cos_x, preferred_element_type=jnp.float32)
    return result.reshape(rows, levels, width)

def reference(increment, multiplier, obs_dual, obs_index, obs_variance, winds, spectral_var):
    cos_x = cosine_table(NX)
    cos_y = cosine_table(NY)
    ends = lax.map(lambda pair: run_window(pair[0], pair[1], False), (increment, winds))
    previous = jnp.concatenate([jnp.zeros_like(ends[:1]), ends[:-1]], axis=0)
    next_dual = jnp.concatenate([multiplier[1:], jnp.zeros_like(multiplier[:1])], axis=0)
    back = lax.map(lambda pair: run_window(pair[0], pair[1], True), (next_dual, winds))
    spread_cov = lax.map(lambda field: covariance(field, spectral_var, cos_x, cos_y), multiplier)
    model_rows = spread_cov + (increment - previous)
    blocks = increment.reshape(NSUB, NY // 4, 4, FL, NX // 16, 16).sum(axis=(2, 5)).reshape(NSUB, -1)
    band = (jnp.arange(NOBS, dtype=jnp.int32) // OBS_DEV).astype(jnp.int32)
    global_index = (band[None, :] * NBLK + obs_index).astype(jnp.int32)
    observed = jnp.take_along_axis(blocks, global_index, axis=1) / 8.0
    obs_rows = obs_variance * obs_dual + observed
    scatter_rows = jnp.arange(NSUB, dtype=jnp.int32)[:, None] + jnp.zeros_like(global_index)
    summed = jnp.zeros(blocks.shape, jnp.float32).at[scatter_rows, global_index].add(obs_dual) / 8.0
    summed = summed.reshape(NSUB, NY // 4, 1, FL, NX // 16, 1)
    spread_obs = jnp.broadcast_to(summed, (NSUB, NY // 4, 4, FL, NX // 16, 16)).reshape(NSUB, NY, FL, NX)
    state_rows = multiplier - back + spread_obs
    return (model_rows, obs_rows, state_rows)
```

```python
import math

import jax
import jax.numpy as jnp
import numpy as np
from jax import lax
from jax.experimental import pallas as pl
from jax.experimental.pallas import tpu as pltpu
from jax.sharding import PartitionSpec as P
import ml_dtypes

STEPS = 4
HALF = 4
F32 = jnp.float32
BF16 = jnp.bfloat16


def cosine_table(count):
    wave = np.arange(count)[:, None]
    point = np.arange(count)[None, :]
    phase = (2 * point + 1) * wave % (4 * count)
    table = np.cos(phase * (math.pi / (2.0 * count))) * math.sqrt(2.0 / count)
    table = np.where(wave == 0, table * math.sqrt(0.5), table)
    return table.astype(np.float32).astype(ml_dtypes.bfloat16)


def block_permutation():
    perm = np.zeros((512, 512), np.float32)
    for i in range(4):
        for j in range(4):
            for b in range(32):
                perm[i * 128 + j * 32 + b, j * 128 + i * 32 + b] = 1.0
    return perm.astype(ml_dtypes.bfloat16)


def block_sums(levels, rows, width):
    cols = (np.arange(width)[:, None] // 16 == np.arange(width // 16)[None, :]).astype(np.float32)
    out = np.arange(rows // 4 * levels)[:, None]
    inn = np.arange(levels * rows)[None, :]
    lines = ((out % levels == inn // rows) & (out // levels == inn % rows // 4)).astype(np.float32)
    return cols.astype(ml_dtypes.bfloat16), lines.astype(ml_dtypes.bfloat16)


def nt(a, b):
    return lax.dot_general(a, b, (((1,), (1,)), ((), ())), preferred_element_type=F32)


def tn(a, b):
    return lax.dot_general(a, b, (((0,), (0,)), ((), ())), preferred_element_type=F32)


def nn(a, b):
    return jnp.dot(a, b, preferred_element_type=F32)


def parts(a):
    first = a.astype(BF16)
    rest = a - first.astype(F32)
    second = rest.astype(BF16)
    third = (rest - second.astype(F32)).astype(BF16)
    return first, second, third


def low_half(shape):
    return lax.broadcasted_iota(jnp.int32, shape, len(shape) - 2) < HALF


def start_kernel(mult_ref, table_ref, flat_ref, spec_ref, head_ref, tail_ref):
    levels = mult_ref.shape[0]
    rows, width = mult_ref.shape[1:]
    flat = mult_ref[...].reshape(levels * rows, width).astype(BF16)
    flat_ref[...] = flat
    half = levels // 2
    first = mult_ref[:, :8, :]
    last = mult_ref[:, rows - 8 :, :]
    low = low_half((half, 8, width))
    head = jnp.where(low, first[:half], pltpu.roll(first[half:], HALF, 1))
    tail = jnp.where(low, pltpu.roll(last[half:], HALF, 1), last[:half])
    head_ref[...] = head.reshape(half * 8, width).astype(BF16)
    tail_ref[...] = tail.reshape(half * 8, width).astype(BF16)
    spec_ref[...] = nt(table_ref[...], flat).astype(BF16)


def edge_kernel(incr_ref, wind_ref, head_ref, tail_ref):
    levels, rows, width = incr_ref.shape
    low = low_half((levels, 8, width))
    head = jnp.where(low, incr_ref[:, :8, :], pltpu.roll(wind_ref[:, :8, :], HALF, 1))
    tail = jnp.where(low, pltpu.roll(wind_ref[:, rows - 8 :, :], HALF, 1), incr_ref[:, rows - 8 :, :])
    head_ref[...] = head.reshape(levels * 8, width).astype(BF16)
    tail_ref[...] = tail.reshape(levels * 8, width).astype(BF16)


def coefficients(level, levels, edge_ref, wind_ref, head_ref, tail_ref, coef_ref):
    rows, width = wind_ref.shape[1:]
    low = low_half((8, width))
    shape = (rows + 8, width)
    row = lax.broadcasted_iota(jnp.int32, shape, 0)
    col = lax.broadcasted_iota(jnp.int32, shape, 1)

    def extended(index):
        at = pl.ds(pl.multiple_of(index * 8, 8), 8)
        margin = jnp.where(low, tail_ref[at, :], head_ref[at, :])
        return jnp.concatenate([wind_ref[index], pltpu.roll(margin, HALF, 0)], axis=0)

    u = extended(level)
    v = extended(level + levels // 2)
    coef_ref[0] = jnp.where(col == width - 1, 0.0, 1.0 - u)
    coef_ref[1] = jnp.where(col == 0, 0.0, 1.0 + u)
    coef_ref[2] = jnp.where((row == rows - 1) & (edge_ref[1] != 0), 0.0, 1.0 - v)
    coef_ref[3] = jnp.where((row == 0) & (edge_ref[0] != 0), 0.0, 1.0 + v)


def forward_steps(x, coef_ref):
    rows, width = x.shape
    for _ in range(STEPS):
        x = (
            x
            + coef_ref[0] * pltpu.roll(x, width - 1, 1)
            + coef_ref[1] * pltpu.roll(x, 1, 1)
            + coef_ref[2] * pltpu.roll(x, rows - 1, 0)
            + coef_ref[3] * pltpu.roll(x, 1, 0)
        )
    return x * (0.2**STEPS)


def backward_steps(y, coef_ref):
    rows, width = y.shape
    for _ in range(STEPS):
        y = (
            y
            + pltpu.roll(coef_ref[1] * y, width - 1, 1)
            + pltpu.roll(coef_ref[0] * y, 1, 1)
            + pltpu.roll(coef_ref[3] * y, rows - 1, 0)
            + pltpu.roll(coef_ref[2] * y, 1, 0)
        )
    return y * (0.2**STEPS)


def one_hots(index, blocks):
    count = index.shape[1]
    high = lax.broadcasted_iota(jnp.int32, (blocks[0], count), 0) == (index >> 6)
    low = lax.broadcasted_iota(jnp.int32, (blocks[1], count), 0) == (index & 63)
    return high, low


def forward_kernel(
    edge_ref, incr_ref, wind_ref, head_in, tail_in, index_ref, dual_ref, variance_ref, cols_ref, lines_ref,
    ends_ref, obs_ref, head_ref, tail_ref, coef_ref,
):
    levels, rows, width = incr_ref.shape
    head_ref[...] = head_in[...].astype(F32)
    tail_ref[...] = tail_in[...].astype(F32)
    low = low_half((8, width))

    def at_level(level, carry):
        coefficients(level, levels, edge_ref, wind_ref, head_ref, tail_ref, coef_ref)
        for group in range(2):
            index = level + group * (levels // 2)
            at = pl.ds(pl.multiple_of(index * 8, 8), 8)
            margin = jnp.where(low, head_ref[at, :], tail_ref[at, :])
            x = forward_steps(jnp.concatenate([incr_ref[index], margin], axis=0), coef_ref)
            ends_ref[pl.ds(pl.multiple_of(index * rows, rows), rows), :] = x[:rows].astype(BF16)
        return carry

    lax.fori_loop(0, levels // 2, at_level, 0)
    cols, lines = cols_ref[...], lines_ref[...]
    narrow = sum(nn(p, cols) for p in parts(incr_ref[...].reshape(levels * rows, width)))
    sums = sum(nn(lines, p) for p in parts(narrow))
    high, low_hot = one_hots(index_ref[...], sums.shape)
    high = high.astype(BF16)
    picked = sum(tn(p, high) for p in parts(sums))
    observed = jnp.sum(jnp.where(low_hot, picked, 0.0), axis=0, keepdims=True) * 0.125
    obs_ref[...] = variance_ref[...] * dual_ref[...] + observed


def backward_kernel(
    edge_ref, next_ref, next_head, next_tail, wind_ref, head_in, tail_in, mult_ref, index_ref, dual_ref,
    cols_ref, lines_ref, state_ref, head_ref, tail_ref, coef_ref, nhead_ref, ntail_ref,
):
    levels, rows, width = mult_ref.shape
    head_ref[...] = head_in[...].astype(F32)
    tail_ref[...] = tail_in[...].astype(F32)
    nhead_ref[...] = next_head[...].astype(F32)
    ntail_ref[...] = next_tail[...].astype(F32)
    low = low_half((8, width))
    cols, lines = cols_ref[...], lines_ref[...]
    blocks = (lines.shape[0], cols.shape[1])
    high, low_hot = one_hots(index_ref[...], blocks)
    low_hot = low_hot.astype(BF16)
    summed = sum(nt(p, low_hot) for p in parts(jnp.where(high, dual_ref[...], 0.0))) * 0.125
    tall = sum(tn(lines, p) for p in parts(summed))
    spread = sum(nt(p, cols) for p in parts(tall))
    state_ref[...] = mult_ref[...] + spread.reshape(levels, rows, width)

    def at_level(level, carry):
        coefficients(level, levels, edge_ref, wind_ref, head_ref, tail_ref, coef_ref)
        at = pl.ds(pl.multiple_of(level * 8, 8), 8)
        head, tail = nhead_ref[at, :], ntail_ref[at, :]
        for group in range(2):
            index = level + group * (levels // 2)
            if group == 0:
                margin = jnp.where(low, head, tail)
            else:
                margin = pltpu.roll(jnp.where(low, tail, head), HALF, 0)
            main = next_ref[pl.ds(pl.multiple_of(index * rows, rows), rows), :].astype(F32)
            y = backward_steps(jnp.concatenate([main, margin], axis=0), coef_ref)
            state_ref[index] = state_ref[index] - y[:rows]
        return carry

    lax.fori_loop(0, levels // 2, at_level, 0)


def gather_lines(came_ref, perm_ref, lines_ref):
    count, rows, wide = came_ref.shape
    groups, fields = count // 4, wide // 128
    perm = perm_ref[...]
    for g in range(fields):
        piece = came_ref[:, :, g * 128 : (g + 1) * 128].reshape(groups, 4, rows, 128)
        left = jnp.concatenate([piece[:, i].reshape(groups * rows, 128) for i in range(4)], axis=1)
        moved = nn(left, perm).astype(BF16)
        for i in range(4):
            for b in range(groups):
                lines_ref[(4 * g + i) * rows : (4 * g + i + 1) * rows, b * 128 : (b + 1) * 128] = moved[
                    b * rows : (b + 1) * rows, i * 128 : (i + 1) * 128
                ]


def latitude_kernel(came_ref, var_ref, turned_ref, perm_ref, out_ref, lines_ref):
    gather_lines(came_ref, perm_ref, lines_ref)
    scaled = (nn(lines_ref[...], turned_ref[...]) * var_ref[...]).astype(BF16)
    out_ref[...] = nt(turned_ref[...], scaled).astype(BF16)


def finish_kernel(came_ref, incr_ref, prev_ref, table_ref, perm_ref, out_ref, lines_ref):
    gather_lines(came_ref, perm_ref, lines_ref)
    covar = nn(lines_ref[...], table_ref[...])
    out_ref[...] = covar + (incr_ref[...] - prev_ref[...].astype(F32))


VMEM = pl.BlockSpec(memory_space=pltpu.VMEM)
SMEM = pl.BlockSpec(memory_space=pltpu.SMEM)


def call(kernel, outs, ins, scratch=(), name=None):
    specs = [SMEM if a.ndim == 1 else VMEM for a in ins]
    return pl.pallas_call(
        kernel,
        out_shape=outs,
        in_specs=specs,
        out_specs=jax.tree.map(lambda _: VMEM, outs),
        scratch_shapes=list(scratch),
        compiler_params=pltpu.CompilerParams(vmem_limit_bytes=40 * 1024 * 1024),
        name=name,
    )(*ins)


def local(increment, multiplier, obs_dual, obs_index, obs_variance, winds, spectral_var):
    rows, levels, width = increment.shape[1:]
    count = lax.axis_size("space")
    times = lax.axis_size("tm")
    lat = rows * count
    waves = width // count
    incr = jnp.transpose(increment[0], (1, 0, 2))
    mult = jnp.transpose(multiplier[0], (1, 0, 2))
    wind = jnp.transpose(winds[0], (1, 0, 2))
    var = jnp.transpose(spectral_var, (1, 2, 0)).reshape(levels * waves, lat)
    table = cosine_table(width)
    turned = np.ascontiguousarray(table.T)
    cols, lines = block_sums(levels, rows, width)
    perm = block_permutation()
    place = lax.axis_index("space")
    edge = jnp.stack([place == 0, place == count - 1]).astype(jnp.int32)
    full = levels * rows

    def shape(*dims):
        return jax.ShapeDtypeStruct(dims, BF16)

    flat, spec, mult_head, mult_tail = call(
        start_kernel,
        (shape(full, width), shape(width, full), shape(levels * 4, width), shape(levels * 4, width)),
        (mult, table),
        name="start",
    )
    head, tail = call(edge_kernel, (shape(levels * 8, width), shape(levels * 8, width)), (incr, wind), name="edges")

    came = lax.all_to_all(spec.reshape(count, waves, full), "space", 0, 0, tiled=True)
    ring = range(count - 1)
    down = [(i + 1, i) for i in ring]
    up = [(i, i + 1) for i in ring]
    head = lax.ppermute(head, "space", down)
    tail = lax.ppermute(tail, "space", up)
    both = ("tm", "space")
    mult_head = lax.ppermute(
        mult_head, both, [((t + 1) * count + a, t * count + b) for t in range(times - 1) for a, b in down]
    )
    mult_tail = lax.ppermute(
        mult_tail, both, [((t + 1) * count + a, t * count + b) for t in range(times - 1) for a, b in up]
    )
    coming = lax.ppermute(flat, "tm", [(t + 1, t) for t in range(times - 1)])

    margin = [pltpu.VMEM((levels * 8, width), F32)] * 2 + [pltpu.VMEM((4, rows + 8, width), F32)]
    ends, obs_rows = call(
        forward_kernel,
        (shape(full, width), jax.ShapeDtypeStruct(obs_dual.shape, F32)),
        (edge, incr, wind, head, tail, obs_index, obs_dual, obs_variance, cols, lines),
        margin,
        name="forward",
    )
    previous = lax.ppermute(ends, "tm", [(t, t + 1) for t in range(times - 1)])

    back = call(
        latitude_kernel,
        shape(lat, full),
        (came, var, turned, perm),
        [pltpu.VMEM((full, lat), BF16)],
        name="latitude",
    )
    returned = lax.all_to_all(back.reshape(count, rows, full), "space", 0, 0, tiled=True)

    state_rows = call(
        backward_kernel,
        jax.ShapeDtypeStruct((levels, rows, width), F32),
        (edge, coming, mult_head, mult_tail, wind, head, tail, mult, obs_index, obs_dual, cols, lines),
        margin + [pltpu.VMEM((levels * 4, width), F32)] * 2,
        name="backward",
    )
    model_rows = call(
        finish_kernel,
        jax.ShapeDtypeStruct((full, width), F32),
        (returned, incr.reshape(full, width), previous, table, perm),
        [pltpu.VMEM((full, width), BF16)],
        name="finish",
    )

    def placed(field):
        return jnp.transpose(field.reshape(levels, rows, width), (1, 0, 2))[None]

    return (placed(model_rows), obs_rows, placed(state_rows))


def solution(mesh):
    specs = (
        P("tm", "space", None, None),
        P("tm", "space", None, None),
        P("tm", "space"),
        P("tm", "space"),
        P("tm", "space"),
        P("tm", "space", None, None),
        P(None, None, "space"),
    )
    return jax.shard_map(
        local,
        mesh=mesh,
        in_specs=specs,
        out_specs=(P("tm", "space", None, None), P("tm", "space"), P("tm", "space", None, None)),
        check_vma=False,
    )
```

```python
import math

import jax
import jax.numpy as jnp
import numpy as np
from jax import lax
from jax.experimental import pallas as pl
from jax.experimental.pallas import tpu as pltpu
from jax.sharding import PartitionSpec as P
import ml_dtypes

STEPS = 4
HALF = 4
F32 = jnp.float32
BF16 = jnp.bfloat16


def cosine_table(count):
    wave = np.arange(count)[:, None]
    point = np.arange(count)[None, :]
    phase = (2 * point + 1) * wave % (4 * count)
    table = np.cos(phase * (math.pi / (2.0 * count))) * math.sqrt(2.0 / count)
    table = np.where(wave == 0, table * math.sqrt(0.5), table)
    return table.astype(np.float32).astype(ml_dtypes.bfloat16)


def block_sums(levels, rows, width):
    cols = (np.arange(width)[:, None] // 16 == np.arange(width // 16)[None, :]).astype(np.float32)
    out = np.arange(rows // 4 * levels)[:, None]
    inn = np.arange(levels * rows)[None, :]
    lines = ((out % levels == inn // rows) & (out // levels == inn % rows // 4)).astype(np.float32)
    return cols.astype(ml_dtypes.bfloat16), lines.astype(ml_dtypes.bfloat16)


def nt(a, b):
    return lax.dot_general(a, b, (((1,), (1,)), ((), ())), preferred_element_type=F32)


def tn(a, b):
    return lax.dot_general(a, b, (((0,), (0,)), ((), ())), preferred_element_type=F32)


def nn(a, b):
    return jnp.dot(a, b, preferred_element_type=F32)


def parts(a):
    first = a.astype(BF16)
    rest = a - first.astype(F32)
    second = rest.astype(BF16)
    third = (rest - second.astype(F32)).astype(BF16)
    return first, second, third


def low_half(shape):
    return lax.broadcasted_iota(jnp.int32, shape, len(shape) - 2) < HALF


class Copies:
    def __init__(self, sems):
        self.sems = sems
        self.count = 0

    def start(self, source, target):
        copy = pltpu.make_async_copy(source, target, self.sems.at[self.count])
        self.count += 1
        copy.start()
        return copy


def start_kernel(
    mult_hbm, table_hbm, incr_hbm, wind_hbm,
    flat_hbm, spec_hbm, mhead_hbm, mtail_hbm, head_hbm, tail_hbm,
    mult_ref, table_ref, edge_ref, flat_ref, spec_ref, mhead_ref, mtail_ref, head_ref, tail_ref, sems,
):
    levels, rows, width = mult_ref.shape
    half = levels // 2
    copies = Copies(sems)
    mult_in = [copies.start(mult_hbm.at[pl.ds(3 * i, 3)], mult_ref.at[pl.ds(3 * i, 3)]) for i in range(4)]
    table_in = [
        copies.start(table_hbm.at[pl.ds(256 * i, 256)], table_ref.at[pl.ds(256 * i, 256)]) for i in range(4)
    ]
    edge_in = [
        copies.start(source.at[:, pl.ds(at, 8), :], edge_ref.at[i])
        for i, (source, at) in enumerate(
            [(incr_hbm, 0), (wind_hbm, 0), (incr_hbm, rows - 8), (wind_hbm, rows - 8)]
        )
    ]
    out = []
    for copy in mult_in:
        copy.wait()
    flat_ref[...] = mult_ref[...].reshape(levels * rows, width).astype(BF16)
    out.append(copies.start(flat_ref, flat_hbm))
    first = mult_ref[:, :8, :]
    last = mult_ref[:, rows - 8 :, :]
    low = low_half((half, 8, width))
    head = jnp.where(low, first[:half], pltpu.roll(first[half:], HALF, 1))
    tail = jnp.where(low, pltpu.roll(last[half:], HALF, 1), last[:half])
    mhead_ref[...] = head.reshape(half * 8, width).astype(BF16)
    mtail_ref[...] = tail.reshape(half * 8, width).astype(BF16)
    out.append(copies.start(mhead_ref, mhead_hbm))
    out.append(copies.start(mtail_ref, mtail_hbm))
    flat = flat_ref[...]
    for i, copy in enumerate(table_in):
        copy.wait()
        part = pl.ds(256 * i, 256)
        spec_ref[part] = nt(table_ref[part], flat).astype(BF16)
        out.append(copies.start(spec_ref.at[part], spec_hbm.at[part]))
    for copy in edge_in:
        copy.wait()
    low = low_half((levels, 8, width))
    head = jnp.where(low, edge_ref[0], pltpu.roll(edge_ref[1], HALF, 1))
    tail = jnp.where(low, pltpu.roll(edge_ref[3], HALF, 1), edge_ref[2])
    head_ref[...] = head.reshape(levels * 8, width).astype(BF16)
    tail_ref[...] = tail.reshape(levels * 8, width).astype(BF16)
    out.append(copies.start(head_ref, head_hbm))
    out.append(copies.start(tail_ref, tail_hbm))
    for copy in out:
        copy.wait()


TILES = 5


def spread_rows(stage_ref, main, margin):
    rows, width = main.shape
    across = width // 128
    for c in range(across):
        stage_ref[c, :rows, :] = main[:, c * 128 : (c + 1) * 128]
        stage_ref[c, rows:, :] = margin[:, c * 128 : (c + 1) * 128]
    return [[stage_ref[c, pl.ds(t, 8, stride=TILES), :] for t in range(TILES)] for c in range(across)]


def join_rows(stage_ref, tiles, rows):
    for c, column in enumerate(tiles):
        for t, tile in enumerate(column):
            stage_ref[c, pl.ds(t, 8, stride=TILES), :] = tile * (0.2**STEPS)
    return jnp.concatenate([stage_ref[c, :rows, :] for c in range(len(tiles))], axis=1)


def coefficients(level, levels, edge_ref, wind_ref, head_ref, tail_ref, stage_ref, coef_ref):
    rows = wind_ref.shape[1]
    low = low_half((8, wind_ref.shape[2]))
    sublane = lax.broadcasted_iota(jnp.int32, (8, 128), 0)

    def extended(index, stage):
        at = pl.ds(pl.multiple_of(index * 8, 8), 8)
        margin = pltpu.roll(jnp.where(low, tail_ref[at, :], head_ref[at, :]), HALF, 0)
        return spread_rows(stage, wind_ref[index], margin)

    u = extended(level, stage_ref.at[0])
    v = extended(level + levels // 2, stage_ref.at[1])
    first = (sublane == 0) & (edge_ref[0] != 0)
    last = (sublane == (rows - 1) // TILES) & (edge_ref[1] != 0)
    for c in range(len(u)):
        for t in range(TILES):
            north, south = 1.0 - v[c][t], 1.0 + v[c][t]
            if t == (rows - 1) % TILES:
                north = jnp.where(last, 0.0, north)
            if t == 0:
                south = jnp.where(first, 0.0, south)
            coef_ref[0, c, t] = 1.0 - u[c][t]
            coef_ref[1, c, t] = 1.0 + u[c][t]
            coef_ref[2, c, t] = north
            coef_ref[3, c, t] = south


def north_of(column, t):
    return column[t + 1] if t < TILES - 1 else pltpu.roll(column[0], 7, 0)


def south_of(column, t):
    return column[t - 1] if t > 0 else pltpu.roll(column[TILES - 1], 1, 0)


def forward_steps(x, coef_ref):
    lane = lax.broadcasted_iota(jnp.int32, (8, 128), 1)
    first, last = lane == 0, lane == 127
    ends = len(x) - 1
    for _ in range(STEPS):
        new = []
        for c in range(len(x)):
            column = []
            for t in range(TILES):
                here = x[c][t]
                east = pltpu.roll(jnp.where(first, x[c + 1][t] if c < ends else 0.0, here), 127, 1)
                west = pltpu.roll(jnp.where(last, x[c - 1][t] if c > 0 else 0.0, here), 1, 1)
                column.append(
                    (here + coef_ref[0, c, t] * east)
                    + coef_ref[1, c, t] * west
                    + (coef_ref[2, c, t] * north_of(x[c], t) + coef_ref[3, c, t] * south_of(x[c], t))
                )
            new.append(column)
        x = new
    return x


def backward_steps(y, coef_ref):
    lane = lax.broadcasted_iota(jnp.int32, (8, 128), 1)
    first, last = lane == 0, lane == 127
    ends = len(y) - 1
    for _ in range(STEPS):
        new = []
        for c in range(len(y)):
            column = []
            up = [coef_ref[3, c, t] * y[c][t] for t in range(TILES)]
            down = [coef_ref[2, c, t] * y[c][t] for t in range(TILES)]
            for t in range(TILES):
                here = y[c][t]
                after = coef_ref[1, c + 1, t] * y[c + 1][t] if c < ends else 0.0
                before = coef_ref[0, c - 1, t] * y[c - 1][t] if c > 0 else 0.0
                east = pltpu.roll(jnp.where(first, after, coef_ref[1, c, t] * here), 127, 1)
                west = pltpu.roll(jnp.where(last, before, coef_ref[0, c, t] * here), 1, 1)
                column.append((here + east) + west + (north_of(up, t) + south_of(down, t)))
            new.append(column)
        y = new
    return y


def one_hots(index, blocks):
    count = index.shape[1]
    high = lax.broadcasted_iota(jnp.int32, (blocks[0], count), 0) == (index >> 6)
    low = lax.broadcasted_iota(jnp.int32, (blocks[1], count), 0) == (index & 63)
    return high, low


def forward_kernel(
    edge_ref, incr_hbm, wind_hbm, head_hbm, tail_hbm, ends_hbm,
    incr_ref, wind_ref, head_in, tail_in, head_ref, tail_ref, stage_ref, coef_ref, ends_ref, sems, level_sems,
):
    levels, rows, width = incr_ref.shape
    half = levels // 2
    copies = Copies(sems)
    margin_in = [copies.start(head_hbm, head_in), copies.start(tail_hbm, tail_in)]

    def fetch(kind, index):
        source, target = ((wind_hbm, wind_ref), (incr_hbm, incr_ref))[kind]
        return pltpu.make_async_copy(source.at[index], target.at[index], level_sems.at[kind, index])

    def put(index):
        part = pl.ds(pl.multiple_of(index * rows, rows), rows)
        return pltpu.make_async_copy(ends_ref.at[part], ends_hbm.at[part], level_sems.at[2, index])

    for level in range(half):
        for index in (level, level + half):
            for kind in range(2):
                fetch(kind, index).start()
    for copy in margin_in:
        copy.wait()
    head_ref[...] = head_in[...].astype(F32)
    tail_ref[...] = tail_in[...].astype(F32)
    low = low_half((8, width))

    def at_level(level, carry):
        for index in (level, level + half):
            for kind in range(2):
                fetch(kind, index).wait()
        coefficients(level, levels, edge_ref, wind_ref, head_ref, tail_ref, stage_ref, coef_ref)
        for group in range(2):
            index = level + group * half
            at = pl.ds(pl.multiple_of(index * 8, 8), 8)
            margin = jnp.where(low, head_ref[at, :], tail_ref[at, :])
            x = forward_steps(spread_rows(stage_ref.at[2 * group], incr_ref[index], margin), coef_ref)
            ends = join_rows(stage_ref.at[2 * group + 1], x, rows)
            ends_ref[pl.ds(pl.multiple_of(index * rows, rows), rows), :] = ends.astype(BF16)
            put(index).start()
        return carry

    lax.fori_loop(0, half, at_level, 0)
    for index in range(levels):
        put(index).wait()


def backward_kernel(
    edge_ref, next_hbm, nhead_hbm, ntail_hbm, wind_hbm, head_hbm, tail_hbm, mult_hbm, incr_hbm,
    index_ref, dual_ref, variance_ref, cols_hbm, lines_hbm,
    state_hbm, obs_ref,
    next_ref, wind_ref, mult_ref, incr_ref, cols_ref, lines_ref, head_in, tail_in, nhead_in, ntail_in,
    head_ref, tail_ref, nhead_ref, ntail_ref, stage_ref, coef_ref, spread_ref, state_ref, sems, level_sems,
):
    levels, rows, width = mult_ref.shape
    half = levels // 2
    copies = Copies(sems)
    block_in = [copies.start(cols_hbm, cols_ref), copies.start(lines_hbm, lines_ref)]
    margin_in = [
        copies.start(source, target)
        for source, target in (
            (head_hbm, head_in), (tail_hbm, tail_in), (nhead_hbm, nhead_in), (ntail_hbm, ntail_in)
        )
    ]
    incr_in = [copies.start(incr_hbm.at[pl.ds(3 * i, 3)], incr_ref.at[pl.ds(3 * i, 3)]) for i in range(4)]
    fields_in = [
        copies.start(source.at[pl.ds(start, size)], target.at[pl.ds(start, size)])
        for source, target, size in ((wind_hbm, wind_ref, 6), (next_hbm, next_ref, 192), (mult_hbm, mult_ref, 6))
        for start in (0, size)
    ]
    for copy in block_in:
        copy.wait()
    cols, lines = cols_ref[...], lines_ref[...]
    blocks = (lines.shape[0], cols.shape[1])
    high, low_hot = one_hots(index_ref[...], blocks)
    weights = low_hot.astype(BF16)
    summed = sum(nt(p, weights) for p in parts(jnp.where(high, dual_ref[...], 0.0))) * 0.125
    tall = sum(tn(lines, p) for p in parts(summed))
    spread_ref[...] = sum(nt(p, cols) for p in parts(tall))
    for copy in incr_in:
        copy.wait()
    narrow = sum(nn(p, cols) for p in parts(incr_ref[...].reshape(levels * rows, width)))
    sums = sum(nn(lines, p) for p in parts(narrow))
    high = high.astype(BF16)
    picked = sum(tn(p, high) for p in parts(sums))
    observed = jnp.sum(jnp.where(low_hot, picked, 0.0), axis=0, keepdims=True) * 0.125
    obs_ref[...] = variance_ref[...] * dual_ref[...] + observed
    for copy in margin_in + fields_in:
        copy.wait()
    head_ref[...] = head_in[...].astype(F32)
    tail_ref[...] = tail_in[...].astype(F32)
    nhead_ref[...] = nhead_in[...].astype(F32)
    ntail_ref[...] = ntail_in[...].astype(F32)
    low = low_half((8, width))

    def put(index):
        return pltpu.make_async_copy(state_ref.at[index], state_hbm.at[index], level_sems.at[index])

    def at_level(level, carry):
        coefficients(level, levels, edge_ref, wind_ref, head_ref, tail_ref, stage_ref, coef_ref)
        at = pl.ds(pl.multiple_of(level * 8, 8), 8)
        head, tail = nhead_ref[at, :], ntail_ref[at, :]
        for group in range(2):
            index = level + group * half
            if group == 0:
                margin = jnp.where(low, head, tail)
            else:
                margin = pltpu.roll(jnp.where(low, tail, head), HALF, 0)
            part = pl.ds(pl.multiple_of(index * rows, rows), rows)
            y = backward_steps(spread_rows(stage_ref.at[2 * group], next_ref[part, :].astype(F32), margin), coef_ref)
            back = join_rows(stage_ref.at[2 * group + 1], y, rows)
            state_ref[index] = (mult_ref[index] - back) + spread_ref[part, :]
            put(index).start()
        return carry

    lax.fori_loop(0, half, at_level, 0)
    for index in range(levels):
        put(index).wait()


def gather_lines(came_in, came_ref, lines_ref):
    count, rows, wide = came_ref.shape
    groups, fields = count // 4, wide // 128
    source = lax.broadcasted_iota(jnp.int32, (512, 512), 0)
    target = lax.broadcasted_iota(jnp.int32, (512, 512), 1)
    swapped = ((target & 127) >> 5) * 128 + (target >> 7) * 32 + (target & 31)
    perm = (source == swapped).astype(BF16)
    for copy in came_in:
        copy.wait()
    for g in range(fields):
        piece = came_ref[:, :, g * 128 : (g + 1) * 128].reshape(groups, 4, rows, 128)
        left = jnp.concatenate([piece[:, i].reshape(groups * rows, 128) for i in range(4)], axis=1)
        moved = nn(left, perm).astype(BF16)
        for i in range(4):
            for b in range(groups):
                lines_ref[(4 * g + i) * rows : (4 * g + i + 1) * rows, b * 128 : (b + 1) * 128] = moved[
                    b * rows : (b + 1) * rows, i * 128 : (i + 1) * 128
                ]


def quarters(copies, source, target):
    size = target.shape[0] // 4
    return [copies.start(source.at[pl.ds(size * i, size)], target.at[pl.ds(size * i, size)]) for i in range(4)]


def quarter_columns(copies, source, target):
    size = target.shape[1] // 4
    return [copies.start(source.at[:, pl.ds(size * i, size)], target.at[:, pl.ds(size * i, size)]) for i in range(4)]


def latitude_kernel(
    came_hbm, var_hbm, turned_hbm, _head, _tail, out_hbm,
    came_ref, var_ref, turned_ref, lines_ref, scaled_ref, out_ref, sems,
):
    copies = Copies(sems)
    came_in = quarters(copies, came_hbm, came_ref)
    turned_in = quarter_columns(copies, turned_hbm, turned_ref)
    var_in = quarter_columns(copies, var_hbm, var_ref)
    gather_lines(came_in, came_ref, lines_ref)
    lines = lines_ref[...]
    for i in range(4):
        turned_in[i].wait()
        var_in[i].wait()
        part = pl.ds(256 * i, 256)
        scaled_ref[:, part] = (nn(lines, turned_ref[:, part]) * var_ref[:, part]).astype(BF16)
    scaled = scaled_ref[...]
    out = []
    for i in range(2):
        part = pl.ds(512 * i, 512)
        out_ref[part] = nt(turned_ref[part], scaled).astype(BF16)
        out.append(copies.start(out_ref.at[part], out_hbm.at[part]))
    for copy in out:
        copy.wait()


def finish_kernel(
    came_hbm, incr_hbm, prev_hbm, table_hbm, out_hbm,
    came_ref, incr_ref, prev_ref, table_ref, lines_ref, out_ref, sems,
):
    copies = Copies(sems)
    came_in = quarters(copies, came_hbm, came_ref)
    table_in = quarter_columns(copies, table_hbm, table_ref)
    incr_in = quarter_columns(copies, incr_hbm, incr_ref)
    prev_in = quarter_columns(copies, prev_hbm, prev_ref)
    gather_lines(came_in, came_ref, lines_ref)
    lines = lines_ref[...]
    out = []
    for i in range(4):
        table_in[i].wait()
        incr_in[i].wait()
        prev_in[i].wait()
        part = pl.ds(256 * i, 256)
        covar = nn(lines, table_ref[:, part])
        out_ref[:, part] = covar + (incr_ref[:, part] - prev_ref[:, part].astype(F32))
        out.append(copies.start(out_ref.at[:, part], out_hbm.at[:, part]))
    for copy in out:
        copy.wait()


VMEM = pl.BlockSpec(memory_space=pltpu.VMEM)
SMEM = pl.BlockSpec(memory_space=pltpu.SMEM)
HBM = pl.BlockSpec(memory_space=pl.ANY)


def call(kernel, outs, ins, scratch, name):
    def place(a):
        if len(a.shape) == 1:
            return SMEM
        return VMEM if a.shape[0] == 1 else HBM

    return pl.pallas_call(
        kernel,
        out_shape=outs,
        in_specs=[place(a) for a in ins],
        out_specs=jax.tree.map(place, outs),
        scratch_shapes=list(scratch),
        compiler_params=pltpu.CompilerParams(vmem_limit_bytes=56 * 1024 * 1024),
        name=name,
    )(*ins)


def local(increment, multiplier, obs_dual, obs_index, obs_variance, winds, spectral_var):
    rows, levels, width = increment.shape[1:]
    count = lax.axis_size("space")
    times = lax.axis_size("tm")
    lat = rows * count
    waves = width // count
    full = levels * rows
    incr = jnp.transpose(increment[0], (1, 0, 2))
    mult = jnp.transpose(multiplier[0], (1, 0, 2))
    wind = jnp.transpose(winds[0], (1, 0, 2))
    var = jnp.transpose(spectral_var, (1, 2, 0)).reshape(full, lat)
    table = cosine_table(width)
    turned = np.ascontiguousarray(table.T)
    cols, lines = block_sums(levels, rows, width)
    place = lax.axis_index("space")
    edge = jnp.stack([place == 0, place == count - 1]).astype(jnp.int32)

    def shape(*dims):
        return jax.ShapeDtypeStruct(dims, BF16)

    def wide(*dims):
        return pltpu.VMEM(dims, F32)

    def short(*dims):
        return pltpu.VMEM(dims, BF16)

    def sems(*dims):
        return pltpu.SemaphoreType.DMA(dims)

    field = (levels, rows, width)
    flat, spec, mult_head, mult_tail, head, tail = call(
        start_kernel,
        (
            shape(full, width), shape(width, full), shape(levels * 4, width), shape(levels * 4, width),
            shape(levels * 8, width), shape(levels * 8, width),
        ),
        (mult, table, incr, wind),
        [
            wide(*field), short(width, width), wide(4, levels, 8, width), short(full, width), short(width, full),
            short(levels * 4, width), short(levels * 4, width), short(levels * 8, width), short(levels * 8, width),
            sems(24),
        ],
        "start",
    )
    came = lax.all_to_all(spec.reshape(count, waves, full), "space", 0, 0, tiled=True)
    ring = range(count - 1)
    down = [(i + 1, i) for i in ring]
    up = [(i, i + 1) for i in ring]
    head = lax.ppermute(head, "space", down)
    tail = lax.ppermute(tail, "space", up)
    both = ("tm", "space")
    mult_head = lax.ppermute(
        mult_head, both, [((t + 1) * count + a, t * count + b) for t in range(times - 1) for a, b in down]
    )
    mult_tail = lax.ppermute(
        mult_tail, both, [((t + 1) * count + a, t * count + b) for t in range(times - 1) for a, b in up]
    )
    coming = lax.ppermute(flat, "tm", [(t + 1, t) for t in range(times - 1)])

    across = width // 128
    stages = [wide(4, across, rows + 8, 128), wide(4, across, TILES, 8, 128)]
    ends = call(
        forward_kernel,
        shape(full, width),
        (edge, incr, wind, head, tail),
        [
            wide(*field), wide(*field), short(levels * 8, width), short(levels * 8, width),
            wide(levels * 8, width), wide(levels * 8, width), *stages, short(full, width), sems(2), sems(3, levels),
        ],
        "forward",
    )
    previous = lax.ppermute(ends, "tm", [(t, t + 1) for t in range(times - 1)])

    back = call(
        latitude_kernel,
        shape(lat, full),
        (came, var, turned, mult_head, mult_tail),
        [
            short(count, waves, full), wide(full, lat), short(lat, lat), short(full, lat), short(full, lat),
            short(lat, full), sems(16),
        ],
        "latitude",
    )
    returned = lax.all_to_all(back.reshape(count, rows, full), "space", 0, 0, tiled=True)

    state_rows, obs_rows = call(
        backward_kernel,
        (jax.ShapeDtypeStruct(field, F32), jax.ShapeDtypeStruct(obs_dual.shape, F32)),
        (
            edge, coming, mult_head, mult_tail, wind, head, tail, mult, incr, obs_index, obs_dual, obs_variance,
            cols, lines,
        ),
        [
            short(full, width), wide(*field), wide(*field), wide(*field), short(*cols.shape), short(*lines.shape),
            short(levels * 8, width), short(levels * 8, width), short(levels * 4, width), short(levels * 4, width),
            wide(levels * 8, width), wide(levels * 8, width), wide(levels * 4, width), wide(levels * 4, width),
            *stages, wide(full, width), wide(*field), sems(16), sems(levels),
        ],
        "backward",
    )
    model_rows = call(
        finish_kernel,
        jax.ShapeDtypeStruct((full, width), F32),
        (returned, incr.reshape(full, width), previous, table),
        [
            short(count, rows, full), wide(full, width), short(full, width), short(width, width),
            short(full, width), wide(full, width), sems(20),
        ],
        "finish",
    )

    def placed(whole):
        return jnp.transpose(whole.reshape(field), (1, 0, 2))[None]

    return (placed(model_rows), obs_rows, placed(state_rows))


def solution(mesh):
    specs = (
        P("tm", "space", None, None),
        P("tm", "space", None, None),
        P("tm", "space"),
        P("tm", "space"),
        P("tm", "space"),
        P("tm", "space", None, None),
        P(None, None, "space"),
    )
    return jax.shard_map(
        local,
        mesh=mesh,
        in_specs=specs,
        out_specs=(P("tm", "space", None, None), P("tm", "space"), P("tm", "space", None, None)),
        check_vma=False,
    )
```

```python
import math

import jax
import jax.numpy as jnp
import numpy as np
from jax import lax
from jax.experimental import pallas as pl
from jax.experimental.pallas import tpu as pltpu
from jax.sharding import PartitionSpec as P
import ml_dtypes

STEPS = 4
HALF = 4
F32 = jnp.float32
BF16 = jnp.bfloat16


def cosine_table(count):
    wave = np.arange(count)[:, None]
    point = np.arange(count)[None, :]
    phase = (2 * point + 1) * wave % (4 * count)
    table = np.cos(phase * (math.pi / (2.0 * count))) * math.sqrt(2.0 / count)
    table = np.where(wave == 0, table * math.sqrt(0.5), table)
    return table.astype(np.float32).astype(ml_dtypes.bfloat16)


def block_sums(levels, rows, width):
    cols = (np.arange(width)[:, None] // 16 == np.arange(width // 16)[None, :]).astype(np.float32)
    out = np.arange(rows // 4 * levels)[:, None]
    inn = np.arange(levels * rows)[None, :]
    lines = ((out % levels == inn // rows) & (out // levels == inn % rows // 4)).astype(np.float32)
    return cols.astype(ml_dtypes.bfloat16), lines.astype(ml_dtypes.bfloat16)


def nt(a, b):
    return lax.dot_general(a, b, (((1,), (1,)), ((), ())), preferred_element_type=F32)


def tn(a, b):
    return lax.dot_general(a, b, (((0,), (0,)), ((), ())), preferred_element_type=F32)


def nn(a, b):
    return jnp.dot(a, b, preferred_element_type=F32)


def parts(a):
    first = a.astype(BF16)
    return first, (a - first.astype(F32)).astype(BF16)


def low_half(shape):
    return lax.broadcasted_iota(jnp.int32, shape, len(shape) - 2) < HALF


class Copies:
    def __init__(self, sems):
        self.sems = sems
        self.count = 0

    def start(self, source, target):
        copy = pltpu.make_async_copy(source, target, self.sems.at[self.count])
        self.count += 1
        copy.start()
        return copy


def start_kernel(
    mult_hbm, table_hbm, incr_hbm, wind_hbm,
    whole_hbm, spec_hbm, head_hbm, tail_hbm,
    mult_ref, table_ref, edge_ref, flat_ref, spec_ref, head_ref, tail_ref, sems,
):
    levels, rows, width = mult_ref.shape
    half = levels // 2
    copies = Copies(sems)
    mult_in = copies.start(mult_hbm, mult_ref)
    table_in = copies.start(table_hbm, table_ref)
    edge_in = [
        copies.start(source.at[:, pl.ds(at, 8), :], edge_ref.at[i])
        for i, (source, at) in enumerate(
            [(incr_hbm, 0), (wind_hbm, 0), (incr_hbm, rows - 8), (wind_hbm, rows - 8)]
        )
    ]
    out = []
    mult_in.wait()
    flat_ref[...] = mult_ref[...].reshape(levels * rows, width).astype(BF16)
    out.append(copies.start(flat_ref, whole_hbm.at[pl.ds(0, levels * rows)]))
    first = mult_ref[:, :8, :]
    last = mult_ref[:, rows - 8 :, :]
    low = low_half((half, 8, width))
    head = jnp.where(low, first[:half], pltpu.roll(first[half:], HALF, 1))
    tail = jnp.where(low, pltpu.roll(last[half:], HALF, 1), last[:half])
    head_ref[levels * 8 :] = head.reshape(half * 8, width).astype(BF16)
    tail_ref[levels * 8 :] = tail.reshape(half * 8, width).astype(BF16)
    flat = flat_ref[...]
    table_in.wait()
    for i in range(2):
        part = pl.ds(512 * i, 512)
        spec_ref[part] = nt(table_ref[part], flat).astype(BF16)
        out.append(copies.start(spec_ref.at[part], spec_hbm.at[part]))
    for copy in edge_in:
        copy.wait()
    low = low_half((levels, 8, width))
    head = jnp.where(low, edge_ref[0], pltpu.roll(edge_ref[1], HALF, 1))
    tail = jnp.where(low, pltpu.roll(edge_ref[3], HALF, 1), edge_ref[2])
    head_ref[: levels * 8] = head.reshape(levels * 8, width).astype(BF16)
    tail_ref[: levels * 8] = tail.reshape(levels * 8, width).astype(BF16)
    out.append(copies.start(head_ref, head_hbm))
    out.append(copies.start(tail_ref, tail_hbm))
    for copy in out:
        copy.wait()


TILES = 5


def spread_rows(stage_ref, main, margin):
    rows, width = main.shape
    across = width // 128
    for c in range(across):
        stage_ref[c, :rows, :] = main[:, c * 128 : (c + 1) * 128]
        stage_ref[c, rows:, :] = margin[:, c * 128 : (c + 1) * 128]
    return [[stage_ref[c, pl.ds(t, 8, stride=TILES), :] for t in range(TILES)] for c in range(across)]


def join_rows(stage_ref, tiles, rows):
    for c, column in enumerate(tiles):
        for t, tile in enumerate(column):
            stage_ref[c, pl.ds(t, 8, stride=TILES), :] = tile * (0.2**STEPS)
    return jnp.concatenate([stage_ref[c, :rows, :] for c in range(len(tiles))], axis=1)


def coefficients(level, levels, wind_ref, head_ref, tail_ref, stage_ref, coef_ref):
    rows = wind_ref.shape[1]
    low = low_half((8, wind_ref.shape[2]))
    sublane = lax.broadcasted_iota(jnp.int32, (8, 128), 0)

    def extended(index, stage):
        at = pl.ds(pl.multiple_of(index * 8, 8), 8)
        margin = pltpu.roll(jnp.where(low, tail_ref[at, :], head_ref[at, :]), HALF, 0)
        return spread_rows(stage, wind_ref[index], margin)

    u = extended(level, stage_ref.at[0])
    v = extended(level + levels // 2, stage_ref.at[1])
    place = lax.axis_index("space")
    first = (sublane == 0) & (place == 0)
    last = (sublane == (rows - 1) // TILES) & (place == lax.axis_size("space") - 1)
    for c in range(len(u)):
        for t in range(TILES):
            north, south = 1.0 - v[c][t], 1.0 + v[c][t]
            if t == (rows - 1) % TILES:
                north = jnp.where(last, 0.0, north)
            if t == 0:
                south = jnp.where(first, 0.0, south)
            coef_ref[0, c, t] = 1.0 - u[c][t]
            coef_ref[1, c, t] = 1.0 + u[c][t]
            coef_ref[2, c, t] = north
            coef_ref[3, c, t] = south


def north_of(column, t):
    return column[t + 1] if t < TILES - 1 else pltpu.roll(column[0], 7, 0)


def south_of(column, t):
    return column[t - 1] if t > 0 else pltpu.roll(column[TILES - 1], 1, 0)


def forward_steps(x, coef_ref):
    lane = lax.broadcasted_iota(jnp.int32, (8, 128), 1)
    first, last = lane == 0, lane == 127
    ends = len(x) - 1
    for _ in range(STEPS):
        new = []
        for c in range(len(x)):
            column = []
            for t in range(TILES):
                here = x[c][t]
                east = pltpu.roll(jnp.where(first, x[c + 1][t] if c < ends else 0.0, here), 127, 1)
                west = pltpu.roll(jnp.where(last, x[c - 1][t] if c > 0 else 0.0, here), 1, 1)
                column.append(
                    (here + coef_ref[0, c, t] * east)
                    + coef_ref[1, c, t] * west
                    + (coef_ref[2, c, t] * north_of(x[c], t) + coef_ref[3, c, t] * south_of(x[c], t))
                )
            new.append(column)
        x = new
    return x


def backward_steps(y, coef_ref):
    lane = lax.broadcasted_iota(jnp.int32, (8, 128), 1)
    first, last = lane == 0, lane == 127
    ends = len(y) - 1
    for _ in range(STEPS):
        new = []
        for c in range(len(y)):
            column = []
            up = [coef_ref[3, c, t] * y[c][t] for t in range(TILES)]
            down = [coef_ref[2, c, t] * y[c][t] for t in range(TILES)]
            for t in range(TILES):
                here = y[c][t]
                after = coef_ref[1, c + 1, t] * y[c + 1][t] if c < ends else 0.0
                before = coef_ref[0, c - 1, t] * y[c - 1][t] if c > 0 else 0.0
                east = pltpu.roll(jnp.where(first, after, coef_ref[1, c, t] * here), 127, 1)
                west = pltpu.roll(jnp.where(last, before, coef_ref[0, c, t] * here), 1, 1)
                column.append((here + east) + west + (north_of(up, t) + south_of(down, t)))
            new.append(column)
        y = new
    return y


def one_hots(index, blocks):
    count = index.shape[1]
    high = lax.broadcasted_iota(jnp.int32, (blocks[0], count), 0) == (index >> 6)
    low = lax.broadcasted_iota(jnp.int32, (blocks[1], count), 0) == (index & 63)
    return high, low


def forward_kernel(
    incr_hbm, wind_hbm, head_hbm, tail_hbm, _whole_in, ends_hbm, whole_hbm,
    incr_ref, wind_ref, head_in, tail_in, far_ref, head_ref, tail_ref, stage_ref, coef_ref, ends_ref, sems, level_sems,
):
    levels, rows, width = incr_ref.shape
    half = levels // 2
    copies = Copies(sems)
    full = levels * rows
    near, far = pl.ds(0, levels * 8), pl.ds(levels * 8, levels * 4)
    margin_in = [copies.start(head_hbm.at[near], head_in), copies.start(tail_hbm.at[near], tail_in)]

    def fetch(kind, index):
        source, target = ((wind_hbm, wind_ref), (incr_hbm, incr_ref))[kind]
        return pltpu.make_async_copy(source.at[index], target.at[index], level_sems.at[kind, index])

    def put(index):
        part = pl.ds(pl.multiple_of(index * rows, rows), rows)
        return pltpu.make_async_copy(ends_ref.at[part], ends_hbm.at[part], level_sems.at[2, index])

    for level in range(half):
        for index in (level, level + half):
            for kind in range(2):
                fetch(kind, index).start()
    far_in = [
        copies.start(head_hbm.at[far], far_ref.at[pl.ds(0, levels * 4)]),
        copies.start(tail_hbm.at[far], far_ref.at[pl.ds(levels * 4, levels * 4)]),
    ]
    for copy in margin_in:
        copy.wait()
    head_ref[...] = head_in[...].astype(F32)
    tail_ref[...] = tail_in[...].astype(F32)
    low = low_half((8, width))

    def at_level(level, carry):
        for index in (level, level + half):
            for kind in range(2):
                fetch(kind, index).wait()
        coefficients(level, levels, wind_ref, head_ref, tail_ref, stage_ref, coef_ref)
        for group in range(2):
            index = level + group * half
            at = pl.ds(pl.multiple_of(index * 8, 8), 8)
            margin = jnp.where(low, head_ref[at, :], tail_ref[at, :])
            x = forward_steps(spread_rows(stage_ref.at[2 * group], incr_ref[index], margin), coef_ref)
            ends = join_rows(stage_ref.at[2 * group + 1], x, rows)
            ends_ref[pl.ds(pl.multiple_of(index * rows, rows), rows), :] = ends.astype(BF16)
            put(index).start()
        return carry

    for copy in far_in:
        copy.wait()
    joined = copies.start(far_ref, whole_hbm.at[pl.ds(full, levels * 8)])
    lax.fori_loop(0, half, at_level, 0)
    joined.wait()
    for index in range(levels):
        put(index).wait()


def backward_kernel(
    whole_hbm, wind_hbm, head_hbm, tail_hbm, mult_hbm, incr_hbm,
    index_ref, dual_ref, variance_ref, cols_hbm, lines_hbm,
    state_hbm, obs_ref,
    next_ref, wind_ref, mult_ref, incr_ref, cols_ref, lines_ref, head_in, tail_in, nhead_in, ntail_in,
    head_ref, tail_ref, nhead_ref, ntail_ref, stage_ref, coef_ref, spread_ref, state_ref, sems, level_sems,
):
    levels, rows, width = mult_ref.shape
    half = levels // 2
    copies = Copies(sems)
    block_in = [copies.start(cols_hbm, cols_ref), copies.start(lines_hbm, lines_ref)]
    full = levels * rows
    near, next_head, next_tail = pl.ds(0, levels * 8), pl.ds(full, levels * 4), pl.ds(full + levels * 4, levels * 4)
    margin_in = [
        copies.start(source, target)
        for source, target in (
            (head_hbm.at[near], head_in), (tail_hbm.at[near], tail_in),
            (whole_hbm.at[next_head], nhead_in), (whole_hbm.at[next_tail], ntail_in),
        )
    ]
    incr_in = copies.start(incr_hbm, incr_ref)
    fields_in = [
        copies.start(source, target)
        for source, target in ((wind_hbm, wind_ref), (whole_hbm.at[pl.ds(0, full)], next_ref), (mult_hbm, mult_ref))
    ]
    for copy in block_in:
        copy.wait()
    cols, lines = cols_ref[...], lines_ref[...]
    blocks = (lines.shape[0], cols.shape[1])
    high, low_hot = one_hots(index_ref[...], blocks)
    weights = low_hot.astype(BF16)
    summed = sum(nt(p, weights) for p in parts(jnp.where(high, dual_ref[...], 0.0))) * 0.125
    tall = sum(tn(lines, p) for p in parts(summed))
    spread_ref[...] = sum(nt(p, cols) for p in parts(tall))
    incr_in.wait()
    narrow = sum(nn(p, cols) for p in parts(incr_ref[...].reshape(levels * rows, width)))
    sums = sum(nn(lines, p) for p in parts(narrow))
    high = high.astype(BF16)
    picked = sum(tn(p, high) for p in parts(sums))
    observed = jnp.sum(jnp.where(low_hot, picked, 0.0), axis=0, keepdims=True) * 0.125
    obs_ref[...] = variance_ref[...] * dual_ref[...] + observed
    for copy in margin_in + fields_in:
        copy.wait()
    head_ref[...] = head_in[...].astype(F32)
    tail_ref[...] = tail_in[...].astype(F32)
    nhead_ref[...] = nhead_in[...].astype(F32)
    ntail_ref[...] = ntail_in[...].astype(F32)
    low = low_half((8, width))

    def put(index):
        return pltpu.make_async_copy(state_ref.at[index], state_hbm.at[index], level_sems.at[index])

    def at_level(level, carry):
        coefficients(level, levels, wind_ref, head_ref, tail_ref, stage_ref, coef_ref)
        at = pl.ds(pl.multiple_of(level * 8, 8), 8)
        head, tail = nhead_ref[at, :], ntail_ref[at, :]
        for group in range(2):
            index = level + group * half
            if group == 0:
                margin = jnp.where(low, head, tail)
            else:
                margin = pltpu.roll(jnp.where(low, tail, head), HALF, 0)
            part = pl.ds(pl.multiple_of(index * rows, rows), rows)
            y = backward_steps(spread_rows(stage_ref.at[2 * group], next_ref[part, :].astype(F32), margin), coef_ref)
            back = join_rows(stage_ref.at[2 * group + 1], y, rows)
            state_ref[index] = (mult_ref[index] - back) + spread_ref[part, :]
            put(index).start()
        return carry

    lax.fori_loop(0, half, at_level, 0)
    for index in range(levels):
        put(index).wait()


def gather_lines(came_in, came_ref, lines_ref):
    count, rows, wide = came_ref.shape
    groups, fields = count // 4, wide // 128
    source = lax.broadcasted_iota(jnp.int32, (512, 512), 0)
    target = lax.broadcasted_iota(jnp.int32, (512, 512), 1)
    swapped = ((target & 127) >> 5) * 128 + (target >> 7) * 32 + (target & 31)
    perm = (source == swapped).astype(BF16)
    came_in.wait()
    for g in range(fields):
        piece = came_ref[:, :, g * 128 : (g + 1) * 128].reshape(groups, 4, rows, 128)
        left = jnp.concatenate([piece[:, i].reshape(groups * rows, 128) for i in range(4)], axis=1)
        moved = nn(left, perm).astype(BF16)
        for i in range(4):
            for b in range(groups):
                lines_ref[(4 * g + i) * rows : (4 * g + i + 1) * rows, b * 128 : (b + 1) * 128] = moved[
                    b * rows : (b + 1) * rows, i * 128 : (i + 1) * 128
                ]


def latitude_kernel(
    came_hbm, var_hbm, turned_hbm, out_hbm,
    came_ref, var_ref, turned_ref, lines_ref, scaled_ref, out_ref, sems,
):
    copies = Copies(sems)
    came_in = copies.start(came_hbm, came_ref)
    turned_in = copies.start(turned_hbm, turned_ref)
    var_in = copies.start(var_hbm, var_ref)
    gather_lines(came_in, came_ref, lines_ref)
    turned_in.wait()
    latitude = nn(lines_ref[...], turned_ref[...])
    var_in.wait()
    scaled_ref[...] = (latitude * var_ref[...]).astype(BF16)
    scaled = scaled_ref[...]
    out = []
    for i in range(2):
        part = pl.ds(512 * i, 512)
        out_ref[part] = nt(turned_ref[part], scaled).astype(BF16)
        out.append(copies.start(out_ref.at[part], out_hbm.at[part]))
    for copy in out:
        copy.wait()


def finish_kernel(
    came_hbm, incr_hbm, prev_hbm, table_hbm, out_hbm,
    came_ref, incr_ref, prev_ref, table_ref, lines_ref, out_ref, sems,
):
    copies = Copies(sems)
    came_in = copies.start(came_hbm, came_ref)
    table_in = copies.start(table_hbm, table_ref)
    prev_in = copies.start(prev_hbm, prev_ref)
    incr_in = copies.start(incr_hbm, incr_ref)
    gather_lines(came_in, came_ref, lines_ref)
    table_in.wait()
    table = table_ref[...]
    out = []
    for i in range(3):
        part = pl.ds(128 * i, 128)
        covar = nn(lines_ref[part], table)
        if i == 0:
            prev_in.wait()
            incr_in.wait()
        out_ref[part] = covar + (incr_ref[part] - prev_ref[part].astype(F32))
        out.append(copies.start(out_ref.at[part], out_hbm.at[part]))
    for copy in out:
        copy.wait()


VMEM = pl.BlockSpec(memory_space=pltpu.VMEM)
HBM = pl.BlockSpec(memory_space=pl.ANY)


def call(kernel, outs, ins, scratch, name, aliases=None):
    def place(a):
        return VMEM if a.shape[0] == 1 else HBM

    return pl.pallas_call(
        kernel,
        out_shape=outs,
        in_specs=[place(a) for a in ins],
        out_specs=jax.tree.map(place, outs),
        scratch_shapes=list(scratch),
        compiler_params=pltpu.CompilerParams(vmem_limit_bytes=60 * 1024 * 1024),
        input_output_aliases=aliases or {},
        name=name,
    )(*ins)


def local(increment, multiplier, obs_dual, obs_index, obs_variance, winds, spectral_var):
    rows, levels, width = increment.shape[1:]
    count = lax.axis_size("space")
    times = lax.axis_size("tm")
    lat = rows * count
    waves = width // count
    full = levels * rows
    incr = jnp.transpose(increment[0], (1, 0, 2))
    mult = jnp.transpose(multiplier[0], (1, 0, 2))
    wind = jnp.transpose(winds[0], (1, 0, 2))
    var = jnp.transpose(spectral_var, (1, 2, 0)).reshape(full, lat)
    table = cosine_table(width)
    turned = np.ascontiguousarray(table.T)
    cols, lines = block_sums(levels, rows, width)

    def shape(*dims):
        return jax.ShapeDtypeStruct(dims, BF16)

    def wide(*dims):
        return pltpu.VMEM(dims, F32)

    def short(*dims):
        return pltpu.VMEM(dims, BF16)

    def sems(*dims):
        return pltpu.SemaphoreType.DMA(dims)

    field = (levels, rows, width)
    whole, spec, head, tail = call(
        start_kernel,
        (
            shape(full + levels * 8, width), shape(width, full), shape(levels * 12, width),
            shape(levels * 12, width),
        ),
        (mult, table, incr, wind),
        [
            wide(*field), short(width, width), wide(4, levels, 8, width), short(full, width), short(width, full),
            short(levels * 12, width), short(levels * 12, width), sems(12),
        ],
        "start",
    )
    came = lax.all_to_all(spec.reshape(count, waves, full), "space", 0, 0, tiled=True)
    ring = range(count - 1)
    head = lax.ppermute(head, "space", [(i + 1, i) for i in ring])
    tail = lax.ppermute(tail, "space", [(i, i + 1) for i in ring])

    across = width // 128
    stages = [wide(4, across, rows + 8, 128), wide(4, across, TILES, 8, 128)]
    ends, whole = call(
        forward_kernel,
        (shape(full, width), shape(full + levels * 8, width)),
        (incr, wind, head, tail, whole),
        [
            wide(*field), wide(*field), short(levels * 8, width), short(levels * 8, width), short(levels * 8, width),
            wide(levels * 8, width), wide(levels * 8, width), *stages, short(full, width), sems(5), sems(3, levels),
        ],
        "forward",
        {4: 1},
    )
    coming = lax.ppermute(whole, "tm", [(t + 1, t) for t in range(times - 1)])
    previous = lax.ppermute(ends, "tm", [(t, t + 1) for t in range(times - 1)])

    back = call(
        latitude_kernel,
        shape(lat, full),
        (came, var, turned),
        [
            short(count, waves, full), wide(full, lat), short(lat, lat), short(full, lat), short(full, lat),
            short(lat, full), sems(16),
        ],
        "latitude",
    )
    returned = lax.all_to_all(back.reshape(count, rows, full), "space", 0, 0, tiled=True)

    state_rows, obs_rows = call(
        backward_kernel,
        (jax.ShapeDtypeStruct(field, F32), jax.ShapeDtypeStruct(obs_dual.shape, F32)),
        (
            coming, wind, head, tail, mult, incr, obs_index, obs_dual, obs_variance, cols, lines,
        ),
        [
            short(full, width), wide(*field), wide(*field), wide(*field), short(*cols.shape), short(*lines.shape),
            short(levels * 8, width), short(levels * 8, width), short(levels * 4, width), short(levels * 4, width),
            wide(levels * 8, width), wide(levels * 8, width), wide(levels * 4, width), wide(levels * 4, width),
            *stages, wide(full, width), wide(*field), sems(16), sems(levels),
        ],
        "backward",
    )
    model_rows = call(
        finish_kernel,
        jax.ShapeDtypeStruct((full, width), F32),
        (returned, incr.reshape(full, width), previous, table),
        [
            short(count, rows, full), wide(full, width), short(full, width), short(width, width),
            short(full, width), wide(full, width), sems(20),
        ],
        "finish",
    )

    def placed(whole):
        return jnp.transpose(whole.reshape(field), (1, 0, 2))[None]

    return (placed(model_rows), obs_rows, placed(state_rows))


def solution(mesh):
    specs = (
        P("tm", "space", None, None),
        P("tm", "space", None, None),
        P("tm", "space"),
        P("tm", "space"),
        P("tm", "space"),
        P("tm", "space", None, None),
        P(None, None, "space"),
    )
    return jax.shard_map(
        local,
        mesh=mesh,
        in_specs=specs,
        out_specs=(P("tm", "space", None, None), P("tm", "space"), P("tm", "space", None, None)),
        check_vma=False,
    )
```

```python
import math

import jax
import jax.numpy as jnp
import numpy as np
from jax import lax
from jax.experimental import pallas as pl
from jax.experimental.pallas import tpu as pltpu
from jax.sharding import PartitionSpec as P
import ml_dtypes

STEPS = 4
HALF = 4
F32 = jnp.float32
BF16 = jnp.bfloat16


def cosine_table(count):
    wave = np.arange(count)[:, None]
    point = np.arange(count)[None, :]
    phase = (2 * point + 1) * wave % (4 * count)
    table = np.cos(phase * (math.pi / (2.0 * count))) * math.sqrt(2.0 / count)
    table = np.where(wave == 0, table * math.sqrt(0.5), table)
    return table.astype(np.float32).astype(ml_dtypes.bfloat16)


def block_sums(levels, rows, width):
    cols = (np.arange(width)[:, None] // 16 == np.arange(width // 16)[None, :]).astype(np.float32)
    out = np.arange(rows // 4 * levels)[:, None]
    inn = np.arange(levels * rows)[None, :]
    lines = ((out % levels == inn // rows) & (out // levels == inn % rows // 4)).astype(np.float32)
    return cols.astype(ml_dtypes.bfloat16), lines.astype(ml_dtypes.bfloat16)


def nt(a, b):
    return lax.dot_general(a, b, (((1,), (1,)), ((), ())), preferred_element_type=F32)


def tn(a, b):
    return lax.dot_general(a, b, (((0,), (0,)), ((), ())), preferred_element_type=F32)


def nn(a, b):
    return jnp.dot(a, b, preferred_element_type=F32)


def parts(a):
    first = a.astype(BF16)
    return first, (a - first.astype(F32)).astype(BF16)


def low_half(shape):
    return lax.broadcasted_iota(jnp.int32, shape, len(shape) - 2) < HALF


class Copies:
    def __init__(self, sems):
        self.sems = sems
        self.count = 0

    def start(self, source, target):
        copy = pltpu.make_async_copy(source, target, self.sems.at[self.count])
        self.count += 1
        copy.start()
        return copy


def edge_kernel(mult_hbm, incr_hbm, wind_hbm, head_hbm, tail_hbm, edge_ref, head_ref, tail_ref, sems):
    levels, rows, width = mult_hbm.shape
    half = levels // 2
    copies = Copies(sems)
    coming = [
        copies.start(source.at[:, pl.ds(at, 8), :], edge_ref.at[3 * end + i])
        for end, at in enumerate((0, rows - 8))
        for i, source in enumerate((incr_hbm, wind_hbm, mult_hbm))
    ]
    out = []
    for end, (part_ref, part_hbm) in enumerate(((head_ref, head_hbm), (tail_ref, tail_hbm))):
        for copy in coming[3 * end : 3 * end + 3]:
            copy.wait()
        incr, wind, mult = edge_ref[3 * end], edge_ref[3 * end + 1], edge_ref[3 * end + 2]
        wind = pltpu.roll(wind, HALF, 1)
        second = pltpu.roll(mult[half:], HALF, 1)
        low, less = low_half((levels, 8, width)), low_half((half, 8, width))
        if end == 0:
            field, dual = jnp.where(low, incr, wind), jnp.where(less, mult[:half], second)
        else:
            field, dual = jnp.where(low, wind, incr), jnp.where(less, second, mult[:half])
        part_ref[: levels * 8] = field.reshape(levels * 8, width).astype(BF16)
        part_ref[levels * 8 :] = dual.reshape(half * 8, width).astype(BF16)
        out.append(copies.start(part_ref, part_hbm))
    for copy in out:
        copy.wait()


def start_kernel(mult_hbm, table_hbm, _after, flat_hbm, spec_hbm, mult_ref, table_ref, flat_ref, spec_ref, sems):
    levels, rows, width = mult_ref.shape
    copies = Copies(sems)
    mult_in = copies.start(mult_hbm, mult_ref)
    table_in = copies.start(table_hbm, table_ref)
    mult_in.wait()
    flat_ref[...] = mult_ref[...].reshape(levels * rows, width).astype(BF16)
    out = [copies.start(flat_ref, flat_hbm)]
    flat = flat_ref[...]
    table_in.wait()
    for i in range(2):
        part = pl.ds(512 * i, 512)
        spec_ref[part] = nt(table_ref[part], flat).astype(BF16)
        out.append(copies.start(spec_ref.at[part], spec_hbm.at[part]))
    for copy in out:
        copy.wait()


def order_kernel(_spec_in, _head, _tail, _spec_out):
    pass


TILES = 5


def spread_rows(stage_ref, main, margin):
    rows, width = main.shape
    across = width // 128
    for c in range(across):
        stage_ref[c, :rows, :] = main[:, c * 128 : (c + 1) * 128]
        stage_ref[c, rows:, :] = margin[:, c * 128 : (c + 1) * 128]
    return [[stage_ref[c, pl.ds(t, 8, stride=TILES), :] for t in range(TILES)] for c in range(across)]


def join_rows(stage_ref, tiles, rows):
    for c, column in enumerate(tiles):
        for t, tile in enumerate(column):
            stage_ref[c, pl.ds(t, 8, stride=TILES), :] = tile * (0.2**STEPS)
    return jnp.concatenate([stage_ref[c, :rows, :] for c in range(len(tiles))], axis=1)


def coefficients(level, levels, wind_ref, head_ref, tail_ref, stage_ref, coef_ref):
    rows = wind_ref.shape[1]
    low = low_half((8, wind_ref.shape[2]))
    sublane = lax.broadcasted_iota(jnp.int32, (8, 128), 0)

    def extended(index, stage):
        at = pl.ds(pl.multiple_of(index * 8, 8), 8)
        margin = pltpu.roll(jnp.where(low, tail_ref[at, :], head_ref[at, :]), HALF, 0)
        return spread_rows(stage, wind_ref[index], margin)

    u = extended(level, stage_ref.at[0])
    v = extended(level + levels // 2, stage_ref.at[1])
    place = lax.axis_index("space")
    first = (sublane == 0) & (place == 0)
    last = (sublane == (rows - 1) // TILES) & (place == lax.axis_size("space") - 1)
    for c in range(len(u)):
        for t in range(TILES):
            north, south = 1.0 - v[c][t], 1.0 + v[c][t]
            if t == (rows - 1) % TILES:
                north = jnp.where(last, 0.0, north)
            if t == 0:
                south = jnp.where(first, 0.0, south)
            coef_ref[0, c, t] = 1.0 - u[c][t]
            coef_ref[1, c, t] = 1.0 + u[c][t]
            coef_ref[2, c, t] = north
            coef_ref[3, c, t] = south


def north_of(column, t):
    return column[t + 1] if t < TILES - 1 else pltpu.roll(column[0], 7, 0)


def south_of(column, t):
    return column[t - 1] if t > 0 else pltpu.roll(column[TILES - 1], 1, 0)


def forward_steps(x, coef_ref):
    lane = lax.broadcasted_iota(jnp.int32, (8, 128), 1)
    first, last = lane == 0, lane == 127
    ends = len(x) - 1
    for _ in range(STEPS):
        new = []
        for c in range(len(x)):
            column = []
            for t in range(TILES):
                here = x[c][t]
                east = pltpu.roll(jnp.where(first, x[c + 1][t] if c < ends else 0.0, here), 127, 1)
                west = pltpu.roll(jnp.where(last, x[c - 1][t] if c > 0 else 0.0, here), 1, 1)
                column.append(
                    (here + coef_ref[0, c, t] * east)
                    + coef_ref[1, c, t] * west
                    + (coef_ref[2, c, t] * north_of(x[c], t) + coef_ref[3, c, t] * south_of(x[c], t))
                )
            new.append(column)
        x = new
    return x


def backward_steps(y, coef_ref):
    lane = lax.broadcasted_iota(jnp.int32, (8, 128), 1)
    first, last = lane == 0, lane == 127
    ends = len(y) - 1
    for _ in range(STEPS):
        new = []
        for c in range(len(y)):
            column = []
            up = [coef_ref[3, c, t] * y[c][t] for t in range(TILES)]
            down = [coef_ref[2, c, t] * y[c][t] for t in range(TILES)]
            for t in range(TILES):
                here = y[c][t]
                after = coef_ref[1, c + 1, t] * y[c + 1][t] if c < ends else 0.0
                before = coef_ref[0, c - 1, t] * y[c - 1][t] if c > 0 else 0.0
                east = pltpu.roll(jnp.where(first, after, coef_ref[1, c, t] * here), 127, 1)
                west = pltpu.roll(jnp.where(last, before, coef_ref[0, c, t] * here), 1, 1)
                column.append((here + east) + west + (north_of(up, t) + south_of(down, t)))
            new.append(column)
        y = new
    return y


def one_hots(index, blocks):
    count = index.shape[1]
    high = lax.broadcasted_iota(jnp.int32, (blocks[0], count), 0) == (index >> 6)
    low = lax.broadcasted_iota(jnp.int32, (blocks[1], count), 0) == (index & 63)
    return high, low


def forward_kernel(
    incr_hbm, wind_hbm, head_hbm, tail_hbm, ends_hbm, far_hbm,
    incr_ref, wind_ref, head_in, tail_in, far_ref, head_ref, tail_ref, stage_ref, coef_ref, ends_ref, sems, level_sems,
):
    levels, rows, width = incr_ref.shape
    half = levels // 2
    copies = Copies(sems)
    near, far = pl.ds(0, levels * 8), pl.ds(levels * 8, levels * 4)
    margin_in = [copies.start(head_hbm.at[near], head_in), copies.start(tail_hbm.at[near], tail_in)]

    def fetch(kind, index):
        source, target = ((wind_hbm, wind_ref), (incr_hbm, incr_ref))[kind]
        return pltpu.make_async_copy(source.at[index], target.at[index], level_sems.at[kind, index])

    def put(index):
        part = pl.ds(pl.multiple_of(index * rows, rows), rows)
        return pltpu.make_async_copy(ends_ref.at[part], ends_hbm.at[part], level_sems.at[2, index])

    for level in range(half):
        for index in (level, level + half):
            for kind in range(2):
                fetch(kind, index).start()
    far_in = [
        copies.start(head_hbm.at[far], far_ref.at[pl.ds(0, levels * 4)]),
        copies.start(tail_hbm.at[far], far_ref.at[pl.ds(levels * 4, levels * 4)]),
    ]
    for copy in margin_in:
        copy.wait()
    head_ref[...] = head_in[...].astype(F32)
    tail_ref[...] = tail_in[...].astype(F32)
    low = low_half((8, width))

    def at_level(level, carry):
        for index in (level, level + half):
            for kind in range(2):
                fetch(kind, index).wait()
        coefficients(level, levels, wind_ref, head_ref, tail_ref, stage_ref, coef_ref)

        def at_group(group):
            index = level + group * half
            at = pl.ds(pl.multiple_of(index * 8, 8), 8)
            margin = jnp.where(low, head_ref[at, :], tail_ref[at, :])
            x = forward_steps(spread_rows(stage_ref.at[2 + 2 * group], incr_ref[index], margin), coef_ref)
            ends = join_rows(stage_ref.at[3 + 2 * group], x, rows)
            ends_ref[pl.ds(pl.multiple_of(index * rows, rows), rows), :] = ends.astype(BF16)
            put(index).start()

        for group in range(2):
            at_group(group)
        return carry

    for copy in far_in:
        copy.wait()
    joined = copies.start(far_ref, far_hbm)
    lax.fori_loop(0, half, at_level, 0)
    joined.wait()
    for index in range(levels):
        put(index).wait()


def observe_kernel(
    incr_hbm, index_ref, dual_ref, variance_ref, cols_hbm, lines_hbm, _after,
    tall_ref, obs_ref, incr_ref, cols_ref, lines_ref, sems,
):
    levels, rows, width = incr_ref.shape
    copies = Copies(sems)
    block_in = [copies.start(cols_hbm, cols_ref), copies.start(lines_hbm, lines_ref)]
    incr_in = copies.start(incr_hbm, incr_ref)
    for copy in block_in:
        copy.wait()
    cols, lines = cols_ref[...], lines_ref[...]
    blocks = (lines.shape[0], cols.shape[1])
    high, low_hot = one_hots(index_ref[...], blocks)
    weights = low_hot.astype(BF16)
    summed = sum(nt(p, weights) for p in parts(jnp.where(high, dual_ref[...], 0.0))) * 0.125
    tall_ref[...] = sum(tn(lines, p) for p in parts(summed))
    incr_in.wait()
    narrow = sum(nn(p, cols) for p in parts(incr_ref[...].reshape(levels * rows, width)))
    sums = sum(nn(lines, p) for p in parts(narrow))
    high = high.astype(BF16)
    picked = sum(tn(p, high) for p in parts(sums))
    observed = jnp.sum(jnp.where(low_hot, picked, 0.0), axis=0, keepdims=True) * 0.125
    obs_ref[...] = variance_ref[...] * dual_ref[...] + observed


def backward_kernel(
    coming_hbm, far_hbm, wind_hbm, head_hbm, tail_hbm, mult_hbm, tall_ref, cols_hbm,
    state_hbm,
    next_ref, wind_ref, mult_ref, cols_ref, head_in, tail_in, far_in,
    head_ref, tail_ref, far_ref, margins_ref, stage_ref, coef_ref, spread_ref, state_ref, sems, level_sems,
):
    levels, rows, width = mult_ref.shape
    half = levels // 2
    copies = Copies(sems)
    near = pl.ds(0, levels * 8)
    arriving = [
        copies.start(source, target)
        for source, target in (
            (cols_hbm, cols_ref), (head_hbm.at[near], head_in), (tail_hbm.at[near], tail_in),
            (far_hbm, far_in), (wind_hbm, wind_ref), (coming_hbm, next_ref), (mult_hbm, mult_ref),
        )
    ]
    arriving[0].wait()
    spread_ref[...] = sum(nt(p, cols_ref[...]) for p in parts(tall_ref[...]))
    for copy in arriving[1:]:
        copy.wait()
    head_ref[...] = head_in[...].astype(F32)
    tail_ref[...] = tail_in[...].astype(F32)
    far_ref[...] = far_in[...].astype(F32)
    low = low_half((8, width))

    def put(index):
        return pltpu.make_async_copy(state_ref.at[index], state_hbm.at[index], level_sems.at[index])

    def at_level(level, carry):
        coefficients(level, levels, wind_ref, head_ref, tail_ref, stage_ref, coef_ref)
        at = pl.ds(pl.multiple_of(level * 8, 8), 8)
        head, tail = far_ref[at, :], far_ref[pl.ds(pl.multiple_of(level * 8 + levels * 4, 8), 8), :]
        margins_ref[0] = jnp.where(low, head, tail)
        margins_ref[1] = pltpu.roll(jnp.where(low, tail, head), HALF, 0)

        def at_group(group):
            index = level + group * half
            part = pl.ds(pl.multiple_of(index * rows, rows), rows)
            main = next_ref[part, :].astype(F32)
            y = backward_steps(spread_rows(stage_ref.at[2 + 2 * group], main, margins_ref[group]), coef_ref)
            back = join_rows(stage_ref.at[3 + 2 * group], y, rows)
            state_ref[index] = (mult_ref[index] - back) + spread_ref[part, :]
            put(index).start()

        for group in range(2):
            at_group(group)
        return carry

    lax.fori_loop(0, half, at_level, 0)
    for index in range(levels):
        put(index).wait()


def gather_lines(came_in, came_ref, lines_ref):
    count, rows, wide = came_ref.shape
    groups, fields = count // 4, wide // 128
    source = lax.broadcasted_iota(jnp.int32, (512, 512), 0)
    target = lax.broadcasted_iota(jnp.int32, (512, 512), 1)
    swapped = ((target & 127) >> 5) * 128 + (target >> 7) * 32 + (target & 31)
    perm = (source == swapped).astype(BF16)
    came_in.wait()
    for g in range(fields):
        piece = came_ref[:, :, g * 128 : (g + 1) * 128].reshape(groups, 4, rows, 128)
        left = jnp.concatenate([piece[:, i].reshape(groups * rows, 128) for i in range(4)], axis=1)
        moved = nn(left, perm).astype(BF16)
        for i in range(4):
            for b in range(groups):
                lines_ref[(4 * g + i) * rows : (4 * g + i + 1) * rows, b * 128 : (b + 1) * 128] = moved[
                    b * rows : (b + 1) * rows, i * 128 : (i + 1) * 128
                ]


def latitude_kernel(
    came_hbm, var_hbm, turned_hbm, out_hbm,
    came_ref, var_ref, turned_ref, lines_ref, scaled_ref, out_ref, sems,
):
    copies = Copies(sems)
    came_in = copies.start(came_hbm, came_ref)
    turned_in = copies.start(turned_hbm, turned_ref)
    var_in = copies.start(var_hbm, var_ref)
    gather_lines(came_in, came_ref, lines_ref)
    turned_in.wait()
    latitude = nn(lines_ref[...], turned_ref[...])
    var_in.wait()
    scaled_ref[...] = (latitude * var_ref[...]).astype(BF16)
    scaled = scaled_ref[...]
    out = []
    for i in range(2):
        part = pl.ds(512 * i, 512)
        out_ref[part] = nt(turned_ref[part], scaled).astype(BF16)
        out.append(copies.start(out_ref.at[part], out_hbm.at[part]))
    for copy in out:
        copy.wait()


def finish_kernel(
    came_hbm, incr_hbm, prev_hbm, table_hbm, out_hbm,
    came_ref, incr_ref, prev_ref, table_ref, lines_ref, out_ref, sems,
):
    copies = Copies(sems)
    came_in = copies.start(came_hbm, came_ref)
    table_in = copies.start(table_hbm, table_ref)
    prev_in = copies.start(prev_hbm, prev_ref)
    incr_in = copies.start(incr_hbm, incr_ref)
    gather_lines(came_in, came_ref, lines_ref)
    table_in.wait()
    table = table_ref[...]
    out = []
    for i in range(3):
        part = pl.ds(128 * i, 128)
        covar = nn(lines_ref[part], table)
        if i == 0:
            prev_in.wait()
            incr_in.wait()
        out_ref[part] = covar + (incr_ref[part] - prev_ref[part].astype(F32))
        out.append(copies.start(out_ref.at[part], out_hbm.at[part]))
    for copy in out:
        copy.wait()


VMEM = pl.BlockSpec(memory_space=pltpu.VMEM)
HBM = pl.BlockSpec(memory_space=pl.ANY)


def call(kernel, outs, ins, scratch, name, aliases=None):
    def place(a):
        return VMEM if a.shape[0] == 1 or (len(a.shape) == 2 and a.shape[1] < 128 and a.dtype == F32) else HBM

    return pl.pallas_call(
        kernel,
        out_shape=outs,
        in_specs=[place(a) for a in ins],
        out_specs=jax.tree.map(place, outs),
        scratch_shapes=list(scratch),
        input_output_aliases=aliases or {},
        name=name,
    )(*ins)


def local(increment, multiplier, obs_dual, obs_index, obs_variance, winds, spectral_var):
    rows, levels, width = increment.shape[1:]
    count = lax.axis_size("space")
    times = lax.axis_size("tm")
    lat = rows * count
    waves = width // count
    full = levels * rows
    incr = jnp.transpose(increment[0], (1, 0, 2))
    mult = jnp.transpose(multiplier[0], (1, 0, 2))
    wind = jnp.transpose(winds[0], (1, 0, 2))
    var = jnp.transpose(spectral_var, (1, 2, 0)).reshape(full, lat)
    table = cosine_table(width)
    turned = np.ascontiguousarray(table.T)
    cols, lines = block_sums(levels, rows, width)

    def shape(*dims):
        return jax.ShapeDtypeStruct(dims, BF16)

    def wide(*dims):
        return pltpu.VMEM(dims, F32)

    def short(*dims):
        return pltpu.VMEM(dims, BF16)

    def sems(*dims):
        return pltpu.SemaphoreType.DMA(dims)

    field = (levels, rows, width)
    head, tail = call(
        edge_kernel,
        (shape(levels * 12, width), shape(levels * 12, width)),
        (mult, incr, wind),
        [wide(6, levels, 8, width), short(levels * 12, width), short(levels * 12, width), sems(8)],
        "edges",
    )
    flat, spec = call(
        start_kernel,
        (shape(full, width), shape(width, full)),
        (mult, table, head),
        [wide(*field), short(width, width), short(full, width), short(width, full), sems(8)],
        "start",
    )
    ring = range(count - 1)
    head = lax.ppermute(head, "space", [(i + 1, i) for i in ring])
    tail = lax.ppermute(tail, "space", [(i, i + 1) for i in ring])
    spec = call(order_kernel, shape(width, full), (spec, head, tail), [], "order", {0: 0})
    came = lax.all_to_all(spec.reshape(count, waves, full), "space", 0, 0, tiled=True)
    coming = lax.ppermute(flat, "tm", [(t + 1, t) for t in range(times - 1)])

    across = width // 128
    stages = [wide(6, across, rows + 8, 128), wide(4, across, TILES, 8, 128)]
    ends, far = call(
        forward_kernel,
        (shape(full, width), shape(levels * 8, width)),
        (incr, wind, head, tail),
        [
            wide(*field), wide(*field), short(levels * 8, width), short(levels * 8, width), short(levels * 8, width),
            wide(levels * 8, width), wide(levels * 8, width), *stages, short(full, width), sems(5), sems(3, levels),
        ],
        "forward",
    )
    far = lax.ppermute(far, "tm", [(t + 1, t) for t in range(times - 1)])
    previous = lax.ppermute(ends, "tm", [(t, t + 1) for t in range(times - 1)])

    back = call(
        latitude_kernel,
        shape(lat, full),
        (came, var, turned),
        [
            short(count, waves, full), wide(full, lat), short(lat, lat), short(full, lat), short(full, lat),
            short(lat, full), sems(16),
        ],
        "latitude",
    )
    returned = lax.all_to_all(back.reshape(count, rows, full), "space", 0, 0, tiled=True)

    tall, obs_rows = call(
        observe_kernel,
        (jax.ShapeDtypeStruct((full, cols.shape[1]), F32), jax.ShapeDtypeStruct(obs_dual.shape, F32)),
        (incr, obs_index, obs_dual, obs_variance, cols, lines, back),
        [wide(*field), short(*cols.shape), short(*lines.shape), sems(3)],
        "observe",
    )
    state_rows = call(
        backward_kernel,
        jax.ShapeDtypeStruct(field, F32),
        (coming, far, wind, head, tail, mult, tall, cols),
        [
            short(full, width), wide(*field), wide(*field), short(*cols.shape),
            short(levels * 8, width), short(levels * 8, width), short(levels * 8, width),
            wide(levels * 8, width), wide(levels * 8, width), wide(levels * 8, width), wide(2, 8, width),
            *stages, wide(full, width), wide(*field), sems(8), sems(levels),
        ],
        "backward",
    )
    model_rows = call(
        finish_kernel,
        jax.ShapeDtypeStruct((full, width), F32),
        (returned, incr.reshape(full, width), previous, table),
        [
            short(count, rows, full), wide(full, width), short(full, width), short(width, width),
            short(full, width), wide(full, width), sems(20),
        ],
        "finish",
    )

    def placed(whole):
        return jnp.transpose(whole.reshape(field), (1, 0, 2))[None]

    return (placed(model_rows), obs_rows, placed(state_rows))


def solution(mesh):
    specs = (
        P("tm", "space", None, None),
        P("tm", "space", None, None),
        P("tm", "space"),
        P("tm", "space"),
        P("tm", "space"),
        P("tm", "space", None, None),
        P(None, None, "space"),
    )
    return jax.shard_map(
        local,
        mesh=mesh,
        in_specs=specs,
        out_specs=(P("tm", "space", None, None), P("tm", "space"), P("tm", "space", None, None)),
        check_vma=False,
    )
```

```python
import math

import jax
import jax.numpy as jnp
import numpy as np
from jax import lax
from jax.experimental import pallas as pl
from jax.experimental.pallas import tpu as pltpu
from jax.sharding import PartitionSpec as P
import ml_dtypes

STEPS = 4
HALF = 4
F32 = jnp.float32
BF16 = jnp.bfloat16


def cosine_table(count):
    wave = np.arange(count)[:, None]
    point = np.arange(count)[None, :]
    phase = (2 * point + 1) * wave % (4 * count)
    table = np.cos(phase * (math.pi / (2.0 * count))) * math.sqrt(2.0 / count)
    table = np.where(wave == 0, table * math.sqrt(0.5), table)
    return table.astype(np.float32).astype(ml_dtypes.bfloat16)


def block_sums(levels, rows, width):
    cols = (np.arange(width)[:, None] // 16 == np.arange(width // 16)[None, :]).astype(np.float32)
    out = np.arange(rows // 4 * levels)[:, None]
    inn = np.arange(levels * rows)[None, :]
    lines = ((out % levels == inn // rows) & (out // levels == inn % rows // 4)).astype(np.float32)
    return cols.astype(ml_dtypes.bfloat16), lines.astype(ml_dtypes.bfloat16)


def nt(a, b):
    return lax.dot_general(a, b, (((1,), (1,)), ((), ())), preferred_element_type=F32)


def tn(a, b):
    return lax.dot_general(a, b, (((0,), (0,)), ((), ())), preferred_element_type=F32)


def nn(a, b):
    return jnp.dot(a, b, preferred_element_type=F32)


def parts(a):
    first = a.astype(BF16)
    return first, (a - first.astype(F32)).astype(BF16)


def low_half(shape):
    return lax.broadcasted_iota(jnp.int32, shape, len(shape) - 2) < HALF


class Copies:
    def __init__(self, sems):
        self.sems = sems
        self.count = 0

    def start(self, source, target):
        copy = pltpu.make_async_copy(source, target, self.sems.at[self.count])
        self.count += 1
        copy.start()
        return copy


def edge_kernel(mult_hbm, incr_hbm, wind_hbm, head_ref, tail_ref, edge_ref, sems):
    levels, rows, width = mult_hbm.shape
    half = levels // 2
    copies = Copies(sems)
    coming = [
        copies.start(source.at[:, pl.ds(at, 8), :], edge_ref.at[3 * end + i])
        for end, at in enumerate((0, rows - 8))
        for i, source in enumerate((incr_hbm, wind_hbm, mult_hbm))
    ]
    for end, part_ref in enumerate((head_ref, tail_ref)):
        for copy in coming[3 * end : 3 * end + 3]:
            copy.wait()
        incr, wind, mult = edge_ref[3 * end], edge_ref[3 * end + 1], edge_ref[3 * end + 2]
        wind = pltpu.roll(wind, HALF, 1)
        second = pltpu.roll(mult[half:], HALF, 1)
        low, less = low_half((levels, 8, width)), low_half((half, 8, width))
        if end == 0:
            field, dual = jnp.where(low, incr, wind), jnp.where(less, mult[:half], second)
        else:
            field, dual = jnp.where(low, wind, incr), jnp.where(less, second, mult[:half])
        part_ref[: levels * 8] = field.reshape(levels * 8, width).astype(BF16)
        part_ref[levels * 8 :] = dual.reshape(half * 8, width).astype(BF16)


def start_kernel(mult_hbm, table_hbm, _after, whole_hbm, spec_hbm, mult_ref, table_ref, flat_ref, spec_ref, sems):
    levels, rows, width = mult_ref.shape
    copies = Copies(sems)
    mult_in = copies.start(mult_hbm, mult_ref)
    table_in = copies.start(table_hbm, table_ref)
    mult_in.wait()
    flat_ref[...] = mult_ref[...].reshape(levels * rows, width).astype(BF16)
    out = [copies.start(flat_ref, whole_hbm.at[pl.ds(0, levels * rows)])]
    flat = flat_ref[...]
    table_in.wait()
    for i in range(2):
        part = pl.ds(512 * i, 512)
        spec_ref[part] = nt(table_ref[part], flat).astype(BF16)
        out.append(copies.start(spec_ref.at[part], spec_hbm.at[part]))
    for copy in out:
        copy.wait()


def order_kernel(_spec_in, _head, _tail, _spec_out):
    pass


def join_kernel(_whole_in, head_ref, tail_ref, whole_hbm, sems):
    copies = Copies(sems)
    size = whole_hbm.shape[0] // 10
    start, far = whole_hbm.shape[0] - 2 * size, head_ref.shape[0] - size
    out = [
        copies.start(source.at[pl.ds(far, size)], whole_hbm.at[pl.ds(start + size * i, size)])
        for i, source in enumerate((head_ref, tail_ref))
    ]
    for copy in out:
        copy.wait()


TILES = 5


def spread_rows(stage_ref, main, margin):
    rows, width = main.shape
    across = width // 128
    for c in range(across):
        stage_ref[c, :rows, :] = main[:, c * 128 : (c + 1) * 128]
        stage_ref[c, rows:, :] = margin[:, c * 128 : (c + 1) * 128]
    return [[stage_ref[c, pl.ds(t, 8, stride=TILES), :] for t in range(TILES)] for c in range(across)]


def join_rows(stage_ref, tiles, rows):
    for c, column in enumerate(tiles):
        for t, tile in enumerate(column):
            stage_ref[c, pl.ds(t, 8, stride=TILES), :] = tile * (0.2**STEPS)
    return jnp.concatenate([stage_ref[c, :rows, :] for c in range(len(tiles))], axis=1)


def coefficients(level, levels, wind_ref, head_ref, tail_ref, stage_ref, coef_ref):
    rows = wind_ref.shape[1]
    low = low_half((8, wind_ref.shape[2]))
    sublane = lax.broadcasted_iota(jnp.int32, (8, 128), 0)

    def extended(index, stage):
        at = pl.ds(pl.multiple_of(index * 8, 8), 8)
        margin = pltpu.roll(jnp.where(low, tail_ref[at, :], head_ref[at, :]), HALF, 0)
        return spread_rows(stage, wind_ref[index], margin)

    u = extended(level, stage_ref.at[0])
    v = extended(level + levels // 2, stage_ref.at[1])
    place = lax.axis_index("space")
    first = (sublane == 0) & (place == 0)
    last = (sublane == (rows - 1) // TILES) & (place == lax.axis_size("space") - 1)
    for c in range(len(u)):
        for t in range(TILES):
            north, south = 1.0 - v[c][t], 1.0 + v[c][t]
            if t == (rows - 1) % TILES:
                north = jnp.where(last, 0.0, north)
            if t == 0:
                south = jnp.where(first, 0.0, south)
            coef_ref[0, c, t] = 1.0 - u[c][t]
            coef_ref[1, c, t] = 1.0 + u[c][t]
            coef_ref[2, c, t] = north
            coef_ref[3, c, t] = south


def north_of(column, t):
    return column[t + 1] if t < TILES - 1 else pltpu.roll(column[0], 7, 0)


def south_of(column, t):
    return column[t - 1] if t > 0 else pltpu.roll(column[TILES - 1], 1, 0)


def forward_steps(x, coef_ref):
    lane = lax.broadcasted_iota(jnp.int32, (8, 128), 1)
    first, last = lane == 0, lane == 127
    ends = len(x) - 1
    for _ in range(STEPS):
        new = []
        for c in range(len(x)):
            column = []
            for t in range(TILES):
                here = x[c][t]
                east = pltpu.roll(jnp.where(first, x[c + 1][t] if c < ends else 0.0, here), 127, 1)
                west = pltpu.roll(jnp.where(last, x[c - 1][t] if c > 0 else 0.0, here), 1, 1)
                column.append(
                    (here + coef_ref[0, c, t] * east)
                    + coef_ref[1, c, t] * west
                    + (coef_ref[2, c, t] * north_of(x[c], t) + coef_ref[3, c, t] * south_of(x[c], t))
                )
            new.append(column)
        x = new
    return x


def backward_steps(y, coef_ref):
    lane = lax.broadcasted_iota(jnp.int32, (8, 128), 1)
    first, last = lane == 0, lane == 127
    ends = len(y) - 1
    for _ in range(STEPS):
        new = []
        for c in range(len(y)):
            column = []
            up = [coef_ref[3, c, t] * y[c][t] for t in range(TILES)]
            down = [coef_ref[2, c, t] * y[c][t] for t in range(TILES)]
            for t in range(TILES):
                here = y[c][t]
                after = coef_ref[1, c + 1, t] * y[c + 1][t] if c < ends else 0.0
                before = coef_ref[0, c - 1, t] * y[c - 1][t] if c > 0 else 0.0
                east = pltpu.roll(jnp.where(first, after, coef_ref[1, c, t] * here), 127, 1)
                west = pltpu.roll(jnp.where(last, before, coef_ref[0, c, t] * here), 1, 1)
                column.append((here + east) + west + (north_of(up, t) + south_of(down, t)))
            new.append(column)
        y = new
    return y


def one_hots(index, blocks):
    count = index.shape[1]
    high = lax.broadcasted_iota(jnp.int32, (blocks[0], count), 0) == (index >> 6)
    low = lax.broadcasted_iota(jnp.int32, (blocks[1], count), 0) == (index & 63)
    return high, low


def forward_kernel(
    incr_hbm, wind_hbm, head_in, tail_in, ends_hbm,
    incr_ref, wind_ref, head_ref, tail_ref, stage_ref, coef_ref, ends_ref, level_sems,
):
    levels, rows, width = incr_ref.shape
    half = levels // 2

    def fetch(kind, index):
        source, target = ((wind_hbm, wind_ref), (incr_hbm, incr_ref))[kind]
        return pltpu.make_async_copy(source.at[index], target.at[index], level_sems.at[kind, index])

    def put(index):
        part = pl.ds(pl.multiple_of(index * rows, rows), rows)
        return pltpu.make_async_copy(ends_ref.at[part], ends_hbm.at[part], level_sems.at[2, index])

    for level in range(half):
        for index in (level, level + half):
            for kind in range(2):
                fetch(kind, index).start()
    head_ref[...] = head_in[: levels * 8].astype(F32)
    tail_ref[...] = tail_in[: levels * 8].astype(F32)
    low = low_half((8, width))

    def at_level(level, carry):
        for index in (level, level + half):
            for kind in range(2):
                fetch(kind, index).wait()
        coefficients(level, levels, wind_ref, head_ref, tail_ref, stage_ref, coef_ref)

        def at_group(group):
            index = level + group * half
            at = pl.ds(pl.multiple_of(index * 8, 8), 8)
            margin = jnp.where(low, head_ref[at, :], tail_ref[at, :])
            x = forward_steps(spread_rows(stage_ref.at[2 + 2 * group], incr_ref[index], margin), coef_ref)
            ends = join_rows(stage_ref.at[3 + 2 * group], x, rows)
            ends_ref[pl.ds(pl.multiple_of(index * rows, rows), rows), :] = ends.astype(BF16)
            put(index).start()

        for group in range(2):
            at_group(group)
        return carry

    lax.fori_loop(0, half, at_level, 0)
    for index in range(levels):
        put(index).wait()


def observe_kernel(
    incr_hbm, index_ref, dual_ref, variance_ref, cols_hbm, lines_hbm, _after,
    tall_ref, obs_ref, incr_ref, cols_ref, lines_ref, sems,
):
    levels, rows, width = incr_ref.shape
    copies = Copies(sems)
    block_in = [copies.start(cols_hbm, cols_ref), copies.start(lines_hbm, lines_ref)]
    incr_in = copies.start(incr_hbm, incr_ref)
    for copy in block_in:
        copy.wait()
    cols, lines = cols_ref[...], lines_ref[...]
    blocks = (lines.shape[0], cols.shape[1])
    high, low_hot = one_hots(index_ref[...], blocks)
    weights = low_hot.astype(BF16)
    summed = sum(nt(p, weights) for p in parts(jnp.where(high, dual_ref[...], 0.0))) * 0.125
    tall_ref[...] = sum(tn(lines, p) for p in parts(summed))
    incr_in.wait()
    narrow = sum(nn(p, cols) for p in parts(incr_ref[...].reshape(levels * rows, width)))
    sums = sum(nn(lines, p) for p in parts(narrow))
    high = high.astype(BF16)
    picked = sum(tn(p, high) for p in parts(sums))
    observed = jnp.sum(jnp.where(low_hot, picked, 0.0), axis=0, keepdims=True) * 0.125
    obs_ref[...] = variance_ref[...] * dual_ref[...] + observed


def backward_kernel(
    coming_ref, wind_hbm, head_in, tail_in, mult_hbm, tall_ref, cols_hbm,
    state_hbm,
    wind_ref, mult_ref, cols_ref,
    head_ref, tail_ref, far_ref, margins_ref, stage_ref, coef_ref, spread_ref, state_ref, sems, level_sems,
):
    levels, rows, width = mult_ref.shape
    half = levels // 2
    copies = Copies(sems)
    full = levels * rows
    arriving = [
        copies.start(source, target)
        for source, target in ((cols_hbm, cols_ref), (wind_hbm, wind_ref), (mult_hbm, mult_ref))
    ]
    arriving[0].wait()
    spread_ref[...] = sum(nt(p, cols_ref[...]) for p in parts(tall_ref[...]))
    for copy in arriving[1:]:
        copy.wait()
    head_ref[...] = head_in[: levels * 8].astype(F32)
    tail_ref[...] = tail_in[: levels * 8].astype(F32)
    far_ref[...] = coming_ref[full:].astype(F32)
    low = low_half((8, width))

    def put(index):
        return pltpu.make_async_copy(state_ref.at[index], state_hbm.at[index], level_sems.at[index])

    def at_level(level, carry):
        coefficients(level, levels, wind_ref, head_ref, tail_ref, stage_ref, coef_ref)
        at = pl.ds(pl.multiple_of(level * 8, 8), 8)
        head, tail = far_ref[at, :], far_ref[pl.ds(pl.multiple_of(level * 8 + levels * 4, 8), 8), :]
        margins_ref[0] = jnp.where(low, head, tail)
        margins_ref[1] = pltpu.roll(jnp.where(low, tail, head), HALF, 0)

        def at_group(group):
            index = level + group * half
            part = pl.ds(pl.multiple_of(index * rows, rows), rows)
            main = coming_ref[part, :].astype(F32)
            y = backward_steps(spread_rows(stage_ref.at[2 + 2 * group], main, margins_ref[group]), coef_ref)
            back = join_rows(stage_ref.at[3 + 2 * group], y, rows)
            state_ref[index] = (mult_ref[index] - back) + spread_ref[part, :]
            put(index).start()

        for group in range(2):
            at_group(group)
        return carry

    lax.fori_loop(0, half, at_level, 0)
    for index in range(levels):
        put(index).wait()


def gather_lines(came_ref, lines_ref):
    count, rows, wide = came_ref.shape
    groups, fields = count // 4, wide // 128
    source = lax.broadcasted_iota(jnp.int32, (512, 512), 0)
    target = lax.broadcasted_iota(jnp.int32, (512, 512), 1)
    swapped = ((target & 127) >> 5) * 128 + (target >> 7) * 32 + (target & 31)
    perm = (source == swapped).astype(BF16)
    for g in range(fields):
        piece = came_ref[:, :, g * 128 : (g + 1) * 128].reshape(groups, 4, rows, 128)
        left = jnp.concatenate([piece[:, i].reshape(groups * rows, 128) for i in range(4)], axis=1)
        moved = nn(left, perm).astype(BF16)
        for i in range(4):
            for b in range(groups):
                lines_ref[(4 * g + i) * rows : (4 * g + i + 1) * rows, b * 128 : (b + 1) * 128] = moved[
                    b * rows : (b + 1) * rows, i * 128 : (i + 1) * 128
                ]


def latitude_kernel(
    came_ref, var_hbm, turned_hbm, out_hbm,
    var_ref, turned_ref, lines_ref, scaled_ref, out_ref, sems,
):
    copies = Copies(sems)
    turned_in = copies.start(turned_hbm, turned_ref)
    var_in = copies.start(var_hbm, var_ref)
    gather_lines(came_ref, lines_ref)
    turned_in.wait()
    latitude = nn(lines_ref[...], turned_ref[...])
    var_in.wait()
    scaled_ref[...] = (latitude * var_ref[...]).astype(BF16)
    scaled = scaled_ref[...]
    out = []
    for i in range(2):
        part = pl.ds(512 * i, 512)
        out_ref[part] = nt(turned_ref[part], scaled).astype(BF16)
        out.append(copies.start(out_ref.at[part], out_hbm.at[part]))
    for copy in out:
        copy.wait()


def finish_kernel(
    came_ref, incr_hbm, prev_ref, table_hbm, out_hbm,
    incr_ref, table_ref, lines_ref, out_ref, sems,
):
    copies = Copies(sems)
    table_in = copies.start(table_hbm, table_ref)
    incr_in = copies.start(incr_hbm, incr_ref)
    gather_lines(came_ref, lines_ref)
    table_in.wait()
    table = table_ref[...]
    out = []
    for i in range(3):
        part = pl.ds(128 * i, 128)
        covar = nn(lines_ref[part], table)
        if i == 0:
            incr_in.wait()
        out_ref[part] = covar + (incr_ref[part] - prev_ref[part].astype(F32))
        out.append(copies.start(out_ref.at[part], out_hbm.at[part]))
    for copy in out:
        copy.wait()


VMEM = pl.BlockSpec(memory_space=pltpu.VMEM)
HBM = pl.BlockSpec(memory_space=pl.ANY)


def call(kernel, outs, ins, scratch, name, aliases=None, near=()):
    def place(index, a):
        small = a.shape[0] == 1 or (len(a.shape) == 2 and a.shape[1] < 128 and a.dtype == F32)
        return VMEM if small or index in near else HBM

    single = not isinstance(outs, tuple)
    out_specs = [place(len(ins) + i, a) for i, a in enumerate((outs,) if single else outs)]
    return pl.pallas_call(
        kernel,
        out_shape=outs,
        in_specs=[place(i, a) for i, a in enumerate(ins)],
        out_specs=out_specs[0] if single else tuple(out_specs),
        scratch_shapes=list(scratch),
        compiler_params=pltpu.CompilerParams(vmem_limit_bytes=52 * 1024 * 1024),
        input_output_aliases=aliases or {},
        name=name,
    )(*ins)


def local(increment, multiplier, obs_dual, obs_index, obs_variance, winds, spectral_var):
    rows, levels, width = increment.shape[1:]
    count = lax.axis_size("space")
    times = lax.axis_size("tm")
    lat = rows * count
    waves = width // count
    full = levels * rows
    incr = jnp.transpose(increment[0], (1, 0, 2))
    mult = jnp.transpose(multiplier[0], (1, 0, 2))
    wind = jnp.transpose(winds[0], (1, 0, 2))
    var = jnp.transpose(spectral_var, (1, 2, 0)).reshape(full, lat)
    table = cosine_table(width)
    turned = np.ascontiguousarray(table.T)
    cols, lines = block_sums(levels, rows, width)

    def shape(*dims):
        return jax.ShapeDtypeStruct(dims, BF16)

    def wide(*dims):
        return pltpu.VMEM(dims, F32)

    def short(*dims):
        return pltpu.VMEM(dims, BF16)

    def sems(*dims):
        return pltpu.SemaphoreType.DMA(dims)

    field = (levels, rows, width)
    head, tail = call(
        edge_kernel,
        (shape(levels * 12, width), shape(levels * 12, width)),
        (mult, incr, wind),
        [wide(6, levels, 8, width), sems(6)],
        "edges",
        near=(3, 4),
    )
    whole, spec = call(
        start_kernel,
        (shape(full + levels * 8, width), shape(width, full)),
        (mult, table, head),
        [wide(*field), short(width, width), short(full, width), short(width, full), sems(8)],
        "start",
    )
    ring = range(count - 1)
    head = lax.ppermute(head, "space", [(i + 1, i) for i in ring])
    tail = lax.ppermute(tail, "space", [(i, i + 1) for i in ring])
    spec = call(order_kernel, shape(width, full), (spec, head, tail), [], "order", {0: 0}, near=(1, 2))
    came = lax.all_to_all(spec.reshape(count, waves, full), "space", 0, 0, tiled=True)
    whole = call(
        join_kernel,
        shape(full + levels * 8, width),
        (whole, head, tail),
        [sems(2)],
        "join",
        {0: 0},
        near=(1, 2),
    )
    coming = lax.ppermute(whole, "tm", [(t + 1, t) for t in range(times - 1)])

    across = width // 128
    stages = [wide(6, across, rows + 8, 128), wide(4, across, TILES, 8, 128)]
    ends = call(
        forward_kernel,
        shape(full, width),
        (incr, wind, head, tail),
        [
            wide(*field), wide(*field), wide(levels * 8, width), wide(levels * 8, width), *stages,
            short(full, width), sems(3, levels),
        ],
        "forward",
        near=(2, 3),
    )
    previous = lax.ppermute(ends, "tm", [(t, t + 1) for t in range(times - 1)])

    back = call(
        latitude_kernel,
        shape(lat, full),
        (came, var, turned),
        [
            wide(full, lat), short(lat, lat), short(full, lat), short(full, lat),
            short(lat, full), sems(16),
        ],
        "latitude",
        near=(0,),
    )
    returned = lax.all_to_all(back.reshape(count, rows, full), "space", 0, 0, tiled=True)

    tall, obs_rows = call(
        observe_kernel,
        (jax.ShapeDtypeStruct((full, cols.shape[1]), F32), jax.ShapeDtypeStruct(obs_dual.shape, F32)),
        (incr, obs_index, obs_dual, obs_variance, cols, lines, back),
        [wide(*field), short(*cols.shape), short(*lines.shape), sems(3)],
        "observe",
    )
    state_rows = call(
        backward_kernel,
        jax.ShapeDtypeStruct(field, F32),
        (coming, wind, head, tail, mult, tall, cols),
        [
            wide(*field), wide(*field), short(*cols.shape),
            wide(levels * 8, width), wide(levels * 8, width), wide(levels * 8, width), wide(2, 8, width),
            *stages, wide(full, width), wide(*field), sems(3), sems(levels),
        ],
        "backward",
        near=(0, 2, 3),
    )
    model_rows = call(
        finish_kernel,
        jax.ShapeDtypeStruct((full, width), F32),
        (returned, incr.reshape(full, width), previous, table),
        [
            wide(full, width), short(width, width),
            short(full, width), wide(full, width), sems(20),
        ],
        "finish",
        near=(0, 2),
    )

    def placed(whole):
        return jnp.transpose(whole.reshape(field), (1, 0, 2))[None]

    return (placed(model_rows), obs_rows, placed(state_rows))


def solution(mesh):
    specs = (
        P("tm", "space", None, None),
        P("tm", "space", None, None),
        P("tm", "space"),
        P("tm", "space"),
        P("tm", "space"),
        P("tm", "space", None, None),
        P(None, None, "space"),
    )
    return jax.shard_map(
        local,
        mesh=mesh,
        in_specs=specs,
        out_specs=(P("tm", "space", None, None), P("tm", "space"), P("tm", "space", None, None)),
        check_vma=False,
    )
```

```python
import math

import jax
import jax.numpy as jnp
import numpy as np
from jax import lax
from jax.experimental import pallas as pl
from jax.experimental.pallas import tpu as pltpu
from jax.sharding import PartitionSpec as P
import ml_dtypes

STEPS = 4
HALF = 4
F32 = jnp.float32
BF16 = jnp.bfloat16


def cosine_table(count):
    wave = np.arange(count)[:, None]
    point = np.arange(count)[None, :]
    phase = (2 * point + 1) * wave % (4 * count)
    table = np.cos(phase * (math.pi / (2.0 * count))) * math.sqrt(2.0 / count)
    table = np.where(wave == 0, table * math.sqrt(0.5), table)
    return table.astype(np.float32).astype(ml_dtypes.bfloat16)


def block_sums(levels, rows, width):
    cols = (np.arange(width)[:, None] // 16 == np.arange(width // 16)[None, :]).astype(np.float32)
    out = np.arange(rows // 4 * levels)[:, None]
    inn = np.arange(levels * rows)[None, :]
    lines = ((out % levels == inn // rows) & (out // levels == inn % rows // 4)).astype(np.float32)
    return cols.astype(ml_dtypes.bfloat16), lines.astype(ml_dtypes.bfloat16)


def nt(a, b):
    return lax.dot_general(a, b, (((1,), (1,)), ((), ())), preferred_element_type=F32)


def tn(a, b):
    return lax.dot_general(a, b, (((0,), (0,)), ((), ())), preferred_element_type=F32)


def nn(a, b):
    return jnp.dot(a, b, preferred_element_type=F32)


def parts(a):
    first = a.astype(BF16)
    return first, (a - first.astype(F32)).astype(BF16)


def low_half(shape):
    return lax.broadcasted_iota(jnp.int32, shape, len(shape) - 2) < HALF


class Copies:
    def __init__(self, sems):
        self.sems = sems
        self.count = 0

    def start(self, source, target):
        copy = pltpu.make_async_copy(source, target, self.sems.at[self.count])
        self.count += 1
        copy.start()
        return copy


def edge_kernel(mult_hbm, incr_hbm, wind_hbm, head_ref, tail_ref, edge_ref, sems):
    levels, rows, width = mult_hbm.shape
    half = levels // 2
    copies = Copies(sems)
    coming = [
        copies.start(source.at[:, pl.ds(at, 8), :], edge_ref.at[3 * end + i])
        for end, at in enumerate((0, rows - 8))
        for i, source in enumerate((incr_hbm, wind_hbm, mult_hbm))
    ]
    for end, part_ref in enumerate((head_ref, tail_ref)):
        for copy in coming[3 * end : 3 * end + 3]:
            copy.wait()
        incr, wind, mult = edge_ref[3 * end], edge_ref[3 * end + 1], edge_ref[3 * end + 2]
        wind = pltpu.roll(wind, HALF, 1)
        second = pltpu.roll(mult[half:], HALF, 1)
        low, less = low_half((levels, 8, width)), low_half((half, 8, width))
        if end == 0:
            field, dual = jnp.where(low, incr, wind), jnp.where(less, mult[:half], second)
        else:
            field, dual = jnp.where(low, wind, incr), jnp.where(less, second, mult[:half])
        part_ref[: levels * 8] = field.reshape(levels * 8, width).astype(BF16)
        part_ref[levels * 8 :] = dual.reshape(half * 8, width).astype(BF16)


def start_kernel(mult_ref, table_ref, _after, whole_hbm, spec_hbm, flat_ref, spec_ref, sems):
    levels, rows, width = mult_ref.shape
    copies = Copies(sems)
    half = table_ref.shape[0] // 2
    flat = mult_ref[...].reshape(levels * rows, width).astype(BF16)
    flat_ref[...] = flat
    out = [copies.start(flat_ref, whole_hbm.at[pl.ds(0, levels * rows)])]
    for i in range(2):
        part = pl.ds(half * i, half)
        spec_ref[part] = nt(table_ref[part], flat).astype(BF16)
        out.append(copies.start(spec_ref.at[part], spec_hbm.at[part]))
    for copy in out:
        copy.wait()


def order_kernel(_spec_in, _head, _tail, _spec_out):
    pass


def join_kernel(_whole_in, head_ref, tail_ref, whole_hbm, sems):
    copies = Copies(sems)
    size = whole_hbm.shape[0] // 10
    start, far = whole_hbm.shape[0] - 2 * size, head_ref.shape[0] - size
    out = [
        copies.start(source.at[pl.ds(far, size)], whole_hbm.at[pl.ds(start + size * i, size)])
        for i, source in enumerate((head_ref, tail_ref))
    ]
    for copy in out:
        copy.wait()


TILES = 5


def spread_rows(stage_ref, main, margin):
    rows, width = main.shape
    across = width // 128
    for c in range(across):
        stage_ref[c, :rows, :] = main[:, c * 128 : (c + 1) * 128]
        stage_ref[c, rows:, :] = margin[:, c * 128 : (c + 1) * 128]
    return [[stage_ref[c, pl.ds(t, 8, stride=TILES), :] for t in range(TILES)] for c in range(across)]


def join_rows(stage_ref, tiles, rows):
    for c, column in enumerate(tiles):
        for t, tile in enumerate(column):
            stage_ref[c, pl.ds(t, 8, stride=TILES), :] = tile * (0.2**STEPS)
    return jnp.concatenate([stage_ref[c, :rows, :] for c in range(len(tiles))], axis=1)


def coefficients(level, levels, wind_ref, head_ref, tail_ref, stage_ref, coef_ref):
    rows = wind_ref.shape[1]
    low = low_half((8, wind_ref.shape[2]))
    sublane = lax.broadcasted_iota(jnp.int32, (8, 128), 0)

    def extended(index, stage):
        at = pl.ds(pl.multiple_of(index * 8, 8), 8)
        margin = pltpu.roll(jnp.where(low, tail_ref[at, :], head_ref[at, :]), HALF, 0)
        return spread_rows(stage, wind_ref[index], margin)

    u = extended(level, stage_ref.at[0])
    v = extended(level + levels // 2, stage_ref.at[1])
    place = lax.axis_index("space")
    first = (sublane == 0) & (place == 0)
    last = (sublane == (rows - 1) // TILES) & (place == lax.axis_size("space") - 1)
    for c in range(len(u)):
        for t in range(TILES):
            north, south = 1.0 - v[c][t], 1.0 + v[c][t]
            if t == (rows - 1) % TILES:
                north = jnp.where(last, 0.0, north)
            if t == 0:
                south = jnp.where(first, 0.0, south)
            coef_ref[0, c, t] = 1.0 - u[c][t]
            coef_ref[1, c, t] = 1.0 + u[c][t]
            coef_ref[2, c, t] = north
            coef_ref[3, c, t] = south


def north_of(column, t):
    return column[t + 1] if t < TILES - 1 else pltpu.roll(column[0], 7, 0)


def south_of(column, t):
    return column[t - 1] if t > 0 else pltpu.roll(column[TILES - 1], 1, 0)


def forward_steps(x, coef_ref):
    lane = lax.broadcasted_iota(jnp.int32, (8, 128), 1)
    first, last = lane == 0, lane == 127
    ends = len(x) - 1
    for _ in range(STEPS):
        new = []
        for c in range(len(x)):
            column = []
            for t in range(TILES):
                here = x[c][t]
                east = pltpu.roll(jnp.where(first, x[c + 1][t] if c < ends else 0.0, here), 127, 1)
                west = pltpu.roll(jnp.where(last, x[c - 1][t] if c > 0 else 0.0, here), 1, 1)
                column.append(
                    (here + coef_ref[0, c, t] * east)
                    + coef_ref[1, c, t] * west
                    + (coef_ref[2, c, t] * north_of(x[c], t) + coef_ref[3, c, t] * south_of(x[c], t))
                )
            new.append(column)
        x = new
    return x


def backward_steps(y, coef_ref):
    lane = lax.broadcasted_iota(jnp.int32, (8, 128), 1)
    first, last = lane == 0, lane == 127
    ends = len(y) - 1
    for _ in range(STEPS):
        new = []
        for c in range(len(y)):
            column = []
            up = [coef_ref[3, c, t] * y[c][t] for t in range(TILES)]
            down = [coef_ref[2, c, t] * y[c][t] for t in range(TILES)]
            for t in range(TILES):
                here = y[c][t]
                after = coef_ref[1, c + 1, t] * y[c + 1][t] if c < ends else 0.0
                before = coef_ref[0, c - 1, t] * y[c - 1][t] if c > 0 else 0.0
                east = pltpu.roll(jnp.where(first, after, coef_ref[1, c, t] * here), 127, 1)
                west = pltpu.roll(jnp.where(last, before, coef_ref[0, c, t] * here), 1, 1)
                column.append((here + east) + west + (north_of(up, t) + south_of(down, t)))
            new.append(column)
        y = new
    return y


def one_hots(index, blocks):
    count = index.shape[1]
    high = lax.broadcasted_iota(jnp.int32, (blocks[0], count), 0) == (index >> 6)
    low = lax.broadcasted_iota(jnp.int32, (blocks[1], count), 0) == (index & 63)
    return high, low


def forward_kernel(
    incr_hbm, wind_hbm, head_in, tail_in, ends_hbm,
    incr_ref, wind_ref, head_ref, tail_ref, stage_ref, coef_ref, ends_ref, level_sems,
):
    levels, rows, width = incr_ref.shape
    half = levels // 2

    def fetch(kind, index):
        source, target = ((wind_hbm, wind_ref), (incr_hbm, incr_ref))[kind]
        return pltpu.make_async_copy(source.at[index], target.at[index], level_sems.at[kind, index])

    def put(index):
        part = pl.ds(pl.multiple_of(index * rows, rows), rows)
        return pltpu.make_async_copy(ends_ref.at[part], ends_hbm.at[part], level_sems.at[2, index])

    for level in range(half):
        for index in (level, level + half):
            for kind in range(2):
                fetch(kind, index).start()
    head_ref[...] = head_in[: levels * 8].astype(F32)
    tail_ref[...] = tail_in[: levels * 8].astype(F32)
    low = low_half((8, width))

    def at_level(level, carry):
        for index in (level, level + half):
            for kind in range(2):
                fetch(kind, index).wait()
        coefficients(level, levels, wind_ref, head_ref, tail_ref, stage_ref, coef_ref)

        def at_group(group):
            index = level + group * half
            at = pl.ds(pl.multiple_of(index * 8, 8), 8)
            margin = jnp.where(low, head_ref[at, :], tail_ref[at, :])
            x = forward_steps(spread_rows(stage_ref.at[2 + 2 * group], incr_ref[index], margin), coef_ref)
            ends = join_rows(stage_ref.at[3 + 2 * group], x, rows)
            ends_ref[pl.ds(pl.multiple_of(index * rows, rows), rows), :] = ends.astype(BF16)
            put(index).start()

        for group in range(2):
            at_group(group)
        return carry

    lax.fori_loop(0, half, at_level, 0)
    for index in range(levels):
        put(index).wait()


def observe_kernel(
    incr_hbm, index_ref, dual_ref, variance_ref, cols_hbm, lines_hbm, _after,
    tall_ref, obs_ref, incr_ref, cols_ref, lines_ref, sems,
):
    levels, rows, width = incr_ref.shape
    copies = Copies(sems)
    block_in = [copies.start(cols_hbm, cols_ref), copies.start(lines_hbm, lines_ref)]
    incr_in = copies.start(incr_hbm, incr_ref)
    for copy in block_in:
        copy.wait()
    cols, lines = cols_ref[...], lines_ref[...]
    blocks = (lines.shape[0], cols.shape[1])
    high, low_hot = one_hots(index_ref[...], blocks)
    weights = low_hot.astype(BF16)
    summed = sum(nt(p, weights) for p in parts(jnp.where(high, dual_ref[...], 0.0))) * 0.125
    tall_ref[...] = sum(tn(lines, p) for p in parts(summed))
    incr_in.wait()
    narrow = sum(nn(p, cols) for p in parts(incr_ref[...].reshape(levels * rows, width)))
    sums = sum(nn(lines, p) for p in parts(narrow))
    high = high.astype(BF16)
    picked = sum(tn(p, high) for p in parts(sums))
    observed = jnp.sum(jnp.where(low_hot, picked, 0.0), axis=0, keepdims=True) * 0.125
    obs_ref[...] = variance_ref[...] * dual_ref[...] + observed


def backward_kernel(
    coming_ref, wind_hbm, head_in, tail_in, mult_hbm, tall_ref, cols_hbm,
    state_hbm,
    wind_ref, mult_ref, cols_ref,
    head_ref, tail_ref, far_ref, margins_ref, stage_ref, coef_ref, spread_ref, state_ref, sems, level_sems,
):
    levels, rows, width = mult_ref.shape
    half = levels // 2
    copies = Copies(sems)
    full = levels * rows
    arriving = [
        copies.start(source, target)
        for source, target in ((cols_hbm, cols_ref), (wind_hbm, wind_ref), (mult_hbm, mult_ref))
    ]
    arriving[0].wait()
    spread_ref[...] = sum(nt(p, cols_ref[...]) for p in parts(tall_ref[...]))
    for copy in arriving[1:]:
        copy.wait()
    head_ref[...] = head_in[: levels * 8].astype(F32)
    tail_ref[...] = tail_in[: levels * 8].astype(F32)
    far_ref[...] = coming_ref[full:].astype(F32)
    low = low_half((8, width))

    def put(index):
        return pltpu.make_async_copy(state_ref.at[index], state_hbm.at[index], level_sems.at[index])

    def at_level(level, carry):
        coefficients(level, levels, wind_ref, head_ref, tail_ref, stage_ref, coef_ref)
        at = pl.ds(pl.multiple_of(level * 8, 8), 8)
        head, tail = far_ref[at, :], far_ref[pl.ds(pl.multiple_of(level * 8 + levels * 4, 8), 8), :]
        margins_ref[0] = jnp.where(low, head, tail)
        margins_ref[1] = pltpu.roll(jnp.where(low, tail, head), HALF, 0)

        def at_group(group):
            index = level + group * half
            part = pl.ds(pl.multiple_of(index * rows, rows), rows)
            main = coming_ref[part, :].astype(F32)
            y = backward_steps(spread_rows(stage_ref.at[2 + 2 * group], main, margins_ref[group]), coef_ref)
            back = join_rows(stage_ref.at[3 + 2 * group], y, rows)
            state_ref[index] = (mult_ref[index] - back) + spread_ref[part, :]
            put(index).start()

        for group in range(2):
            at_group(group)
        return carry

    lax.fori_loop(0, half, at_level, 0)
    for index in range(levels):
        put(index).wait()


def gather_lines(came_ref, lines_ref):
    count, rows, wide = came_ref.shape
    groups, fields = count // 4, wide // 128
    source = lax.broadcasted_iota(jnp.int32, (512, 512), 0)
    target = lax.broadcasted_iota(jnp.int32, (512, 512), 1)
    swapped = ((target & 127) >> 5) * 128 + (target >> 7) * 32 + (target & 31)
    perm = (source == swapped).astype(BF16)
    for g in range(fields):
        piece = came_ref[:, :, g * 128 : (g + 1) * 128].reshape(groups, 4, rows, 128)
        left = jnp.concatenate([piece[:, i].reshape(groups * rows, 128) for i in range(4)], axis=1)
        moved = nn(left, perm).astype(BF16)
        for i in range(4):
            for b in range(groups):
                lines_ref[(4 * g + i) * rows : (4 * g + i + 1) * rows, b * 128 : (b + 1) * 128] = moved[
                    b * rows : (b + 1) * rows, i * 128 : (i + 1) * 128
                ]


def latitude_kernel(
    came_ref, var_hbm, turned_hbm, out_hbm,
    var_ref, turned_ref, lines_ref, scaled_ref, out_ref, sems,
):
    copies = Copies(sems)
    turned_in = copies.start(turned_hbm, turned_ref)
    var_in = copies.start(var_hbm, var_ref)
    gather_lines(came_ref, lines_ref)
    turned_in.wait()
    latitude = nn(lines_ref[...], turned_ref[...])
    var_in.wait()
    scaled_ref[...] = (latitude * var_ref[...]).astype(BF16)
    scaled = scaled_ref[...]
    out = []
    for i in range(2):
        part = pl.ds(512 * i, 512)
        out_ref[part] = nt(turned_ref[part], scaled).astype(BF16)
        out.append(copies.start(out_ref.at[part], out_hbm.at[part]))
    for copy in out:
        copy.wait()


def finish_kernel(
    came_ref, incr_hbm, prev_ref, table_hbm, out_hbm,
    incr_ref, table_ref, lines_ref, out_ref, sems,
):
    copies = Copies(sems)
    table_in = copies.start(table_hbm, table_ref)
    incr_in = copies.start(incr_hbm, incr_ref)
    gather_lines(came_ref, lines_ref)
    table_in.wait()
    table = table_ref[...]
    out = []
    for i in range(3):
        part = pl.ds(128 * i, 128)
        covar = nn(lines_ref[part], table)
        if i == 0:
            incr_in.wait()
        out_ref[part] = covar + (incr_ref[part] - prev_ref[part].astype(F32))
        out.append(copies.start(out_ref.at[part], out_hbm.at[part]))
    for copy in out:
        copy.wait()


VMEM = pl.BlockSpec(memory_space=pltpu.VMEM)
HBM = pl.BlockSpec(memory_space=pl.ANY)


def call(kernel, outs, ins, scratch, name, aliases=None, near=(), grant=52):
    def place(index, a):
        small = a.shape[0] == 1 or (len(a.shape) == 2 and a.shape[1] < 128 and a.dtype == F32)
        return VMEM if small or index in near else HBM

    single = not isinstance(outs, tuple)
    out_specs = [place(len(ins) + i, a) for i, a in enumerate((outs,) if single else outs)]
    return pl.pallas_call(
        kernel,
        out_shape=outs,
        in_specs=[place(i, a) for i, a in enumerate(ins)],
        out_specs=out_specs[0] if single else tuple(out_specs),
        scratch_shapes=list(scratch),
        compiler_params=pltpu.CompilerParams(vmem_limit_bytes=grant * 1024 * 1024),
        input_output_aliases=aliases or {},
        name=name,
    )(*ins)


def local(increment, multiplier, obs_dual, obs_index, obs_variance, winds, spectral_var):
    rows, levels, width = increment.shape[1:]
    count = lax.axis_size("space")
    times = lax.axis_size("tm")
    lat = rows * count
    waves = width // count
    full = levels * rows
    incr = jnp.transpose(increment[0], (1, 0, 2))
    mult = jnp.transpose(multiplier[0], (1, 0, 2))
    wind = jnp.transpose(winds[0], (1, 0, 2))
    var = jnp.transpose(spectral_var, (1, 2, 0)).reshape(full, lat)
    table = cosine_table(width)
    turned = np.ascontiguousarray(table.T)
    cols, lines = block_sums(levels, rows, width)

    def shape(*dims):
        return jax.ShapeDtypeStruct(dims, BF16)

    def wide(*dims):
        return pltpu.VMEM(dims, F32)

    def short(*dims):
        return pltpu.VMEM(dims, BF16)

    def sems(*dims):
        return pltpu.SemaphoreType.DMA(dims)

    field = (levels, rows, width)
    head, tail = call(
        edge_kernel,
        (shape(levels * 12, width), shape(levels * 12, width)),
        (mult, incr, wind),
        [wide(6, levels, 8, width), sems(6)],
        "edges",
        near=(3, 4),
        grant=52,
    )
    whole, spec = call(
        start_kernel,
        (shape(full + levels * 8, width), shape(width, full)),
        (mult, table, head),
        [short(full, width), short(width, full), sems(3)],
        "start",
        near=(0,1,2),
        grant=40,
    )
    ring = range(count - 1)
    head = lax.ppermute(head, "space", [(i + 1, i) for i in ring])
    tail = lax.ppermute(tail, "space", [(i, i + 1) for i in ring])
    spec = call(order_kernel, shape(width, full), (spec, head, tail), [], "order", {0: 0}, near=(1, 2))
    came = lax.all_to_all(spec.reshape(count, waves, full), "space", 0, 0, tiled=True)
    whole = call(
        join_kernel,
        shape(full + levels * 8, width),
        (whole, head, tail),
        [sems(2)],
        "join",
        {0: 0},
        near=(1, 2),
    )
    coming = lax.ppermute(whole, "tm", [(t + 1, t) for t in range(times - 1)])

    across = width // 128
    stages = [wide(6, across, rows + 8, 128), wide(4, across, TILES, 8, 128)]
    ends = call(
        forward_kernel,
        shape(full, width),
        (incr, wind, head, tail),
        [
            wide(*field), wide(*field), wide(levels * 8, width), wide(levels * 8, width), *stages,
            short(full, width), sems(3, levels),
        ],
        "forward",
        near=(2, 3),
    )
    previous = lax.ppermute(ends, "tm", [(t, t + 1) for t in range(times - 1)])

    back = call(
        latitude_kernel,
        shape(lat, full),
        (came, var, turned),
        [
            wide(full, lat), short(lat, lat), short(full, lat), short(full, lat),
            short(lat, full), sems(16),
        ],
        "latitude",
        near=(0,),
    )
    returned = lax.all_to_all(back.reshape(count, rows, full), "space", 0, 0, tiled=True)

    tall, obs_rows = call(
        observe_kernel,
        (jax.ShapeDtypeStruct((full, cols.shape[1]), F32), jax.ShapeDtypeStruct(obs_dual.shape, F32)),
        (incr, obs_index, obs_dual, obs_variance, cols, lines, back),
        [wide(*field), short(*cols.shape), short(*lines.shape), sems(3)],
        "observe",
    )
    state_rows = call(
        backward_kernel,
        jax.ShapeDtypeStruct(field, F32),
        (coming, wind, head, tail, mult, tall, cols),
        [
            wide(*field), wide(*field), short(*cols.shape),
            wide(levels * 8, width), wide(levels * 8, width), wide(levels * 8, width), wide(2, 8, width),
            *stages, wide(full, width), wide(*field), sems(3), sems(levels),
        ],
        "backward",
        near=(0, 2, 3),
    )
    model_rows = call(
        finish_kernel,
        jax.ShapeDtypeStruct((full, width), F32),
        (returned, incr.reshape(full, width), previous, table),
        [
            wide(full, width), short(width, width),
            short(full, width), wide(full, width), sems(20),
        ],
        "finish",
        near=(0, 2),
    )

    def placed(whole):
        return jnp.transpose(whole.reshape(field), (1, 0, 2))[None]

    return (placed(model_rows), obs_rows, placed(state_rows))


def solution(mesh):
    specs = (
        P("tm", "space", None, None),
        P("tm", "space", None, None),
        P("tm", "space"),
        P("tm", "space"),
        P("tm", "space"),
        P("tm", "space", None, None),
        P(None, None, "space"),
    )
    return jax.shard_map(
        local,
        mesh=mesh,
        in_specs=specs,
        out_specs=(P("tm", "space", None, None), P("tm", "space"), P("tm", "space", None, None)),
        check_vma=False,
    )
```

```python
import math

import jax
import jax.numpy as jnp
import numpy as np
from jax import lax
from jax.experimental import pallas as pl
from jax.experimental.pallas import tpu as pltpu
from jax.sharding import PartitionSpec as P
import ml_dtypes

STEPS = 4
HALF = 4
F32 = jnp.float32
BF16 = jnp.bfloat16


def cosine_table(count):
    wave = np.arange(count)[:, None]
    point = np.arange(count)[None, :]
    phase = (2 * point + 1) * wave % (4 * count)
    table = np.cos(phase * (math.pi / (2.0 * count))) * math.sqrt(2.0 / count)
    table = np.where(wave == 0, table * math.sqrt(0.5), table)
    return table.astype(np.float32).astype(ml_dtypes.bfloat16)


def block_sums(levels, rows, width):
    cols = (np.arange(width)[:, None] // 16 == np.arange(width // 16)[None, :]).astype(np.float32)
    out = np.arange(rows // 4 * levels)[:, None]
    inn = np.arange(levels * rows)[None, :]
    lines = ((out % levels == inn // rows) & (out // levels == inn % rows // 4)).astype(np.float32)
    return cols.astype(ml_dtypes.bfloat16), lines.astype(ml_dtypes.bfloat16)


def nt(a, b):
    return lax.dot_general(a, b, (((1,), (1,)), ((), ())), preferred_element_type=F32)


def tn(a, b):
    return lax.dot_general(a, b, (((0,), (0,)), ((), ())), preferred_element_type=F32)


def nn(a, b):
    return jnp.dot(a, b, preferred_element_type=F32)


def parts(a):
    first = a.astype(BF16)
    return first, (a - first.astype(F32)).astype(BF16)


def low_half(shape):
    return lax.broadcasted_iota(jnp.int32, shape, len(shape) - 2) < HALF


class Copies:
    def __init__(self, sems):
        self.sems = sems
        self.count = 0

    def start(self, source, target):
        copy = pltpu.make_async_copy(source, target, self.sems.at[self.count])
        self.count += 1
        copy.start()
        return copy


def edge_kernel(mult_hbm, incr_hbm, wind_hbm, head_ref, tail_ref, edge_ref, sems):
    levels, rows, width = mult_hbm.shape
    half = levels // 2
    copies = Copies(sems)
    coming = [
        copies.start(source.at[:, pl.ds(at, 8), :], edge_ref.at[3 * end + i])
        for end, at in enumerate((0, rows - 8))
        for i, source in enumerate((incr_hbm, wind_hbm, mult_hbm))
    ]
    for end, part_ref in enumerate((head_ref, tail_ref)):
        for copy in coming[3 * end : 3 * end + 3]:
            copy.wait()
        incr, wind, mult = edge_ref[3 * end], edge_ref[3 * end + 1], edge_ref[3 * end + 2]
        wind = pltpu.roll(wind, HALF, 1)
        second = pltpu.roll(mult[half:], HALF, 1)
        low, less = low_half((levels, 8, width)), low_half((half, 8, width))
        if end == 0:
            field, dual = jnp.where(low, incr, wind), jnp.where(less, mult[:half], second)
        else:
            field, dual = jnp.where(low, wind, incr), jnp.where(less, second, mult[:half])
        part_ref[: levels * 8] = field.reshape(levels * 8, width).astype(BF16)
        part_ref[levels * 8 :] = dual.reshape(half * 8, width).astype(BF16)


def start_kernel(mult_ref, table_ref, _after, whole_hbm, spec_hbm, flat_ref, spec_ref, sems):
    levels, rows, width = mult_ref.shape
    copies = Copies(sems)
    half = table_ref.shape[0] // 2
    flat = mult_ref[...].reshape(levels * rows, width).astype(BF16)
    flat_ref[...] = flat
    out = [copies.start(flat_ref, whole_hbm.at[pl.ds(0, levels * rows)])]
    for i in range(2):
        part = pl.ds(half * i, half)
        spec_ref[part] = nt(table_ref[part], flat).astype(BF16)
        out.append(copies.start(spec_ref.at[part], spec_hbm.at[part]))
    for copy in out:
        copy.wait()


def order_kernel(_spec_in, _head, _tail, _spec_out):
    pass


def join_kernel(_whole_in, head_ref, tail_ref, whole_hbm, sems):
    copies = Copies(sems)
    size = whole_hbm.shape[0] // 10
    start, far = whole_hbm.shape[0] - 2 * size, head_ref.shape[0] - size
    out = [
        copies.start(source.at[pl.ds(far, size)], whole_hbm.at[pl.ds(start + size * i, size)])
        for i, source in enumerate((head_ref, tail_ref))
    ]
    for copy in out:
        copy.wait()


TILES = 5


def spread_rows(stage_ref, main, margin):
    rows, width = main.shape
    across = width // 128
    for c in range(across):
        stage_ref[c, :rows, :] = main[:, c * 128 : (c + 1) * 128]
        stage_ref[c, rows:, :] = margin[:, c * 128 : (c + 1) * 128]
    return [[stage_ref[c, pl.ds(t, 8, stride=TILES), :] for t in range(TILES)] for c in range(across)]


def join_rows(stage_ref, tiles, rows):
    for c, column in enumerate(tiles):
        for t, tile in enumerate(column):
            stage_ref[c, pl.ds(t, 8, stride=TILES), :] = tile * (0.2**STEPS)
    return jnp.concatenate([stage_ref[c, :rows, :] for c in range(len(tiles))], axis=1)


def coefficients(level, levels, wind_ref, head_ref, tail_ref, stage_ref, coef_ref):
    rows = wind_ref.shape[1]
    low = low_half((8, wind_ref.shape[2]))
    sublane = lax.broadcasted_iota(jnp.int32, (8, 128), 0)

    def extended(index, stage):
        at = pl.ds(pl.multiple_of(index * 8, 8), 8)
        margin = pltpu.roll(jnp.where(low, tail_ref[at, :], head_ref[at, :]), HALF, 0)
        return spread_rows(stage, wind_ref[index], margin)

    u = extended(level, stage_ref.at[0])
    v = extended(level + levels // 2, stage_ref.at[1])
    place = lax.axis_index("space")
    start, end = place == 0, place == lax.axis_size("space") - 1

    def cut(value, row, t, edge):
        return jnp.where((sublane == row // TILES) & edge, 0.0, value) if t == row % TILES else value

    for c in range(len(u)):
        for t in range(TILES):
            north, south = 1.0 - v[c][t], 1.0 + v[c][t]
            north = cut(cut(north, rows - 1, t, end), rows + 7, t, start)
            south = cut(cut(south, 0, t, start), rows, t, end)
            coef_ref[0, c, t] = 1.0 - u[c][t]
            coef_ref[1, c, t] = 1.0 + u[c][t]
            coef_ref[2, c, t] = north
            coef_ref[3, c, t] = south


def north_of(column, t):
    return column[t + 1] if t < TILES - 1 else pltpu.roll(column[0], 7, 0)


def south_of(column, t):
    return column[t - 1] if t > 0 else pltpu.roll(column[TILES - 1], 1, 0)


def forward_steps(x, coef_ref):
    lane = lax.broadcasted_iota(jnp.int32, (8, 128), 1)
    first, last = lane == 0, lane == 127
    ends = len(x) - 1
    for _ in range(STEPS):
        new = []
        for c in range(len(x)):
            column = []
            for t in range(TILES):
                here = x[c][t]
                east = pltpu.roll(jnp.where(first, x[c + 1][t] if c < ends else 0.0, here), 127, 1)
                west = pltpu.roll(jnp.where(last, x[c - 1][t] if c > 0 else 0.0, here), 1, 1)
                column.append(
                    (here + coef_ref[0, c, t] * east)
                    + coef_ref[1, c, t] * west
                    + (coef_ref[2, c, t] * north_of(x[c], t) + coef_ref[3, c, t] * south_of(x[c], t))
                )
            new.append(column)
        x = new
    return x


def backward_steps(y, coef_ref):
    lane = lax.broadcasted_iota(jnp.int32, (8, 128), 1)
    first, last = lane == 0, lane == 127
    ends = len(y) - 1
    for _ in range(STEPS):
        new = []
        for c in range(len(y)):
            column = []
            up = [coef_ref[3, c, t] * y[c][t] for t in range(TILES)]
            down = [coef_ref[2, c, t] * y[c][t] for t in range(TILES)]
            for t in range(TILES):
                here = y[c][t]
                after = coef_ref[1, c + 1, t] * y[c + 1][t] if c < ends else 0.0
                before = coef_ref[0, c - 1, t] * y[c - 1][t] if c > 0 else 0.0
                east = pltpu.roll(jnp.where(first, after, coef_ref[1, c, t] * here), 127, 1)
                west = pltpu.roll(jnp.where(last, before, coef_ref[0, c, t] * here), 1, 1)
                column.append((here + east) + west + (north_of(up, t) + south_of(down, t)))
            new.append(column)
        y = new
    return y


def one_hots(index, blocks):
    count = index.shape[1]
    high = lax.broadcasted_iota(jnp.int32, (blocks[0], count), 0) == (index >> 6)
    low = lax.broadcasted_iota(jnp.int32, (blocks[1], count), 0) == (index & 63)
    return high, low


def forward_kernel(
    incr_hbm, wind_hbm, head_in, tail_in, ends_hbm,
    incr_ref, wind_ref, head_ref, tail_ref, stage_ref, coef_ref, ends_ref, level_sems,
):
    levels, rows, width = incr_ref.shape
    half = levels // 2

    def fetch(kind, index):
        source, target = ((wind_hbm, wind_ref), (incr_hbm, incr_ref))[kind]
        return pltpu.make_async_copy(source.at[index], target.at[index], level_sems.at[kind, index])

    def put(index):
        part = pl.ds(pl.multiple_of(index * rows, rows), rows)
        return pltpu.make_async_copy(ends_ref.at[part], ends_hbm.at[part], level_sems.at[2, index])

    for level in range(half):
        for index in (level, level + half):
            for kind in range(2):
                fetch(kind, index).start()
    head_ref[...] = head_in[: levels * 8].astype(F32)
    tail_ref[...] = tail_in[: levels * 8].astype(F32)
    low = low_half((8, width))

    def at_level(level, carry):
        for index in (level, level + half):
            for kind in range(2):
                fetch(kind, index).wait()
        coefficients(level, levels, wind_ref, head_ref, tail_ref, stage_ref, coef_ref)

        def at_group(group):
            index = level + group * half
            at = pl.ds(pl.multiple_of(index * 8, 8), 8)
            margin = jnp.where(low, head_ref[at, :], tail_ref[at, :])
            x = forward_steps(spread_rows(stage_ref.at[2 + 2 * group], incr_ref[index], margin), coef_ref)
            ends = join_rows(stage_ref.at[3 + 2 * group], x, rows)
            ends_ref[pl.ds(pl.multiple_of(index * rows, rows), rows), :] = ends.astype(BF16)
            put(index).start()

        for group in range(2):
            at_group(group)
        return carry

    lax.fori_loop(0, half, at_level, 0)
    for index in range(levels):
        put(index).wait()


def observe_kernel(
    incr_hbm, index_ref, dual_ref, variance_ref, cols_hbm, lines_hbm, _after,
    tall_ref, obs_ref, incr_ref, cols_ref, lines_ref, sems,
):
    levels, rows, width = incr_ref.shape
    copies = Copies(sems)
    block_in = [copies.start(cols_hbm, cols_ref), copies.start(lines_hbm, lines_ref)]
    incr_in = copies.start(incr_hbm, incr_ref)
    for copy in block_in:
        copy.wait()
    cols, lines = cols_ref[...], lines_ref[...]
    blocks = (lines.shape[0], cols.shape[1])
    high, low_hot = one_hots(index_ref[...], blocks)
    weights = low_hot.astype(BF16)
    summed = sum(nt(p, weights) for p in parts(jnp.where(high, dual_ref[...], 0.0))) * 0.125
    tall_ref[...] = sum(tn(lines, p) for p in parts(summed))
    incr_in.wait()
    narrow = sum(nn(p, cols) for p in parts(incr_ref[...].reshape(levels * rows, width)))
    sums = sum(nn(lines, p) for p in parts(narrow))
    high = high.astype(BF16)
    picked = sum(tn(p, high) for p in parts(sums))
    observed = jnp.sum(jnp.where(low_hot, picked, 0.0), axis=0, keepdims=True) * 0.125
    obs_ref[...] = variance_ref[...] * dual_ref[...] + observed


def backward_kernel(
    coming_ref, wind_hbm, head_in, tail_in, mult_hbm, tall_ref, cols_hbm,
    state_hbm,
    wind_ref, mult_ref, cols_ref,
    head_ref, tail_ref, far_ref, margins_ref, stage_ref, coef_ref, spread_ref, state_ref, sems, level_sems,
):
    levels, rows, width = mult_ref.shape
    half = levels // 2
    copies = Copies(sems)
    full = levels * rows
    arriving = [
        copies.start(source, target)
        for source, target in ((cols_hbm, cols_ref), (wind_hbm, wind_ref), (mult_hbm, mult_ref))
    ]
    arriving[0].wait()
    spread_ref[...] = sum(nt(p, cols_ref[...]) for p in parts(tall_ref[...]))
    for copy in arriving[1:]:
        copy.wait()
    head_ref[...] = head_in[: levels * 8].astype(F32)
    tail_ref[...] = tail_in[: levels * 8].astype(F32)
    far_ref[...] = coming_ref[full:].astype(F32)
    low = low_half((8, width))

    def put(index):
        return pltpu.make_async_copy(state_ref.at[index], state_hbm.at[index], level_sems.at[index])

    def at_level(level, carry):
        coefficients(level, levels, wind_ref, head_ref, tail_ref, stage_ref, coef_ref)
        at = pl.ds(pl.multiple_of(level * 8, 8), 8)
        head, tail = far_ref[at, :], far_ref[pl.ds(pl.multiple_of(level * 8 + levels * 4, 8), 8), :]
        margins_ref[0] = jnp.where(low, head, tail)
        margins_ref[1] = pltpu.roll(jnp.where(low, tail, head), HALF, 0)

        def at_group(group):
            index = level + group * half
            part = pl.ds(pl.multiple_of(index * rows, rows), rows)
            main = coming_ref[part, :].astype(F32)
            y = backward_steps(spread_rows(stage_ref.at[2 + 2 * group], main, margins_ref[group]), coef_ref)
            back = join_rows(stage_ref.at[3 + 2 * group], y, rows)
            state_ref[index] = (mult_ref[index] - back) + spread_ref[part, :]
            put(index).start()

        for group in range(2):
            at_group(group)
        return carry

    lax.fori_loop(0, half, at_level, 0)
    for index in range(levels):
        put(index).wait()


def gather_lines(came_ref, lines_ref):
    count, rows, wide = came_ref.shape
    groups, fields = count // 4, wide // 128
    source = lax.broadcasted_iota(jnp.int32, (512, 512), 0)
    target = lax.broadcasted_iota(jnp.int32, (512, 512), 1)
    swapped = ((target & 127) >> 5) * 128 + (target >> 7) * 32 + (target & 31)
    perm = (source == swapped).astype(BF16)
    for g in range(fields):
        piece = came_ref[:, :, g * 128 : (g + 1) * 128].reshape(groups, 4, rows, 128)
        left = jnp.concatenate([piece[:, i].reshape(groups * rows, 128) for i in range(4)], axis=1)
        moved = nn(left, perm).astype(BF16)
        for i in range(4):
            for b in range(groups):
                lines_ref[(4 * g + i) * rows : (4 * g + i + 1) * rows, b * 128 : (b + 1) * 128] = moved[
                    b * rows : (b + 1) * rows, i * 128 : (i + 1) * 128
                ]


def latitude_kernel(
    came_ref, var_hbm, turned_hbm, out_hbm,
    var_ref, turned_ref, lines_ref, scaled_ref, out_ref, sems,
):
    copies = Copies(sems)
    turned_in = copies.start(turned_hbm, turned_ref)
    var_in = copies.start(var_hbm, var_ref)
    gather_lines(came_ref, lines_ref)
    turned_in.wait()
    latitude = nn(lines_ref[...], turned_ref[...])
    var_in.wait()
    scaled_ref[...] = (latitude * var_ref[...]).astype(BF16)
    scaled = scaled_ref[...]
    out = []
    for i in range(2):
        part = pl.ds(512 * i, 512)
        out_ref[part] = nt(turned_ref[part], scaled).astype(BF16)
        out.append(copies.start(out_ref.at[part], out_hbm.at[part]))
    for copy in out:
        copy.wait()


def finish_kernel(
    came_ref, incr_hbm, prev_ref, table_hbm, out_hbm,
    incr_ref, table_ref, lines_ref, out_ref, sems,
):
    copies = Copies(sems)
    table_in = copies.start(table_hbm, table_ref)
    incr_in = copies.start(incr_hbm, incr_ref)
    gather_lines(came_ref, lines_ref)
    table_in.wait()
    table = table_ref[...]
    out = []
    for i in range(3):
        part = pl.ds(128 * i, 128)
        covar = nn(lines_ref[part], table)
        if i == 0:
            incr_in.wait()
        out_ref[part] = covar + (incr_ref[part] - prev_ref[part].astype(F32))
        out.append(copies.start(out_ref.at[part], out_hbm.at[part]))
    for copy in out:
        copy.wait()


VMEM = pl.BlockSpec(memory_space=pltpu.VMEM)
HBM = pl.BlockSpec(memory_space=pl.ANY)


def call(kernel, outs, ins, scratch, name, aliases=None, near=(), grant=52):
    def place(index, a):
        small = a.shape[0] == 1 or (len(a.shape) == 2 and a.shape[1] < 128 and a.dtype == F32)
        return VMEM if small or index in near else HBM

    single = not isinstance(outs, tuple)
    out_specs = [place(len(ins) + i, a) for i, a in enumerate((outs,) if single else outs)]
    return pl.pallas_call(
        kernel,
        out_shape=outs,
        in_specs=[place(i, a) for i, a in enumerate(ins)],
        out_specs=out_specs[0] if single else tuple(out_specs),
        scratch_shapes=list(scratch),
        compiler_params=pltpu.CompilerParams(vmem_limit_bytes=grant * 1024 * 1024),
        input_output_aliases=aliases or {},
        name=name,
    )(*ins)


def local(increment, multiplier, obs_dual, obs_index, obs_variance, winds, spectral_var):
    rows, levels, width = increment.shape[1:]
    count = lax.axis_size("space")
    times = lax.axis_size("tm")
    lat = rows * count
    waves = width // count
    full = levels * rows
    incr = jnp.transpose(increment[0], (1, 0, 2))
    mult = jnp.transpose(multiplier[0], (1, 0, 2))
    wind = jnp.transpose(winds[0], (1, 0, 2))
    var = jnp.transpose(spectral_var, (1, 2, 0)).reshape(full, lat)
    table = cosine_table(width)
    turned = np.ascontiguousarray(table.T)
    cols, lines = block_sums(levels, rows, width)

    def shape(*dims):
        return jax.ShapeDtypeStruct(dims, BF16)

    def wide(*dims):
        return pltpu.VMEM(dims, F32)

    def short(*dims):
        return pltpu.VMEM(dims, BF16)

    def sems(*dims):
        return pltpu.SemaphoreType.DMA(dims)

    field = (levels, rows, width)
    head, tail = call(
        edge_kernel,
        (shape(levels * 12, width), shape(levels * 12, width)),
        (mult, incr, wind),
        [wide(6, levels, 8, width), sems(6)],
        "edges",
        near=(3, 4),
        grant=52,
    )
    whole, spec = call(
        start_kernel,
        (shape(full + levels * 8, width), shape(width, full)),
        (mult, table, head),
        [short(full, width), short(width, full), sems(3)],
        "start",
        near=(0,1,2),
        grant=40,
    )
    ring = [(i, (i + 1) % count) for i in range(count)]
    head = lax.ppermute(head, "space", [(b, a) for a, b in ring])
    tail = lax.ppermute(tail, "space", ring)
    spec = call(order_kernel, shape(width, full), (spec, head, tail), [], "order", {0: 0}, near=(1, 2))
    came = lax.all_to_all(spec.reshape(count, waves, full), "space", 0, 0, tiled=True)
    whole = call(
        join_kernel,
        shape(full + levels * 8, width),
        (whole, head, tail),
        [sems(2)],
        "join",
        {0: 0},
        near=(1, 2),
    )
    coming = lax.ppermute(whole, "tm", [(t + 1, t) for t in range(times - 1)])

    across = width // 128
    stages = [wide(6, across, rows + 8, 128), wide(4, across, TILES, 8, 128)]
    ends = call(
        forward_kernel,
        shape(full, width),
        (incr, wind, head, tail),
        [
            wide(*field), wide(*field), wide(levels * 8, width), wide(levels * 8, width), *stages,
            short(full, width), sems(3, levels),
        ],
        "forward",
        near=(2, 3),
    )
    previous = lax.ppermute(ends, "tm", [(t, t + 1) for t in range(times - 1)])

    back = call(
        latitude_kernel,
        shape(lat, full),
        (came, var, turned),
        [
            wide(full, lat), short(lat, lat), short(full, lat), short(full, lat),
            short(lat, full), sems(16),
        ],
        "latitude",
        near=(0,),
    )
    returned = lax.all_to_all(back.reshape(count, rows, full), "space", 0, 0, tiled=True)

    tall, obs_rows = call(
        observe_kernel,
        (jax.ShapeDtypeStruct((full, cols.shape[1]), F32), jax.ShapeDtypeStruct(obs_dual.shape, F32)),
        (incr, obs_index, obs_dual, obs_variance, cols, lines, back),
        [wide(*field), short(*cols.shape), short(*lines.shape), sems(3)],
        "observe",
    )
    state_rows = call(
        backward_kernel,
        jax.ShapeDtypeStruct(field, F32),
        (coming, wind, head, tail, mult, tall, cols),
        [
            wide(*field), wide(*field), short(*cols.shape),
            wide(levels * 8, width), wide(levels * 8, width), wide(levels * 8, width), wide(2, 8, width),
            *stages, wide(full, width), wide(*field), sems(3), sems(levels),
        ],
        "backward",
        near=(0, 2, 3),
    )
    model_rows = call(
        finish_kernel,
        jax.ShapeDtypeStruct((full, width), F32),
        (returned, incr.reshape(full, width), previous, table),
        [
            wide(full, width), short(width, width),
            short(full, width), wide(full, width), sems(20),
        ],
        "finish",
        near=(0, 2),
    )

    def placed(whole):
        return jnp.transpose(whole.reshape(field), (1, 0, 2))[None]

    return (placed(model_rows), obs_rows, placed(state_rows))


def solution(mesh):
    specs = (
        P("tm", "space", None, None),
        P("tm", "space", None, None),
        P("tm", "space"),
        P("tm", "space"),
        P("tm", "space"),
        P("tm", "space", None, None),
        P(None, None, "space"),
    )
    return jax.shard_map(
        local,
        mesh=mesh,
        in_specs=specs,
        out_specs=(P("tm", "space", None, None), P("tm", "space"), P("tm", "space", None, None)),
        check_vma=False,
    )
```

```python
import math

import jax
import jax.numpy as jnp
import numpy as np
from jax import lax
from jax.experimental import pallas as pl
from jax.experimental.pallas import tpu as pltpu
from jax.sharding import PartitionSpec as P
import ml_dtypes

STEPS = 4
HALF = 4
F32 = jnp.float32
BF16 = jnp.bfloat16


def cosine_table(count):
    wave = np.arange(count)[:, None]
    point = np.arange(count)[None, :]
    phase = (2 * point + 1) * wave % (4 * count)
    table = np.cos(phase * (math.pi / (2.0 * count))) * math.sqrt(2.0 / count)
    table = np.where(wave == 0, table * math.sqrt(0.5), table)
    return table.astype(np.float32).astype(ml_dtypes.bfloat16)


def block_sums(levels, rows, width):
    cols = (np.arange(width)[:, None] // 16 == np.arange(width // 16)[None, :]).astype(np.float32)
    out = np.arange(rows // 4 * levels)[:, None]
    inn = np.arange(levels * rows)[None, :]
    lines = ((out % levels == inn // rows) & (out // levels == inn % rows // 4)).astype(np.float32)
    return cols.astype(ml_dtypes.bfloat16), lines.astype(ml_dtypes.bfloat16)


def nt(a, b):
    return lax.dot_general(a, b, (((1,), (1,)), ((), ())), preferred_element_type=F32)


def tn(a, b):
    return lax.dot_general(a, b, (((0,), (0,)), ((), ())), preferred_element_type=F32)


def nn(a, b):
    return jnp.dot(a, b, preferred_element_type=F32)


def parts(a):
    first = a.astype(BF16)
    return first, (a - first.astype(F32)).astype(BF16)


def low_half(shape):
    return lax.broadcasted_iota(jnp.int32, shape, len(shape) - 2) < HALF


class Copies:
    def __init__(self, sems):
        self.sems = sems
        self.count = 0

    def start(self, source, target):
        copy = pltpu.make_async_copy(source, target, self.sems.at[self.count])
        self.count += 1
        copy.start()
        return copy


def by_parity(even, odd):
    return jnp.where(lax.axis_index("space") % 2 == 0, even, odd)


def edge_kernel(mult_hbm, incr_hbm, wind_hbm, mate_ref, other_ref, edge_ref, sems):
    levels, rows, width = mult_hbm.shape
    half = levels // 2
    copies = Copies(sems)
    coming = [
        copies.start(source.at[:, pl.ds(at, 8), :], edge_ref.at[3 * end + i])
        for end, at in enumerate((0, rows - 8))
        for i, source in enumerate((incr_hbm, wind_hbm, mult_hbm))
    ]
    messages = []
    for end in range(2):
        for copy in coming[3 * end : 3 * end + 3]:
            copy.wait()
        incr, wind, mult = edge_ref[3 * end], edge_ref[3 * end + 1], edge_ref[3 * end + 2]
        wind = pltpu.roll(wind, HALF, 1)
        second = pltpu.roll(mult[half:], HALF, 1)
        low, less = low_half((levels, 8, width)), low_half((half, 8, width))
        if end == 0:
            field, dual = jnp.where(low, incr, wind), jnp.where(less, mult[:half], second)
        else:
            field, dual = jnp.where(low, wind, incr), jnp.where(less, second, mult[:half])
        messages.append((field.reshape(levels * 8, width), dual.reshape(half * 8, width)))
    for part, (head, tail) in zip((pl.ds(0, levels * 8), pl.ds(levels * 8, half * 8)), zip(*messages)):
        mate_ref[part] = by_parity(tail, head).astype(BF16)
        other_ref[part] = by_parity(head, tail).astype(BF16)


def start_kernel(mult_ref, table_ref, _after, whole_hbm, spec_hbm, flat_ref, spec_ref, sems):
    levels, rows, width = mult_ref.shape
    copies = Copies(sems)
    half = table_ref.shape[0] // 2
    flat = mult_ref[...].reshape(levels * rows, width).astype(BF16)
    flat_ref[...] = flat
    out = [copies.start(flat_ref, whole_hbm.at[pl.ds(0, levels * rows)])]
    for i in range(2):
        part = pl.ds(half * i, half)
        spec_ref[part] = nt(table_ref[part], flat).astype(BF16)
        out.append(copies.start(spec_ref.at[part], spec_hbm.at[part]))
    for copy in out:
        copy.wait()


def order_kernel(_spec_in, _head, _tail, _spec_out):
    pass


def join_kernel(_whole_in, mate_ref, other_ref, whole_hbm, sems):
    copies = Copies(sems)
    size = whole_hbm.shape[0] // 10
    start, far = whole_hbm.shape[0] - 2 * size, mate_ref.shape[0] - size
    odd = lax.axis_index("space") % 2
    out = [
        copies.start(source.at[pl.ds(far, size)], whole_hbm.at[pl.ds(pl.multiple_of(start + size * at, 16), size)])
        for source, at in ((mate_ref, odd), (other_ref, 1 - odd))
    ]
    for copy in out:
        copy.wait()


TILES = 5


def spread_rows(stage_ref, main, margin):
    rows, width = main.shape
    across = width // 128
    for c in range(across):
        stage_ref[c, :rows, :] = main[:, c * 128 : (c + 1) * 128]
        stage_ref[c, rows:, :] = margin[:, c * 128 : (c + 1) * 128]
    return [[stage_ref[c, pl.ds(t, 8, stride=TILES), :] for t in range(TILES)] for c in range(across)]


def join_rows(stage_ref, tiles, rows, factor=0.2**STEPS):
    for c, column in enumerate(tiles):
        for t, tile in enumerate(column):
            stage_ref[c, pl.ds(t, 8, stride=TILES), :] = tile * factor
    return jnp.concatenate([stage_ref[c, :rows, :] for c in range(len(tiles))], axis=1)


def coefficients(level, levels, wind_ref, head_ref, tail_ref, stage_ref, coef_ref):
    rows = wind_ref.shape[1]
    low = low_half((8, wind_ref.shape[2]))
    sublane = lax.broadcasted_iota(jnp.int32, (8, 128), 0)

    def extended(index, stage):
        at = pl.ds(pl.multiple_of(index * 8, 8), 8)
        margin = pltpu.roll(jnp.where(low, tail_ref[at, :], head_ref[at, :]), HALF, 0)
        return spread_rows(stage, wind_ref[index], margin)

    u = extended(level, stage_ref.at[0])
    v = extended(level + levels // 2, stage_ref.at[1])
    place = lax.axis_index("space")
    start, end = place == 0, place == lax.axis_size("space") - 1

    def cut(value, row, t, edge):
        return jnp.where((sublane == row // TILES) & edge, 0.0, value) if t == row % TILES else value

    for c in range(len(u)):
        for t in range(TILES):
            north, south = 1.0 - v[c][t], 1.0 + v[c][t]
            north = cut(cut(north, rows - 1, t, end), rows + 7, t, start)
            south = cut(cut(south, 0, t, start), rows, t, end)
            coef_ref[0, c, t] = 1.0 - u[c][t]
            coef_ref[1, c, t] = 1.0 + u[c][t]
            coef_ref[2, c, t] = north
            coef_ref[3, c, t] = south


def north_of(column, t):
    return column[t + 1] if t < TILES - 1 else pltpu.roll(column[0], 7, 0)


def south_of(column, t):
    return column[t - 1] if t > 0 else pltpu.roll(column[TILES - 1], 1, 0)


def forward_steps(x, coef_ref):
    lane = lax.broadcasted_iota(jnp.int32, (8, 128), 1)
    first, last = lane == 0, lane == 127
    ends = len(x) - 1
    for _ in range(STEPS):
        new = []
        for c in range(len(x)):
            column = []
            for t in range(TILES):
                here = x[c][t]
                east = pltpu.roll(jnp.where(first, x[c + 1][t] if c < ends else 0.0, here), 127, 1)
                west = pltpu.roll(jnp.where(last, x[c - 1][t] if c > 0 else 0.0, here), 1, 1)
                column.append(
                    (here + coef_ref[0, c, t] * east)
                    + coef_ref[1, c, t] * west
                    + (coef_ref[2, c, t] * north_of(x[c], t) + coef_ref[3, c, t] * south_of(x[c], t))
                )
            new.append(column)
        x = new
    return x


def backward_steps(y, coef_ref):
    lane = lax.broadcasted_iota(jnp.int32, (8, 128), 1)
    first, last = lane == 0, lane == 127
    ends = len(y) - 1
    for _ in range(STEPS):
        new = []
        for c in range(len(y)):
            column = []
            up = [coef_ref[3, c, t] * y[c][t] for t in range(TILES)]
            down = [coef_ref[2, c, t] * y[c][t] for t in range(TILES)]
            for t in range(TILES):
                here = y[c][t]
                after = coef_ref[1, c + 1, t] * y[c + 1][t] if c < ends else 0.0
                before = coef_ref[0, c - 1, t] * y[c - 1][t] if c > 0 else 0.0
                east = pltpu.roll(jnp.where(first, after, coef_ref[1, c, t] * here), 127, 1)
                west = pltpu.roll(jnp.where(last, before, coef_ref[0, c, t] * here), 1, 1)
                column.append((here + east) + west + (north_of(up, t) + south_of(down, t)))
            new.append(column)
        y = new
    return y


def one_hots(index, blocks):
    count = index.shape[1]
    high = lax.broadcasted_iota(jnp.int32, (blocks[0], count), 0) == (index >> 6)
    low = lax.broadcasted_iota(jnp.int32, (blocks[1], count), 0) == (index & 63)
    return high, low


def forward_kernel(
    incr_hbm, wind_hbm, mate_ref, other_ref, ends_hbm,
    incr_ref, wind_ref, head_ref, tail_ref, stage_ref, coef_ref, ends_ref, level_sems,
):
    levels, rows, width = incr_ref.shape
    half = levels // 2

    def fetch(kind, index):
        source, target = ((wind_hbm, wind_ref), (incr_hbm, incr_ref))[kind]
        return pltpu.make_async_copy(source.at[index], target.at[index], level_sems.at[kind, index])

    def put(index):
        part = pl.ds(pl.multiple_of(index * rows, rows), rows)
        return pltpu.make_async_copy(ends_ref.at[part], ends_hbm.at[part], level_sems.at[2, index])

    for level in range(half):
        for index in (level, level + half):
            for kind in range(2):
                fetch(kind, index).start()
    mate, other = mate_ref[: levels * 8].astype(F32), other_ref[: levels * 8].astype(F32)
    head_ref[...] = by_parity(mate, other)
    tail_ref[...] = by_parity(other, mate)
    low = low_half((8, width))

    def at_level(level, carry):
        for index in (level, level + half):
            for kind in range(2):
                fetch(kind, index).wait()
        coefficients(level, levels, wind_ref, head_ref, tail_ref, stage_ref, coef_ref)

        def at_group(group):
            index = level + group * half
            at = pl.ds(pl.multiple_of(index * 8, 8), 8)
            margin = jnp.where(low, head_ref[at, :], tail_ref[at, :])
            x = forward_steps(spread_rows(stage_ref.at[2 + 2 * group], incr_ref[index], margin), coef_ref)
            ends = join_rows(stage_ref.at[3 + 2 * group], x, rows)
            ends_ref[pl.ds(pl.multiple_of(index * rows, rows), rows), :] = ends.astype(BF16)
            put(index).start()

        for group in range(2):
            at_group(group)
        return carry

    lax.fori_loop(0, half, at_level, 0)
    for index in range(levels):
        put(index).wait()


def observe_kernel(
    incr_hbm, index_ref, dual_ref, variance_ref, cols_hbm, lines_hbm, _after,
    tall_ref, obs_ref, incr_ref, cols_ref, lines_ref, sems,
):
    levels, rows, width = incr_ref.shape
    copies = Copies(sems)
    block_in = [copies.start(cols_hbm, cols_ref), copies.start(lines_hbm, lines_ref)]
    incr_in = copies.start(incr_hbm, incr_ref)
    for copy in block_in:
        copy.wait()
    cols, lines = cols_ref[...], lines_ref[...]
    blocks = (lines.shape[0], cols.shape[1])
    high, low_hot = one_hots(index_ref[...], blocks)
    weights = low_hot.astype(BF16)
    summed = sum(nt(p, weights) for p in parts(jnp.where(high, dual_ref[...], 0.0))) * 0.125
    tall_ref[...] = sum(tn(lines, p) for p in parts(summed))
    incr_in.wait()
    narrow = sum(nn(p, cols) for p in parts(incr_ref[...].reshape(levels * rows, width)))
    sums = sum(nn(lines, p) for p in parts(narrow))
    high = high.astype(BF16)
    picked = sum(tn(p, high) for p in parts(sums))
    observed = jnp.sum(jnp.where(low_hot, picked, 0.0), axis=0, keepdims=True) * 0.125
    obs_ref[...] = variance_ref[...] * dual_ref[...] + observed


def backward_kernel(
    coming_ref, wind_hbm, mate_ref, other_ref, mult_hbm, tall_ref, cols_hbm,
    state_hbm,
    wind_ref, mult_ref, cols_ref,
    head_ref, tail_ref, far_ref, margins_ref, stage_ref, coef_ref, spread_ref, state_ref, sems, level_sems,
):
    levels, rows, width = mult_ref.shape
    half = levels // 2
    copies = Copies(sems)
    full = levels * rows
    arriving = [
        copies.start(source, target)
        for source, target in ((cols_hbm, cols_ref), (wind_hbm, wind_ref), (mult_hbm, mult_ref))
    ]
    arriving[0].wait()
    spread_ref[...] = sum(nt(p, cols_ref[...]) for p in parts(tall_ref[...]))
    for copy in arriving[1:]:
        copy.wait()
    mate, other = mate_ref[: levels * 8].astype(F32), other_ref[: levels * 8].astype(F32)
    head_ref[...] = by_parity(mate, other)
    tail_ref[...] = by_parity(other, mate)
    far_ref[...] = coming_ref[full:].astype(F32)
    low = low_half((8, width))

    def put(index):
        return pltpu.make_async_copy(state_ref.at[index], state_hbm.at[index], level_sems.at[index])

    factor = jnp.where(lax.axis_index("tm") == lax.axis_size("tm") - 1, 0.0, 0.2**STEPS)

    def at_level(level, carry):
        coefficients(level, levels, wind_ref, head_ref, tail_ref, stage_ref, coef_ref)
        at = pl.ds(pl.multiple_of(level * 8, 8), 8)
        head, tail = far_ref[at, :], far_ref[pl.ds(pl.multiple_of(level * 8 + levels * 4, 8), 8), :]
        margins_ref[0] = jnp.where(low, head, tail)
        margins_ref[1] = pltpu.roll(jnp.where(low, tail, head), HALF, 0)

        def at_group(group):
            index = level + group * half
            part = pl.ds(pl.multiple_of(index * rows, rows), rows)
            main = coming_ref[part, :].astype(F32)
            y = backward_steps(spread_rows(stage_ref.at[2 + 2 * group], main, margins_ref[group]), coef_ref)
            back = join_rows(stage_ref.at[3 + 2 * group], y, rows, factor)
            state_ref[index] = (mult_ref[index] - back) + spread_ref[part, :]
            put(index).start()

        for group in range(2):
            at_group(group)
        return carry

    lax.fori_loop(0, half, at_level, 0)
    for index in range(levels):
        put(index).wait()


def gather_lines(came_ref, lines_ref):
    count, rows, wide = came_ref.shape
    groups, fields = count // 4, wide // 128
    source = lax.broadcasted_iota(jnp.int32, (512, 512), 0)
    target = lax.broadcasted_iota(jnp.int32, (512, 512), 1)
    swapped = ((target & 127) >> 5) * 128 + (target >> 7) * 32 + (target & 31)
    perm = (source == swapped).astype(BF16)
    for g in range(fields):
        piece = came_ref[:, :, g * 128 : (g + 1) * 128].reshape(groups, 4, rows, 128)
        left = jnp.concatenate([piece[:, i].reshape(groups * rows, 128) for i in range(4)], axis=1)
        moved = nn(left, perm).astype(BF16)
        for i in range(4):
            for b in range(groups):
                lines_ref[(4 * g + i) * rows : (4 * g + i + 1) * rows, b * 128 : (b + 1) * 128] = moved[
                    b * rows : (b + 1) * rows, i * 128 : (i + 1) * 128
                ]


def latitude_kernel(
    came_ref, var_hbm, turned_hbm, out_hbm,
    var_ref, turned_ref, lines_ref, scaled_ref, out_ref, sems,
):
    copies = Copies(sems)
    turned_in = copies.start(turned_hbm, turned_ref)
    var_in = copies.start(var_hbm, var_ref)
    gather_lines(came_ref, lines_ref)
    turned_in.wait()
    latitude = nn(lines_ref[...], turned_ref[...])
    var_in.wait()
    scaled_ref[...] = (latitude * var_ref[...]).astype(BF16)
    scaled = scaled_ref[...]
    out = []
    for i in range(2):
        part = pl.ds(512 * i, 512)
        out_ref[part] = nt(turned_ref[part], scaled).astype(BF16)
        out.append(copies.start(out_ref.at[part], out_hbm.at[part]))
    for copy in out:
        copy.wait()


def finish_kernel(
    came_ref, incr_hbm, prev_ref, table_hbm, out_hbm,
    incr_ref, table_ref, lines_ref, out_ref, sems,
):
    after = jnp.where(lax.axis_index("tm") == 0, 0.0, 1.0)
    copies = Copies(sems)
    table_in = copies.start(table_hbm, table_ref)
    incr_in = copies.start(incr_hbm, incr_ref)
    gather_lines(came_ref, lines_ref)
    table_in.wait()
    table = table_ref[...]
    out = []
    for i in range(3):
        part = pl.ds(128 * i, 128)
        covar = nn(lines_ref[part], table)
        if i == 0:
            incr_in.wait()
        out_ref[part] = covar + (incr_ref[part] - prev_ref[part].astype(F32) * after)
        out.append(copies.start(out_ref.at[part], out_hbm.at[part]))
    for copy in out:
        copy.wait()


VMEM = pl.BlockSpec(memory_space=pltpu.VMEM)
HBM = pl.BlockSpec(memory_space=pl.ANY)


def call(kernel, outs, ins, scratch, name, aliases=None, near=(), grant=52):
    def place(index, a):
        small = a.shape[0] == 1 or (len(a.shape) == 2 and a.shape[1] < 128 and a.dtype == F32)
        return VMEM if small or index in near else HBM

    single = not isinstance(outs, tuple)
    out_specs = [place(len(ins) + i, a) for i, a in enumerate((outs,) if single else outs)]
    return pl.pallas_call(
        kernel,
        out_shape=outs,
        in_specs=[place(i, a) for i, a in enumerate(ins)],
        out_specs=out_specs[0] if single else tuple(out_specs),
        scratch_shapes=list(scratch),
        compiler_params=pltpu.CompilerParams(vmem_limit_bytes=grant * 1024 * 1024),
        input_output_aliases=aliases or {},
        name=name,
    )(*ins)


def local(increment, multiplier, obs_dual, obs_index, obs_variance, winds, spectral_var):
    rows, levels, width = increment.shape[1:]
    count = lax.axis_size("space")
    times = lax.axis_size("tm")
    lat = rows * count
    waves = width // count
    full = levels * rows
    incr = jnp.transpose(increment[0], (1, 0, 2))
    mult = jnp.transpose(multiplier[0], (1, 0, 2))
    wind = jnp.transpose(winds[0], (1, 0, 2))
    var = jnp.transpose(spectral_var, (1, 2, 0)).reshape(full, lat)
    table = cosine_table(width)
    turned = np.ascontiguousarray(table.T)
    cols, lines = block_sums(levels, rows, width)

    def shape(*dims):
        return jax.ShapeDtypeStruct(dims, BF16)

    def wide(*dims):
        return pltpu.VMEM(dims, F32)

    def short(*dims):
        return pltpu.VMEM(dims, BF16)

    def sems(*dims):
        return pltpu.SemaphoreType.DMA(dims)

    field = (levels, rows, width)
    mate, other = call(
        edge_kernel,
        (shape(levels * 12, width), shape(levels * 12, width)),
        (mult, incr, wind),
        [wide(6, levels, 8, width), sems(6)],
        "edges",
        near=(3, 4),
        grant=52,
    )
    whole, spec = call(
        start_kernel,
        (shape(full + levels * 8, width), shape(width, full)),
        (mult, table, mate),
        [short(full, width), short(width, full), sems(3)],
        "start",
        near=(0,1,2),
        grant=40,
    )
    mates = [(i, i ^ 1) for i in range(count)]
    others = [(i, min(max(((i + 1) ^ 1) - 1, 0), count - 1)) for i in range(count)]
    mate = lax.ppermute(mate, "space", mates)
    other = lax.ppermute(other, "space", others)
    spec = call(order_kernel, shape(width, full), (spec, mate, other), [], "order", {0: 0}, near=(1, 2))
    came = lax.all_to_all(spec.reshape(count, waves, full), "space", 0, 0, tiled=True)
    whole = call(
        join_kernel,
        shape(full + levels * 8, width),
        (whole, mate, other),
        [sems(2)],
        "join",
        {0: 0},
        near=(1, 2),
    )
    coming = lax.ppermute(whole, "tm", [((t + 1) % times, t) for t in range(times)])

    across = width // 128
    stages = [wide(6, across, rows + 8, 128), wide(4, across, TILES, 8, 128)]
    ends = call(
        forward_kernel,
        shape(full, width),
        (incr, wind, mate, other),
        [
            wide(*field), wide(*field), wide(levels * 8, width), wide(levels * 8, width), *stages,
            short(full, width), sems(3, levels),
        ],
        "forward",
        near=(2, 3),
    )
    previous = lax.ppermute(ends, "tm", [(t, (t + 1) % times) for t in range(times)])

    back = call(
        latitude_kernel,
        shape(lat, full),
        (came, var, turned),
        [
            wide(full, lat), short(lat, lat), short(full, lat), short(full, lat),
            short(lat, full), sems(16),
        ],
        "latitude",
        near=(0,),
    )
    returned = lax.all_to_all(back.reshape(count, rows, full), "space", 0, 0, tiled=True)

    tall, obs_rows = call(
        observe_kernel,
        (jax.ShapeDtypeStruct((full, cols.shape[1]), F32), jax.ShapeDtypeStruct(obs_dual.shape, F32)),
        (incr, obs_index, obs_dual, obs_variance, cols, lines, back),
        [wide(*field), short(*cols.shape), short(*lines.shape), sems(3)],
        "observe",
    )
    state_rows = call(
        backward_kernel,
        jax.ShapeDtypeStruct(field, F32),
        (coming, wind, mate, other, mult, tall, cols),
        [
            wide(*field), wide(*field), short(*cols.shape),
            wide(levels * 8, width), wide(levels * 8, width), wide(levels * 8, width), wide(2, 8, width),
            *stages, wide(full, width), wide(*field), sems(3), sems(levels),
        ],
        "backward",
        near=(0, 2, 3),
    )
    model_rows = call(
        finish_kernel,
        jax.ShapeDtypeStruct((full, width), F32),
        (returned, incr.reshape(full, width), previous, table),
        [
            wide(full, width), short(width, width),
            short(full, width), wide(full, width), sems(20),
        ],
        "finish",
        near=(0, 2),
    )

    def placed(whole):
        return jnp.transpose(whole.reshape(field), (1, 0, 2))[None]

    return (placed(model_rows), obs_rows, placed(state_rows))


def solution(mesh):
    specs = (
        P("tm", "space", None, None),
        P("tm", "space", None, None),
        P("tm", "space"),
        P("tm", "space"),
        P("tm", "space"),
        P("tm", "space", None, None),
        P(None, None, "space"),
    )
    return jax.shard_map(
        local,
        mesh=mesh,
        in_specs=specs,
        out_specs=(P("tm", "space", None, None), P("tm", "space"), P("tm", "space", None, None)),
        check_vma=False,
    )
```

```python
import math

import jax
import jax.numpy as jnp
import numpy as np
from jax import lax
from jax.experimental import pallas as pl
from jax.experimental.pallas import tpu as pltpu
from jax.sharding import PartitionSpec as P
import ml_dtypes

STEPS = 4
HALF = 4
F32 = jnp.float32
BF16 = jnp.bfloat16


def cosine_table(count):
    wave = np.arange(count)[:, None]
    point = np.arange(count)[None, :]
    phase = (2 * point + 1) * wave % (4 * count)
    table = np.cos(phase * (math.pi / (2.0 * count))) * math.sqrt(2.0 / count)
    table = np.where(wave == 0, table * math.sqrt(0.5), table)
    return table.astype(np.float32).astype(ml_dtypes.bfloat16)


def block_sums(levels, rows, width):
    cols = (np.arange(width)[:, None] // 16 == np.arange(width // 16)[None, :]).astype(np.float32)
    out = np.arange(rows // 4 * levels)[:, None]
    inn = np.arange(levels * rows)[None, :]
    lines = ((out % levels == inn // rows) & (out // levels == inn % rows // 4)).astype(np.float32)
    return cols.astype(ml_dtypes.bfloat16), lines.astype(ml_dtypes.bfloat16)


def nt(a, b):
    return lax.dot_general(a, b, (((1,), (1,)), ((), ())), preferred_element_type=F32)


def tn(a, b):
    return lax.dot_general(a, b, (((0,), (0,)), ((), ())), preferred_element_type=F32)


def nn(a, b):
    return jnp.dot(a, b, preferred_element_type=F32)


def parts(a):
    first = a.astype(BF16)
    return first, (a - first.astype(F32)).astype(BF16)


def low_half(shape):
    return lax.broadcasted_iota(jnp.int32, shape, len(shape) - 2) < HALF


class Copies:
    def __init__(self, sems):
        self.sems = sems
        self.count = 0

    def start(self, source, target):
        copy = pltpu.make_async_copy(source, target, self.sems.at[self.count])
        self.count += 1
        copy.start()
        return copy


def by_parity(even, odd):
    return jnp.where(lax.axis_index("space") % 2 == 0, even, odd)


def edge_kernel(mult_hbm, incr_hbm, wind_hbm, mate_ref, other_ref, edge_ref, sems):
    levels, rows, width = mult_hbm.shape
    half = levels // 2
    copies = Copies(sems)
    coming = [
        copies.start(source.at[:, pl.ds(at, 8), :], edge_ref.at[3 * end + i])
        for end, at in enumerate((0, rows - 8))
        for i, source in enumerate((incr_hbm, wind_hbm, mult_hbm))
    ]
    messages = []
    for end in range(2):
        for copy in coming[3 * end : 3 * end + 3]:
            copy.wait()
        incr, wind, mult = edge_ref[3 * end], edge_ref[3 * end + 1], edge_ref[3 * end + 2]
        wind = pltpu.roll(wind, HALF, 1)
        second = pltpu.roll(mult[half:], HALF, 1)
        low, less = low_half((levels, 8, width)), low_half((half, 8, width))
        if end == 0:
            field, dual = jnp.where(low, incr, wind), jnp.where(less, mult[:half], second)
        else:
            field, dual = jnp.where(low, wind, incr), jnp.where(less, second, mult[:half])
        messages.append((field.reshape(levels * 8, width), dual.reshape(half * 8, width)))
    for part, (head, tail) in zip((pl.ds(0, levels * 8), pl.ds(levels * 8, half * 8)), zip(*messages)):
        mate_ref[part] = by_parity(tail, head).astype(BF16)
        other_ref[part] = by_parity(head, tail).astype(BF16)


def start_kernel(mult_ref, table_ref, _after, whole_hbm, spec_hbm, flat_ref, spec_ref, sems):
    levels, rows, width = mult_ref.shape
    copies = Copies(sems)
    half = table_ref.shape[0] // 2
    flat = mult_ref[...].reshape(levels * rows, width).astype(BF16)
    flat_ref[...] = flat
    out = [copies.start(flat_ref, whole_hbm.at[pl.ds(0, levels * rows)])]
    for i in range(2):
        part = pl.ds(half * i, half)
        spec_ref[part] = nt(table_ref[part], flat).astype(BF16)
        out.append(copies.start(spec_ref.at[part], spec_hbm.at[part]))
    for copy in out:
        copy.wait()


def order_kernel(_spec_in, _head, _tail, _spec_out):
    pass


def join_kernel(_whole_in, mate_ref, other_ref, whole_hbm, sems):
    copies = Copies(sems)
    size = whole_hbm.shape[0] // 10
    start, far = whole_hbm.shape[0] - 2 * size, mate_ref.shape[0] - size
    odd = lax.axis_index("space") % 2
    out = [
        copies.start(source.at[pl.ds(far, size)], whole_hbm.at[pl.ds(pl.multiple_of(start + size * at, 16), size)])
        for source, at in ((mate_ref, odd), (other_ref, 1 - odd))
    ]
    for copy in out:
        copy.wait()


TILES = 5


def spread_rows(stage_ref, main, margin):
    rows, width = main.shape
    across = width // 128
    for c in range(across):
        stage_ref[c, :rows, :] = main[:, c * 128 : (c + 1) * 128]
        stage_ref[c, rows:, :] = margin[:, c * 128 : (c + 1) * 128]
    return [[stage_ref[c, pl.ds(t, 8, stride=TILES), :] for t in range(TILES)] for c in range(across)]


def join_rows(stage_ref, tiles, rows, factor=0.2**STEPS):
    for c, column in enumerate(tiles):
        for t, tile in enumerate(column):
            stage_ref[c, pl.ds(t, 8, stride=TILES), :] = tile * factor
    return jnp.concatenate([stage_ref[c, :rows, :] for c in range(len(tiles))], axis=1)


def coefficients(level, levels, wind_ref, head_ref, tail_ref, stage_ref, coef_ref):
    rows = wind_ref.shape[1]
    low = low_half((8, wind_ref.shape[2]))
    sublane = lax.broadcasted_iota(jnp.int32, (8, 128), 0)

    def extended(index, stage):
        at = pl.ds(pl.multiple_of(index * 8, 8), 8)
        margin = pltpu.roll(jnp.where(low, tail_ref[at, :], head_ref[at, :]), HALF, 0)
        return spread_rows(stage, wind_ref[index], margin)

    u = extended(level, stage_ref.at[0])
    v = extended(level + levels // 2, stage_ref.at[1])
    place = lax.axis_index("space")
    start, end = place == 0, place == lax.axis_size("space") - 1

    def cut(value, row, t, edge):
        return jnp.where((sublane == row // TILES) & edge, 0.0, value) if t == row % TILES else value

    for c in range(len(u)):
        for t in range(TILES):
            north, south = 1.0 - v[c][t], 1.0 + v[c][t]
            north = cut(cut(north, rows - 1, t, end), rows + 7, t, start)
            south = cut(cut(south, 0, t, start), rows, t, end)
            coef_ref[0, c, t] = 1.0 - u[c][t]
            coef_ref[1, c, t] = 1.0 + u[c][t]
            coef_ref[2, c, t] = north
            coef_ref[3, c, t] = south


def north_of(column, t):
    return column[t + 1] if t < TILES - 1 else pltpu.roll(column[0], 7, 0)


def south_of(column, t):
    return column[t - 1] if t > 0 else pltpu.roll(column[TILES - 1], 1, 0)


def forward_steps(x, coef_ref):
    lane = lax.broadcasted_iota(jnp.int32, (8, 128), 1)
    first, last = lane == 0, lane == 127
    ends = len(x) - 1
    for _ in range(STEPS):
        new = []
        for c in range(len(x)):
            column = []
            for t in range(TILES):
                here = x[c][t]
                east = pltpu.roll(jnp.where(first, x[c + 1][t] if c < ends else 0.0, here), 127, 1)
                west = pltpu.roll(jnp.where(last, x[c - 1][t] if c > 0 else 0.0, here), 1, 1)
                column.append(
                    (here + coef_ref[0, c, t] * east)
                    + coef_ref[1, c, t] * west
                    + (coef_ref[2, c, t] * north_of(x[c], t) + coef_ref[3, c, t] * south_of(x[c], t))
                )
            new.append(column)
        x = new
    return x


def backward_steps(y, coef_ref):
    lane = lax.broadcasted_iota(jnp.int32, (8, 128), 1)
    first, last = lane == 0, lane == 127
    ends = len(y) - 1
    for _ in range(STEPS):
        new = []
        for c in range(len(y)):
            column = []
            up = [coef_ref[3, c, t] * y[c][t] for t in range(TILES)]
            down = [coef_ref[2, c, t] * y[c][t] for t in range(TILES)]
            for t in range(TILES):
                here = y[c][t]
                after = coef_ref[1, c + 1, t] * y[c + 1][t] if c < ends else 0.0
                before = coef_ref[0, c - 1, t] * y[c - 1][t] if c > 0 else 0.0
                east = pltpu.roll(jnp.where(first, after, coef_ref[1, c, t] * here), 127, 1)
                west = pltpu.roll(jnp.where(last, before, coef_ref[0, c, t] * here), 1, 1)
                column.append((here + east) + west + (north_of(up, t) + south_of(down, t)))
            new.append(column)
        y = new
    return y


def one_hots(index, blocks):
    count = index.shape[1]
    high = lax.broadcasted_iota(jnp.int32, (blocks[0], count), 0) == (index >> 6)
    low = lax.broadcasted_iota(jnp.int32, (blocks[1], count), 0) == (index & 63)
    return high, low


def forward_kernel(
    incr_hbm, wind_hbm, mate_ref, other_ref, ends_hbm,
    incr_ref, wind_ref, head_ref, tail_ref, stage_ref, coef_ref, ends_ref, level_sems,
):
    levels, rows, width = incr_ref.shape
    half = levels // 2

    def fetch(kind, index):
        source, target = ((wind_hbm, wind_ref), (incr_hbm, incr_ref))[kind]
        return pltpu.make_async_copy(source.at[index], target.at[index], level_sems.at[kind, index])

    def put(index):
        part = pl.ds(pl.multiple_of(index * rows, rows), rows)
        return pltpu.make_async_copy(ends_ref.at[part], ends_hbm.at[part], level_sems.at[2, index])

    for level in range(half):
        for index in (level, level + half):
            for kind in range(2):
                fetch(kind, index).start()
    mate, other = mate_ref[: levels * 8].astype(F32), other_ref[: levels * 8].astype(F32)
    head_ref[...] = by_parity(mate, other)
    tail_ref[...] = by_parity(other, mate)
    low = low_half((8, width))

    factor = jnp.where(lax.axis_index("tm") == lax.axis_size("tm") - 1, 0.0, 0.2**STEPS)

    def at_level(level, carry):
        for index in (level, level + half):
            for kind in range(2):
                fetch(kind, index).wait()
        coefficients(level, levels, wind_ref, head_ref, tail_ref, stage_ref, coef_ref)

        def at_group(group):
            index = level + group * half
            at = pl.ds(pl.multiple_of(index * 8, 8), 8)
            margin = jnp.where(low, head_ref[at, :], tail_ref[at, :])
            x = forward_steps(spread_rows(stage_ref.at[2 + 2 * group], incr_ref[index], margin), coef_ref)
            ends = join_rows(stage_ref.at[3 + 2 * group], x, rows, factor)
            ends_ref[pl.ds(pl.multiple_of(index * rows, rows), rows), :] = ends.astype(BF16)
            put(index).start()

        for group in range(2):
            at_group(group)
        return carry

    lax.fori_loop(0, half, at_level, 0)
    for index in range(levels):
        put(index).wait()


def observe_kernel(
    incr_hbm, index_ref, dual_ref, variance_ref, cols_hbm, lines_hbm, _after,
    tall_ref, obs_ref, incr_ref, cols_ref, lines_ref, sems,
):
    levels, rows, width = incr_ref.shape
    copies = Copies(sems)
    block_in = [copies.start(cols_hbm, cols_ref), copies.start(lines_hbm, lines_ref)]
    incr_in = copies.start(incr_hbm, incr_ref)
    for copy in block_in:
        copy.wait()
    cols, lines = cols_ref[...], lines_ref[...]
    blocks = (lines.shape[0], cols.shape[1])
    high, low_hot = one_hots(index_ref[...], blocks)
    weights = low_hot.astype(BF16)
    summed = sum(nt(p, weights) for p in parts(jnp.where(high, dual_ref[...], 0.0))) * 0.125
    tall_ref[...] = sum(tn(lines, p) for p in parts(summed))
    incr_in.wait()
    narrow = sum(nn(p, cols) for p in parts(incr_ref[...].reshape(levels * rows, width)))
    sums = sum(nn(lines, p) for p in parts(narrow))
    high = high.astype(BF16)
    picked = sum(tn(p, high) for p in parts(sums))
    observed = jnp.sum(jnp.where(low_hot, picked, 0.0), axis=0, keepdims=True) * 0.125
    obs_ref[...] = variance_ref[...] * dual_ref[...] + observed


def backward_kernel(
    coming_ref, wind_hbm, mate_ref, other_ref, mult_hbm, tall_ref, cols_hbm,
    state_hbm,
    wind_ref, mult_ref, cols_ref,
    head_ref, tail_ref, far_ref, margins_ref, stage_ref, coef_ref, spread_ref, state_ref, sems, level_sems,
):
    levels, rows, width = mult_ref.shape
    half = levels // 2
    copies = Copies(sems)
    full = levels * rows
    arriving = [
        copies.start(source, target)
        for source, target in ((cols_hbm, cols_ref), (wind_hbm, wind_ref), (mult_hbm, mult_ref))
    ]
    arriving[0].wait()
    spread_ref[...] = sum(nt(p, cols_ref[...]) for p in parts(tall_ref[...]))
    for copy in arriving[1:]:
        copy.wait()
    mate, other = mate_ref[: levels * 8].astype(F32), other_ref[: levels * 8].astype(F32)
    head_ref[...] = by_parity(mate, other)
    tail_ref[...] = by_parity(other, mate)
    far_ref[...] = coming_ref[full:].astype(F32)
    low = low_half((8, width))

    def put(index):
        return pltpu.make_async_copy(state_ref.at[index], state_hbm.at[index], level_sems.at[index])

    factor = jnp.where(lax.axis_index("tm") == lax.axis_size("tm") - 1, 0.0, 0.2**STEPS)

    def at_level(level, carry):
        coefficients(level, levels, wind_ref, head_ref, tail_ref, stage_ref, coef_ref)
        at = pl.ds(pl.multiple_of(level * 8, 8), 8)
        head, tail = far_ref[at, :], far_ref[pl.ds(pl.multiple_of(level * 8 + levels * 4, 8), 8), :]
        margins_ref[0] = jnp.where(low, head, tail)
        margins_ref[1] = pltpu.roll(jnp.where(low, tail, head), HALF, 0)

        def at_group(group):
            index = level + group * half
            part = pl.ds(pl.multiple_of(index * rows, rows), rows)
            main = coming_ref[part, :].astype(F32)
            y = backward_steps(spread_rows(stage_ref.at[2 + 2 * group], main, margins_ref[group]), coef_ref)
            back = join_rows(stage_ref.at[3 + 2 * group], y, rows, factor)
            state_ref[index] = (mult_ref[index] - back) + spread_ref[part, :]
            put(index).start()

        for group in range(2):
            at_group(group)
        return carry

    lax.fori_loop(0, half, at_level, 0)
    for index in range(levels):
        put(index).wait()


def gather_lines(came_ref, lines_ref):
    count, rows, wide = came_ref.shape
    groups, fields = count // 4, wide // 128
    source = lax.broadcasted_iota(jnp.int32, (512, 512), 0)
    target = lax.broadcasted_iota(jnp.int32, (512, 512), 1)
    swapped = ((target & 127) >> 5) * 128 + (target >> 7) * 32 + (target & 31)
    perm = (source == swapped).astype(BF16)
    for g in range(fields):
        piece = came_ref[:, :, g * 128 : (g + 1) * 128].reshape(groups, 4, rows, 128)
        left = jnp.concatenate([piece[:, i].reshape(groups * rows, 128) for i in range(4)], axis=1)
        moved = nn(left, perm).astype(BF16)
        for i in range(4):
            for b in range(groups):
                lines_ref[(4 * g + i) * rows : (4 * g + i + 1) * rows, b * 128 : (b + 1) * 128] = moved[
                    b * rows : (b + 1) * rows, i * 128 : (i + 1) * 128
                ]


def latitude_kernel(
    came_ref, var_hbm, turned_hbm, out_hbm,
    var_ref, turned_ref, lines_ref, scaled_ref, out_ref, sems,
):
    copies = Copies(sems)
    turned_in = copies.start(turned_hbm, turned_ref)
    var_in = copies.start(var_hbm, var_ref)
    gather_lines(came_ref, lines_ref)
    turned_in.wait()
    latitude = nn(lines_ref[...], turned_ref[...])
    var_in.wait()
    scaled_ref[...] = (latitude * var_ref[...]).astype(BF16)
    scaled = scaled_ref[...]
    out = []
    for i in range(2):
        part = pl.ds(512 * i, 512)
        out_ref[part] = nt(turned_ref[part], scaled).astype(BF16)
        out.append(copies.start(out_ref.at[part], out_hbm.at[part]))
    for copy in out:
        copy.wait()


def finish_kernel(
    came_ref, incr_hbm, prev_ref, table_hbm, out_hbm,
    incr_ref, table_ref, lines_ref, out_ref, sems,
):
    copies = Copies(sems)
    table_in = copies.start(table_hbm, table_ref)
    incr_in = copies.start(incr_hbm, incr_ref)
    gather_lines(came_ref, lines_ref)
    table_in.wait()
    table = table_ref[...]
    out = []
    for i in range(3):
        part = pl.ds(128 * i, 128)
        covar = nn(lines_ref[part], table)
        if i == 0:
            incr_in.wait()
        out_ref[part] = covar + (incr_ref[part] - prev_ref[part].astype(F32))
        out.append(copies.start(out_ref.at[part], out_hbm.at[part]))
    for copy in out:
        copy.wait()


VMEM = pl.BlockSpec(memory_space=pltpu.VMEM)
HBM = pl.BlockSpec(memory_space=pl.ANY)


def call(kernel, outs, ins, scratch, name, aliases=None, near=(), grant=52):
    def place(index, a):
        small = a.shape[0] == 1 or (len(a.shape) == 2 and a.shape[1] < 128 and a.dtype == F32)
        return VMEM if small or index in near else HBM

    single = not isinstance(outs, tuple)
    out_specs = [place(len(ins) + i, a) for i, a in enumerate((outs,) if single else outs)]
    return pl.pallas_call(
        kernel,
        out_shape=outs,
        in_specs=[place(i, a) for i, a in enumerate(ins)],
        out_specs=out_specs[0] if single else tuple(out_specs),
        scratch_shapes=list(scratch),
        compiler_params=pltpu.CompilerParams(vmem_limit_bytes=grant * 1024 * 1024),
        input_output_aliases=aliases or {},
        name=name,
    )(*ins)


def local(increment, multiplier, obs_dual, obs_index, obs_variance, winds, spectral_var):
    rows, levels, width = increment.shape[1:]
    count = lax.axis_size("space")
    times = lax.axis_size("tm")
    lat = rows * count
    waves = width // count
    full = levels * rows
    incr = jnp.transpose(increment[0], (1, 0, 2))
    mult = jnp.transpose(multiplier[0], (1, 0, 2))
    wind = jnp.transpose(winds[0], (1, 0, 2))
    var = jnp.transpose(spectral_var, (1, 2, 0)).reshape(full, lat)
    table = cosine_table(width)
    turned = np.ascontiguousarray(table.T)
    cols, lines = block_sums(levels, rows, width)

    def shape(*dims):
        return jax.ShapeDtypeStruct(dims, BF16)

    def wide(*dims):
        return pltpu.VMEM(dims, F32)

    def short(*dims):
        return pltpu.VMEM(dims, BF16)

    def sems(*dims):
        return pltpu.SemaphoreType.DMA(dims)

    field = (levels, rows, width)
    mate, other = call(
        edge_kernel,
        (shape(levels * 12, width), shape(levels * 12, width)),
        (mult, incr, wind),
        [wide(6, levels, 8, width), sems(6)],
        "edges",
        near=(3, 4),
        grant=52,
    )
    whole, spec = call(
        start_kernel,
        (shape(full + levels * 8, width), shape(width, full)),
        (mult, table, mate),
        [short(full, width), short(width, full), sems(3)],
        "start",
        near=(0,1,2),
        grant=40,
    )
    mates = [(i, i ^ 1) for i in range(count)]
    others = [(i, min(max(((i + 1) ^ 1) - 1, 0), count - 1)) for i in range(count)]
    mate = lax.ppermute(mate, "space", mates)
    other = lax.ppermute(other, "space", others)
    spec = call(order_kernel, shape(width, full), (spec, mate, other), [], "order", {0: 0}, near=(1, 2))
    came = lax.all_to_all(spec.reshape(count, waves, full), "space", 0, 0, tiled=True)
    whole = call(
        join_kernel,
        shape(full + levels * 8, width),
        (whole, mate, other),
        [sems(2)],
        "join",
        {0: 0},
        near=(1, 2),
    )
    coming = lax.ppermute(whole, "tm", [((t + 1) % times, t) for t in range(times)])

    across = width // 128
    stages = [wide(6, across, rows + 8, 128), wide(4, across, TILES, 8, 128)]
    ends = call(
        forward_kernel,
        shape(full, width),
        (incr, wind, mate, other),
        [
            wide(*field), wide(*field), wide(levels * 8, width), wide(levels * 8, width), *stages,
            short(full, width), sems(3, levels),
        ],
        "forward",
        near=(2, 3),
    )
    previous = lax.ppermute(ends, "tm", [(t, (t + 1) % times) for t in range(times)])

    back = call(
        latitude_kernel,
        shape(lat, full),
        (came, var, turned),
        [
            wide(full, lat), short(lat, lat), short(full, lat), short(full, lat),
            short(lat, full), sems(16),
        ],
        "latitude",
        near=(0,),
    )
    returned = lax.all_to_all(back.reshape(count, rows, full), "space", 0, 0, tiled=True)

    tall, obs_rows = call(
        observe_kernel,
        (jax.ShapeDtypeStruct((full, cols.shape[1]), F32), jax.ShapeDtypeStruct(obs_dual.shape, F32)),
        (incr, obs_index, obs_dual, obs_variance, cols, lines, back),
        [wide(*field), short(*cols.shape), short(*lines.shape), sems(3)],
        "observe",
    )
    state_rows = call(
        backward_kernel,
        jax.ShapeDtypeStruct(field, F32),
        (coming, wind, mate, other, mult, tall, cols),
        [
            wide(*field), wide(*field), short(*cols.shape),
            wide(levels * 8, width), wide(levels * 8, width), wide(levels * 8, width), wide(2, 8, width),
            *stages, wide(full, width), wide(*field), sems(3), sems(levels),
        ],
        "backward",
        near=(0, 2, 3),
    )
    model_rows = call(
        finish_kernel,
        jax.ShapeDtypeStruct((full, width), F32),
        (returned, incr.reshape(full, width), previous, table),
        [
            wide(full, width), short(width, width),
            short(full, width), wide(full, width), sems(20),
        ],
        "finish",
        near=(0, 2),
    )

    def placed(whole):
        return jnp.transpose(whole.reshape(field), (1, 0, 2))[None]

    return (placed(model_rows), obs_rows, placed(state_rows))


def solution(mesh):
    specs = (
        P("tm", "space", None, None),
        P("tm", "space", None, None),
        P("tm", "space"),
        P("tm", "space"),
        P("tm", "space"),
        P("tm", "space", None, None),
        P(None, None, "space"),
    )
    return jax.shard_map(
        local,
        mesh=mesh,
        in_specs=specs,
        out_specs=(P("tm", "space", None, None), P("tm", "space"), P("tm", "space", None, None)),
        check_vma=False,
    )
```

```python
import math

import jax
import jax.numpy as jnp
import numpy as np
from jax import lax
from jax.experimental import pallas as pl
from jax.experimental.pallas import tpu as pltpu
from jax.sharding import PartitionSpec as P
import ml_dtypes

STEPS = 4
HALF = 4
F32 = jnp.float32
BF16 = jnp.bfloat16


def cosine_table(count):
    wave = np.arange(count)[:, None]
    point = np.arange(count)[None, :]
    phase = (2 * point + 1) * wave % (4 * count)
    table = np.cos(phase * (math.pi / (2.0 * count))) * math.sqrt(2.0 / count)
    table = np.where(wave == 0, table * math.sqrt(0.5), table)
    return table.astype(np.float32).astype(ml_dtypes.bfloat16)


def block_sums(levels, rows, width):
    cols = (np.arange(width)[:, None] // 16 == np.arange(width // 16)[None, :]).astype(np.float32)
    out = np.arange(rows // 4 * levels)[:, None]
    inn = np.arange(levels * rows)[None, :]
    lines = ((out % levels == inn // rows) & (out // levels == inn % rows // 4)).astype(np.float32)
    return cols.astype(ml_dtypes.bfloat16), lines.astype(ml_dtypes.bfloat16)


def nt(a, b):
    return lax.dot_general(a, b, (((1,), (1,)), ((), ())), preferred_element_type=F32)


def tn(a, b):
    return lax.dot_general(a, b, (((0,), (0,)), ((), ())), preferred_element_type=F32)


def nn(a, b):
    return jnp.dot(a, b, preferred_element_type=F32)


def parts(a):
    first = a.astype(BF16)
    return first, (a - first.astype(F32)).astype(BF16)


def low_half(shape):
    return lax.broadcasted_iota(jnp.int32, shape, len(shape) - 2) < HALF


class Copies:
    def __init__(self, sems):
        self.sems = sems
        self.count = 0

    def start(self, source, target):
        copy = pltpu.make_async_copy(source, target, self.sems.at[self.count])
        self.count += 1
        copy.start()
        return copy


def by_parity(even, odd):
    return jnp.where(lax.axis_index("space") % 2 == 0, even, odd)


def edge_kernel(mult_hbm, incr_hbm, wind_hbm, other_ref, mate_ref, edge_ref, sems):
    levels, rows, width = mult_hbm.shape
    half = levels // 2
    copies = Copies(sems)
    coming = [
        copies.start(source.at[:, pl.ds(at, 8), :], edge_ref.at[3 * end + i])
        for end, at in enumerate((0, rows - 8))
        for i, source in enumerate((incr_hbm, wind_hbm, mult_hbm))
    ]
    messages = []
    for end in range(2):
        for copy in coming[3 * end : 3 * end + 3]:
            copy.wait()
        incr, wind, mult = edge_ref[3 * end], edge_ref[3 * end + 1], edge_ref[3 * end + 2]
        wind = pltpu.roll(wind, HALF, 1)
        second = pltpu.roll(mult[half:], HALF, 1)
        low, less = low_half((levels, 8, width)), low_half((half, 8, width))
        if end == 0:
            field, dual = jnp.where(low, incr, wind), jnp.where(less, mult[:half], second)
        else:
            field, dual = jnp.where(low, wind, incr), jnp.where(less, second, mult[:half])
        messages.append((field.reshape(levels * 8, width), dual.reshape(half * 8, width)))
    for part, (head, tail) in zip((pl.ds(0, levels * 8), pl.ds(levels * 8, half * 8)), zip(*messages)):
        mate_ref[part] = by_parity(tail, head).astype(BF16)
        other_ref[part] = by_parity(head, tail).astype(BF16)


def start_kernel(mult_ref, table_ref, _after, whole_hbm, spec_hbm, flat_ref, spec_ref, sems):
    levels, rows, width = mult_ref.shape
    copies = Copies(sems)
    half = table_ref.shape[0] // 2
    flat = mult_ref[...].reshape(levels * rows, width).astype(BF16)
    flat_ref[...] = flat
    out = [copies.start(flat_ref, whole_hbm.at[pl.ds(0, levels * rows)])]
    for i in range(2):
        part = pl.ds(half * i, half)
        spec_ref[part] = nt(table_ref[part], flat).astype(BF16)
        out.append(copies.start(spec_ref.at[part], spec_hbm.at[part]))
    for copy in out:
        copy.wait()


def order_kernel(_spec_in, _head, _tail, _spec_out):
    pass


def join_kernel(_whole_in, mate_ref, other_ref, whole_hbm, sems):
    copies = Copies(sems)
    size = whole_hbm.shape[0] // 10
    start, far = whole_hbm.shape[0] - 2 * size, mate_ref.shape[0] - size
    odd = lax.axis_index("space") % 2
    out = [
        copies.start(source.at[pl.ds(far, size)], whole_hbm.at[pl.ds(pl.multiple_of(start + size * at, 16), size)])
        for source, at in ((mate_ref, odd), (other_ref, 1 - odd))
    ]
    for copy in out:
        copy.wait()


TILES = 5


def spread_rows(stage_ref, main, margin):
    rows, width = main.shape
    across = width // 128
    for c in range(across):
        stage_ref[c, :rows, :] = main[:, c * 128 : (c + 1) * 128]
        stage_ref[c, rows:, :] = margin[:, c * 128 : (c + 1) * 128]
    return [[stage_ref[c, pl.ds(t, 8, stride=TILES), :] for t in range(TILES)] for c in range(across)]


def join_rows(stage_ref, tiles, rows, factor=0.2**STEPS):
    for c, column in enumerate(tiles):
        for t, tile in enumerate(column):
            stage_ref[c, pl.ds(t, 8, stride=TILES), :] = tile * factor
    return jnp.concatenate([stage_ref[c, :rows, :] for c in range(len(tiles))], axis=1)


def coefficients(level, levels, wind_ref, head_ref, tail_ref, stage_ref, coef_ref):
    rows = wind_ref.shape[1]
    low = low_half((8, wind_ref.shape[2]))
    sublane = lax.broadcasted_iota(jnp.int32, (8, 128), 0)

    def extended(index, stage):
        at = pl.ds(pl.multiple_of(index * 8, 8), 8)
        margin = pltpu.roll(jnp.where(low, tail_ref[at, :], head_ref[at, :]), HALF, 0)
        return spread_rows(stage, wind_ref[index], margin)

    u = extended(level, stage_ref.at[0])
    v = extended(level + levels // 2, stage_ref.at[1])
    place = lax.axis_index("space")
    start, end = place == 0, place == lax.axis_size("space") - 1

    def cut(value, row, t, edge):
        return jnp.where((sublane == row // TILES) & edge, 0.0, value) if t == row % TILES else value

    for c in range(len(u)):
        for t in range(TILES):
            north, south = 1.0 - v[c][t], 1.0 + v[c][t]
            north = cut(cut(north, rows - 1, t, end), rows + 7, t, start)
            south = cut(cut(south, 0, t, start), rows, t, end)
            coef_ref[0, c, t] = 1.0 - u[c][t]
            coef_ref[1, c, t] = 1.0 + u[c][t]
            coef_ref[2, c, t] = north
            coef_ref[3, c, t] = south


def north_of(column, t):
    return column[t + 1] if t < TILES - 1 else pltpu.roll(column[0], 7, 0)


def south_of(column, t):
    return column[t - 1] if t > 0 else pltpu.roll(column[TILES - 1], 1, 0)


def forward_steps(x, coef_ref):
    lane = lax.broadcasted_iota(jnp.int32, (8, 128), 1)
    first, last = lane == 0, lane == 127
    ends = len(x) - 1
    for _ in range(STEPS):
        new = []
        for c in range(len(x)):
            column = []
            for t in range(TILES):
                here = x[c][t]
                east = pltpu.roll(jnp.where(first, x[c + 1][t] if c < ends else 0.0, here), 127, 1)
                west = pltpu.roll(jnp.where(last, x[c - 1][t] if c > 0 else 0.0, here), 1, 1)
                column.append(
                    (here + coef_ref[0, c, t] * east)
                    + coef_ref[1, c, t] * west
                    + (coef_ref[2, c, t] * north_of(x[c], t) + coef_ref[3, c, t] * south_of(x[c], t))
                )
            new.append(column)
        x = new
    return x


def backward_steps(y, coef_ref):
    lane = lax.broadcasted_iota(jnp.int32, (8, 128), 1)
    first, last = lane == 0, lane == 127
    ends = len(y) - 1
    for _ in range(STEPS):
        new = []
        for c in range(len(y)):
            column = []
            up = [coef_ref[3, c, t] * y[c][t] for t in range(TILES)]
            down = [coef_ref[2, c, t] * y[c][t] for t in range(TILES)]
            for t in range(TILES):
                here = y[c][t]
                after = coef_ref[1, c + 1, t] * y[c + 1][t] if c < ends else 0.0
                before = coef_ref[0, c - 1, t] * y[c - 1][t] if c > 0 else 0.0
                east = pltpu.roll(jnp.where(first, after, coef_ref[1, c, t] * here), 127, 1)
                west = pltpu.roll(jnp.where(last, before, coef_ref[0, c, t] * here), 1, 1)
                column.append((here + east) + west + (north_of(up, t) + south_of(down, t)))
            new.append(column)
        y = new
    return y


def one_hots(index, blocks):
    count = index.shape[1]
    high = lax.broadcasted_iota(jnp.int32, (blocks[0], count), 0) == (index >> 6)
    low = lax.broadcasted_iota(jnp.int32, (blocks[1], count), 0) == (index & 63)
    return high, low


def forward_kernel(
    incr_hbm, wind_hbm, mate_ref, other_ref, ends_hbm,
    incr_ref, wind_ref, head_ref, tail_ref, stage_ref, coef_ref, ends_ref, level_sems,
):
    levels, rows, width = incr_ref.shape
    half = levels // 2

    def fetch(kind, index):
        source, target = ((wind_hbm, wind_ref), (incr_hbm, incr_ref))[kind]
        return pltpu.make_async_copy(source.at[index], target.at[index], level_sems.at[kind, index])

    def put(index):
        part = pl.ds(pl.multiple_of(index * rows, rows), rows)
        return pltpu.make_async_copy(ends_ref.at[part], ends_hbm.at[part], level_sems.at[2, index])

    for level in range(half):
        for index in (level, level + half):
            for kind in range(2):
                fetch(kind, index).start()
    mate, other = mate_ref[: levels * 8].astype(F32), other_ref[: levels * 8].astype(F32)
    head_ref[...] = by_parity(mate, other)
    tail_ref[...] = by_parity(other, mate)
    low = low_half((8, width))

    factor = jnp.where(lax.axis_index("tm") == lax.axis_size("tm") - 1, 0.0, 0.2**STEPS)

    def at_level(level, carry):
        for index in (level, level + half):
            for kind in range(2):
                fetch(kind, index).wait()
        coefficients(level, levels, wind_ref, head_ref, tail_ref, stage_ref, coef_ref)

        def at_group(group):
            index = level + group * half
            at = pl.ds(pl.multiple_of(index * 8, 8), 8)
            margin = jnp.where(low, head_ref[at, :], tail_ref[at, :])
            x = forward_steps(spread_rows(stage_ref.at[2 + 2 * group], incr_ref[index], margin), coef_ref)
            ends = join_rows(stage_ref.at[3 + 2 * group], x, rows, factor)
            ends_ref[pl.ds(pl.multiple_of(index * rows, rows), rows), :] = ends.astype(BF16)
            put(index).start()

        for group in range(2):
            at_group(group)
        return carry

    lax.fori_loop(0, half, at_level, 0)
    for index in range(levels):
        put(index).wait()


def observe_kernel(
    incr_hbm, index_ref, dual_ref, variance_ref, cols_hbm, lines_hbm, _after,
    tall_ref, obs_ref, incr_ref, cols_ref, lines_ref, sems,
):
    levels, rows, width = incr_ref.shape
    copies = Copies(sems)
    block_in = [copies.start(cols_hbm, cols_ref), copies.start(lines_hbm, lines_ref)]
    incr_in = copies.start(incr_hbm, incr_ref)
    for copy in block_in:
        copy.wait()
    cols, lines = cols_ref[...], lines_ref[...]
    blocks = (lines.shape[0], cols.shape[1])
    high, low_hot = one_hots(index_ref[...], blocks)
    weights = low_hot.astype(BF16)
    summed = sum(nt(p, weights) for p in parts(jnp.where(high, dual_ref[...], 0.0))) * 0.125
    tall_ref[...] = sum(tn(lines, p) for p in parts(summed))
    incr_in.wait()
    narrow = sum(nn(p, cols) for p in parts(incr_ref[...].reshape(levels * rows, width)))
    sums = sum(nn(lines, p) for p in parts(narrow))
    high = high.astype(BF16)
    picked = sum(tn(p, high) for p in parts(sums))
    observed = jnp.sum(jnp.where(low_hot, picked, 0.0), axis=0, keepdims=True) * 0.125
    obs_ref[...] = variance_ref[...] * dual_ref[...] + observed


def backward_kernel(
    coming_ref, wind_hbm, mate_ref, other_ref, mult_hbm, tall_ref, cols_hbm,
    state_hbm,
    wind_ref, mult_ref, cols_ref,
    head_ref, tail_ref, far_ref, margins_ref, stage_ref, coef_ref, spread_ref, state_ref, sems, level_sems,
):
    levels, rows, width = mult_ref.shape
    half = levels // 2
    copies = Copies(sems)
    full = levels * rows
    arriving = [
        copies.start(source, target)
        for source, target in ((cols_hbm, cols_ref), (wind_hbm, wind_ref), (mult_hbm, mult_ref))
    ]
    arriving[0].wait()
    spread_ref[...] = sum(nt(p, cols_ref[...]) for p in parts(tall_ref[...]))
    for copy in arriving[1:]:
        copy.wait()
    mate, other = mate_ref[: levels * 8].astype(F32), other_ref[: levels * 8].astype(F32)
    head_ref[...] = by_parity(mate, other)
    tail_ref[...] = by_parity(other, mate)
    far_ref[...] = coming_ref[full:].astype(F32)
    low = low_half((8, width))

    def put(index):
        return pltpu.make_async_copy(state_ref.at[index], state_hbm.at[index], level_sems.at[index])

    factor = jnp.where(lax.axis_index("tm") == lax.axis_size("tm") - 1, 0.0, 0.2**STEPS)

    def at_level(level, carry):
        coefficients(level, levels, wind_ref, head_ref, tail_ref, stage_ref, coef_ref)
        at = pl.ds(pl.multiple_of(level * 8, 8), 8)
        head, tail = far_ref[at, :], far_ref[pl.ds(pl.multiple_of(level * 8 + levels * 4, 8), 8), :]
        margins_ref[0] = jnp.where(low, head, tail)
        margins_ref[1] = pltpu.roll(jnp.where(low, tail, head), HALF, 0)

        def at_group(group):
            index = level + group * half
            part = pl.ds(pl.multiple_of(index * rows, rows), rows)
            main = coming_ref[part, :].astype(F32)
            y = backward_steps(spread_rows(stage_ref.at[2 + 2 * group], main, margins_ref[group]), coef_ref)
            back = join_rows(stage_ref.at[3 + 2 * group], y, rows, factor)
            state_ref[index] = (mult_ref[index] - back) + spread_ref[part, :]
            put(index).start()

        for group in range(2):
            at_group(group)
        return carry

    lax.fori_loop(0, half, at_level, 0)
    for index in range(levels):
        put(index).wait()


def gather_lines(came_ref, lines_ref):
    count, rows, wide = came_ref.shape
    groups, fields = count // 4, wide // 128
    source = lax.broadcasted_iota(jnp.int32, (512, 512), 0)
    target = lax.broadcasted_iota(jnp.int32, (512, 512), 1)
    swapped = ((target & 127) >> 5) * 128 + (target >> 7) * 32 + (target & 31)
    perm = (source == swapped).astype(BF16)
    for g in range(fields):
        piece = came_ref[:, :, g * 128 : (g + 1) * 128].reshape(groups, 4, rows, 128)
        left = jnp.concatenate([piece[:, i].reshape(groups * rows, 128) for i in range(4)], axis=1)
        moved = nn(left, perm).astype(BF16)
        for i in range(4):
            for b in range(groups):
                lines_ref[(4 * g + i) * rows : (4 * g + i + 1) * rows, b * 128 : (b + 1) * 128] = moved[
                    b * rows : (b + 1) * rows, i * 128 : (i + 1) * 128
                ]


def latitude_kernel(
    came_ref, var_hbm, turned_hbm, out_hbm,
    var_ref, turned_ref, lines_ref, scaled_ref, out_ref, sems,
):
    copies = Copies(sems)
    turned_in = copies.start(turned_hbm, turned_ref)
    var_in = copies.start(var_hbm, var_ref)
    gather_lines(came_ref, lines_ref)
    turned_in.wait()
    latitude = nn(lines_ref[...], turned_ref[...])
    var_in.wait()
    scaled_ref[...] = (latitude * var_ref[...]).astype(BF16)
    scaled = scaled_ref[...]
    out = []
    for i in range(2):
        part = pl.ds(512 * i, 512)
        out_ref[part] = nt(turned_ref[part], scaled).astype(BF16)
        out.append(copies.start(out_ref.at[part], out_hbm.at[part]))
    for copy in out:
        copy.wait()


def finish_kernel(
    came_ref, incr_hbm, prev_ref, table_hbm, out_hbm,
    incr_ref, table_ref, lines_ref, out_ref, sems,
):
    copies = Copies(sems)
    table_in = copies.start(table_hbm, table_ref)
    incr_in = copies.start(incr_hbm, incr_ref)
    gather_lines(came_ref, lines_ref)
    table_in.wait()
    table = table_ref[...]
    out = []
    for i in range(3):
        part = pl.ds(128 * i, 128)
        covar = nn(lines_ref[part], table)
        if i == 0:
            incr_in.wait()
        out_ref[part] = covar + (incr_ref[part] - prev_ref[part].astype(F32))
        out.append(copies.start(out_ref.at[part], out_hbm.at[part]))
    for copy in out:
        copy.wait()


VMEM = pl.BlockSpec(memory_space=pltpu.VMEM)
HBM = pl.BlockSpec(memory_space=pl.ANY)


def call(kernel, outs, ins, scratch, name, aliases=None, near=(), grant=52):
    def place(index, a):
        small = a.shape[0] == 1 or (len(a.shape) == 2 and a.shape[1] < 128 and a.dtype == F32)
        return VMEM if small or index in near else HBM

    single = not isinstance(outs, tuple)
    out_specs = [place(len(ins) + i, a) for i, a in enumerate((outs,) if single else outs)]
    return pl.pallas_call(
        kernel,
        out_shape=outs,
        in_specs=[place(i, a) for i, a in enumerate(ins)],
        out_specs=out_specs[0] if single else tuple(out_specs),
        scratch_shapes=list(scratch),
        compiler_params=pltpu.CompilerParams(vmem_limit_bytes=grant * 1024 * 1024),
        input_output_aliases=aliases or {},
        name=name,
    )(*ins)


def local(increment, multiplier, obs_dual, obs_index, obs_variance, winds, spectral_var):
    rows, levels, width = increment.shape[1:]
    count = lax.axis_size("space")
    times = lax.axis_size("tm")
    lat = rows * count
    waves = width // count
    full = levels * rows
    incr = jnp.transpose(increment[0], (1, 0, 2))
    mult = jnp.transpose(multiplier[0], (1, 0, 2))
    wind = jnp.transpose(winds[0], (1, 0, 2))
    var = jnp.transpose(spectral_var, (1, 2, 0)).reshape(full, lat)
    table = cosine_table(width)
    turned = np.ascontiguousarray(table.T)
    cols, lines = block_sums(levels, rows, width)

    def shape(*dims):
        return jax.ShapeDtypeStruct(dims, BF16)

    def wide(*dims):
        return pltpu.VMEM(dims, F32)

    def short(*dims):
        return pltpu.VMEM(dims, BF16)

    def sems(*dims):
        return pltpu.SemaphoreType.DMA(dims)

    field = (levels, rows, width)
    other, mate = call(
        edge_kernel,
        (shape(levels * 12, width), shape(levels * 12, width)),
        (mult, incr, wind),
        [wide(6, levels, 8, width), sems(6)],
        "edges",
        near=(3, 4),
        grant=52,
    )
    whole, spec = call(
        start_kernel,
        (shape(full + levels * 8, width), shape(width, full)),
        (mult, table, other),
        [short(full, width), short(width, full), sems(3)],
        "start",
        near=(0,1,2),
        grant=40,
    )
    mates = [(i, i ^ 1) for i in range(count)]
    others = [(i, min(max(((i + 1) ^ 1) - 1, 0), count - 1)) for i in range(count)]
    other = lax.ppermute(other, "space", others)
    mate = lax.ppermute(mate, "space", mates)
    spec = call(order_kernel, shape(width, full), (spec, other, mate), [], "order", {0: 0}, near=(1, 2))
    came = lax.all_to_all(spec.reshape(count, waves, full), "space", 0, 0, tiled=True)
    whole = call(
        join_kernel,
        shape(full + levels * 8, width),
        (whole, mate, other),
        [sems(2)],
        "join",
        {0: 0},
        near=(1, 2),
    )
    coming = lax.ppermute(whole, "tm", [((t + 1) % times, t) for t in range(times)])

    across = width // 128
    stages = [wide(6, across, rows + 8, 128), wide(4, across, TILES, 8, 128)]
    ends = call(
        forward_kernel,
        shape(full, width),
        (incr, wind, mate, other),
        [
            wide(*field), wide(*field), wide(levels * 8, width), wide(levels * 8, width), *stages,
            short(full, width), sems(3, levels),
        ],
        "forward",
        near=(2, 3),
    )
    previous = lax.ppermute(ends, "tm", [(t, (t + 1) % times) for t in range(times)])

    back = call(
        latitude_kernel,
        shape(lat, full),
        (came, var, turned),
        [
            wide(full, lat), short(lat, lat), short(full, lat), short(full, lat),
            short(lat, full), sems(16),
        ],
        "latitude",
        near=(0,),
    )
    returned = lax.all_to_all(back.reshape(count, rows, full), "space", 0, 0, tiled=True)

    tall, obs_rows = call(
        observe_kernel,
        (jax.ShapeDtypeStruct((full, cols.shape[1]), F32), jax.ShapeDtypeStruct(obs_dual.shape, F32)),
        (incr, obs_index, obs_dual, obs_variance, cols, lines, back),
        [wide(*field), short(*cols.shape), short(*lines.shape), sems(3)],
        "observe",
    )
    state_rows = call(
        backward_kernel,
        jax.ShapeDtypeStruct(field, F32),
        (coming, wind, mate, other, mult, tall, cols),
        [
            wide(*field), wide(*field), short(*cols.shape),
            wide(levels * 8, width), wide(levels * 8, width), wide(levels * 8, width), wide(2, 8, width),
            *stages, wide(full, width), wide(*field), sems(3), sems(levels),
        ],
        "backward",
        near=(0, 2, 3),
    )
    model_rows = call(
        finish_kernel,
        jax.ShapeDtypeStruct((full, width), F32),
        (returned, incr.reshape(full, width), previous, table),
        [
            wide(full, width), short(width, width),
            short(full, width), wide(full, width), sems(20),
        ],
        "finish",
        near=(0, 2),
    )

    def placed(whole):
        return jnp.transpose(whole.reshape(field), (1, 0, 2))[None]

    return (placed(model_rows), obs_rows, placed(state_rows))


def solution(mesh):
    specs = (
        P("tm", "space", None, None),
        P("tm", "space", None, None),
        P("tm", "space"),
        P("tm", "space"),
        P("tm", "space"),
        P("tm", "space", None, None),
        P(None, None, "space"),
    )
    return jax.shard_map(
        local,
        mesh=mesh,
        in_specs=specs,
        out_specs=(P("tm", "space", None, None), P("tm", "space"), P("tm", "space", None, None)),
        check_vma=False,
    )
```
